32 devices in a mesh: dp: 8 (over z, x), mp: 4 (over y, core).
Axes of the slice: x: 2, y: 2, z: 4, core: 2. Of those that a mesh axis runs over, the one named last changes fastest.
Arguments:
- row_ids: int32 [8192, 8, 16], P('dp'), may hold values from 0 to 262143, as said below
- bag_counts: int32 [8192, 8], P('dp'), may hold values from 1 to 16
- labels: int32 [8192, 5], P('dp'), may hold values from 0 to 1
- label_mask: int32 [8192, 5], P('dp'), may hold values from 0 to 1, as said below
- tables: float32 [8, 262144, 64], P(None, ('dp', 'mp')), may hold values from -6 to 6
- table_mom: float32 [8, 262144, 64], P(None, ('dp', 'mp')), may hold values from -5.722046e-06 to 5.722046e-06
- table_avg: float32 [8, 262144, 64], P(None, ('dp', 'mp')), may hold values from -6 to 6
- w_in: float32 [8, 512, 1024], P(None, 'dp', 'mp'), may hold values from -1.75 to 1.75
- w_in_mom: float32 [8, 512, 1024], P(None, 'dp', 'mp'), may hold values from -0.00024414062 to 0.00024414062
- w_in_avg: float32 [8, 512, 1024], P(None, 'dp', 'mp'), may hold values from -1.75 to 1.75
- w_out: float32 [8, 1024, 512], P(None, 'mp', 'dp'), may hold values from -1 to 1
- w_out_mom: float32 [8, 1024, 512], P(None, 'mp', 'dp'), may hold values from -0.00048828125 to 0.00048828125
- w_out_avg: float32 [8, 1024, 512], P(None, 'mp', 'dp'), may hold values from -1 to 1
- gate_w: float32 [5, 512, 8], replicated, may hold values from -0.75 to 0.75
- gate_mom: float32 [5, 512, 8], replicated, may hold values from -0.0024414062 to 0.0024414062
- gate_avg: float32 [5, 512, 8], replicated, may hold values from -0.75 to 0.75
- tower_w: float32 [5, 512, 128], replicated, may hold values from -1 to 1
- tower_w_mom: float32 [5, 512, 128], replicated, may hold values from -0.0048828125 to 0.0048828125
- tower_w_avg: float32 [5, 512, 128], replicated, may hold values from -1 to 1
- tower_v: float32 [5, 128], replicated, may hold values from -2.5 to 2.5
- tower_v_mom: float32 [5, 128], replicated, may hold values from -0.0234375 to 0.0234375
- tower_v_avg: float32 [5, 128], replicated, may hold values from -2.5 to 2.5
Outputs:
- loss_sum: float32 [], replicated
- tables_new: float32 [8, 262144, 64], P(None, ('dp', 'mp'))
- table_mom_new: float32 [8, 262144, 64], P(None, ('dp', 'mp'))
- table_avg_new: float32 [8, 262144, 64], P(None, ('dp', 'mp'))
- w_in_new: float32 [8, 512, 1024], P(None, 'dp', 'mp')
- w_in_mom_new: float32 [8, 512, 1024], P(None, 'dp', 'mp')
- w_in_avg_new: float32 [8, 512, 1024], P(None, 'dp', 'mp')
- w_out_new: float32 [8, 1024, 512], P(None, 'mp', 'dp')
- w_out_mom_new: float32 [8, 1024, 512], P(None, 'mp', 'dp')
- w_out_avg_new: float32 [8, 1024, 512], P(None, 'mp', 'dp')
- gate_new: float32 [5, 512, 8], replicated
- gate_mom_new: float32 [5, 512, 8], replicated
- gate_avg_new: float32 [5, 512, 8], replicated
- tower_w_new: float32 [5, 512, 128], replicated
- tower_w_mom_new: float32 [5, 512, 128], replicated
- tower_w_avg_new: float32 [5, 512, 128], replicated
- tower_v_new: float32 [5, 128], replicated
- tower_v_mom_new: float32 [5, 128], replicated
- tower_v_avg_new: float32 [5, 128], replicated
The draws below stay inside these ranges and needn't reach their ends.
Inputs may be any that keep to these rules, and one draw needn't show every extreme that they name: `row_ids`: the samples split into aligned blocks of 256 (those of one device). In each block, over all 8 x 16 slots, live or not, the rows named lie on each owner (row id // 8192) at most 2048 times, and one owner, the same for all blocks of a draw, is named exactly 2048 times in every block. `label_mask`: the share of ones rises from about a quarter at the first sample to about three quarters at the last.
All inputs are finite; a program needn't handle non-finite values.
Results may differ from the reference program's by a relative error of at most 0.03.
Values may be sent and summed in bfloat16 or wider, within the bound.
No kernel may reach another device: no remote copies, remote signals or barrier semaphores. Data moves between devices by JAX's collectives and lax.ppermute only.
A program may use at most 320 MiB of HBM per device.

```python
import jax
import jax.numpy as jnp
from jax import lax

TABLES = 8
ROWS = 262144
EMB = 64
HID = 1024
EXPERTS = 8
TASKS = 5
TOWER = 128
BAG = 16
B_DEV = 1024
FEAT = 512
SAMPLES = 8192
SUB = 256
OWNERS = 32
ROWS_OWN = 8192
CAP = 2048
N_MP = 4


def draw_row_ids(key, part):
    slot_total = SUB * TABLES * BAG
    block_total = SAMPLES // SUB
    key_hot, key_order, key_row = jax.random.split(key, 3)
    hottest = jax.random.randint(key_hot, (), 0, OWNERS)
    position = jnp.arange(slot_total, dtype=jnp.int32)
    spread_out = (hottest + 1 + (position - CAP) % (OWNERS - 1)) % OWNERS
    owner_list = jnp.where(position < CAP, hottest, spread_out)
    key_list = jax.random.split(key_order, block_total)
    shuffled = jax.vmap(lambda one_key: jax.random.permutation(one_key, owner_list))(key_list)
    within = jax.random.randint(key_row, (block_total, slot_total), 0, ROWS_OWN)
    return (shuffled * ROWS_OWN + within).astype(jnp.int32).reshape(SAMPLES, TABLES, BAG)


def draw_label_mask(key, part):
    ticket = jax.random.randint(key, (SAMPLES, TASKS), 0, 1000)
    level = 250 + jnp.arange(SAMPLES, dtype=jnp.int32) * 500 // SAMPLES
    return (ticket < level[:, None]).astype(jnp.int32)


def place_ends(entries, rng, least, largest):
    spot = [jax.random.randint(jax.random.fold_in(rng, axis), (), 0, length) for axis, length in enumerate(entries.shape)]
    main_axis = entries.shape.index(max(entries.shape))
    beside = spot[:main_axis] + [(spot[main_axis] + 1) % entries.shape[main_axis]] + spot[main_axis + 1:]
    return entries.at[tuple(spot)].set(least).at[tuple(beside)].set(largest)


def levels(key, dims, cuts, low, top_value):
    gain = 1.0
    for dim, parts in cuts:
        draws = jax.random.uniform(jax.random.fold_in(jax.random.fold_in(key, 6), dim), (parts,), jnp.float32, low / len(cuts), top_value / len(cuts))
        gain = gain * jnp.repeat(jnp.exp(draws), dims[dim] // parts).reshape((-1,) + (1,) * (len(dims) - 1 - dim))
    return gain


def noise(key, extent, spread, bound, cuts=(), kind=jnp.bfloat16):
    entries = spread * jax.random.normal(key, extent, jnp.float32)
    if cuts:
        entries = entries * levels(key, extent, cuts, -0.22, 0.18)
    return jnp.clip(entries, -bound, bound).astype(kind)


def setup_inputs(seed: int = 0) -> dict:
    key_of = jax.random.split(jax.random.key(seed), 23)
    return {
        "row_ids": draw_row_ids(jax.random.fold_in(key_of[22], 71), 0),
        "bag_counts": place_ends(jax.random.randint(key_of[1], (SAMPLES, TABLES), 1, BAG + 1), jax.random.fold_in(key_of[1], 1), 1, BAG).astype(jnp.int32),
        "labels": place_ends(jax.random.randint(key_of[2], (SAMPLES, TASKS), 0, 2), jax.random.fold_in(key_of[2], 1), 0, 1).astype(jnp.int32),
        "label_mask": draw_label_mask(jax.random.fold_in(key_of[22], 71), 0),
        "tables": noise(key_of[4], (TABLES, ROWS, EMB), 1.0, 6.0, ((1, 32),), jnp.float32),
        "table_mom": noise(key_of[5], (TABLES, ROWS, EMB), (0.0175 * (SAMPLES * ROWS) ** -0.5), 5.7220458984375e-06, ((1, 32),), jnp.float32),
        "table_avg": noise(key_of[6], (TABLES, ROWS, EMB), 1.0, 6.0, ((1, 32),), jnp.float32),
        "w_in": noise(key_of[7], (EXPERTS, FEAT, HID), (2.5 * FEAT ** -0.5), 1.75, ((1, 8), (2, 4)), jnp.float32),
        "w_in_mom": noise(key_of[8], (EXPERTS, FEAT, HID), (0.0016 * SAMPLES ** -0.5), 0.00024414062, ((1, 8), (2, 4)), jnp.float32),
        "w_in_avg": noise(key_of[9], (EXPERTS, FEAT, HID), (2.5 * FEAT ** -0.5), 1.75, ((1, 8), (2, 4)), jnp.float32),
        "w_out": noise(key_of[10], (EXPERTS, HID, FEAT), (2.0 * HID ** -0.5), 1.0, ((1, 4), (2, 8)), jnp.float32),
        "w_out_mom": noise(key_of[11], (EXPERTS, HID, FEAT), (0.003 * SAMPLES ** -0.5), 0.00048828125, ((1, 4), (2, 8)), jnp.float32),
        "w_out_avg": noise(key_of[12], (EXPERTS, HID, FEAT), (2.0 * HID ** -0.5), 1.0, ((1, 4), (2, 8)), jnp.float32),
        "gate_w": noise(key_of[13], (TASKS, FEAT, EXPERTS), (1.1 * FEAT ** -0.5), 0.75, (), jnp.float32),
        "gate_mom": noise(key_of[14], (TASKS, FEAT, EXPERTS), (0.015 * SAMPLES ** -0.5), 0.0024414062, (), jnp.float32),
        "gate_avg": noise(key_of[15], (TASKS, FEAT, EXPERTS), (1.1 * FEAT ** -0.5), 0.75, (), jnp.float32),
        "tower_w": noise(key_of[16], (TASKS, FEAT, TOWER), (1.5 * FEAT ** -0.5), 1.0, (), jnp.float32),
        "tower_w_mom": noise(key_of[17], (TASKS, FEAT, TOWER), (0.03 * SAMPLES ** -0.5), 0.0048828125, (), jnp.float32),
        "tower_w_avg": noise(key_of[18], (TASKS, FEAT, TOWER), (1.5 * FEAT ** -0.5), 1.0, (), jnp.float32),
        "tower_v": noise(key_of[19], (TASKS, TOWER), (2.0 * TOWER ** -0.5), 2.5, (), jnp.float32),
        "tower_v_mom": noise(key_of[20], (TASKS, TOWER), (0.15 * SAMPLES ** -0.5), 0.0234375, (), jnp.float32),
        "tower_v_avg": noise(key_of[21], (TASKS, TOWER), (2.0 * TOWER ** -0.5), 2.5, (), jnp.float32),
    }


highest = lax.Precision.HIGHEST
mu_rate = 0.5
avg_decay = 0.5
task_weights = (1.0, 0.6, 0.8, 0.4, 1.2)
rates = (5000000.0, 12000.0, 3500.0, 1000.0, 370.0, 200.0)

@jax.custom_vjp
def low(v):
    return lax.optimization_barrier(v.astype(jnp.bfloat16)).astype(jnp.float32)

@jax.custom_vjp
def low_back(v):
    return v

def low_keep(v):
    return (low(v), None)

def low_pass(kept, grad):
    return (grad,)

def back_keep(v):
    return (v, None)

def back_low(kept, grad):
    return (low(grad),)
low.defvjp(low_keep, low_pass)
low_back.defvjp(back_keep, back_low)

def forward(params, row_ids, bag_counts, labels_f, mask_f):
    tables, w_in, w_out, gate_w, tower_w, tower_v = params
    table_low = low(tables)
    w_in_low = low(w_in)
    w_out_low = low(w_out)
    gate_low = low(gate_w)
    tower_low = low(tower_w)
    blocks = SAMPLES // B_DEV
    group_width = HID // N_MP
    task_scale = jnp.asarray(task_weights, dtype=jnp.float32)

    def one_block(running, block_data):
        block_ids, block_counts, block_labels, block_mask = block_data
        looked = table_low[jnp.arange(TABLES)[None, :, None], block_ids]
        slot_share = (jnp.arange(BAG)[None, None, :] < block_counts[:, :, None]).astype(jnp.float32) / block_counts[:, :, None].astype(jnp.float32)
        pooled = lax.optimization_barrier(jnp.sum(looked * slot_share[..., None], axis=2)).reshape(B_DEV, FEAT)
        features = low(pooled)
        hidden = low_back(jnp.einsum('bf,efh->beh', features, w_in_low, precision=highest))
        activated = low(jax.nn.gelu(hidden))
        expert_out = jnp.zeros((B_DEV, EXPERTS, FEAT), jnp.float32)
        for group in range(N_MP):
            low_end = group * group_width
            expert_out = expert_out + low(jnp.einsum('beh,ehf->bef', activated[:, :, low_end:low_end + group_width], w_out_low[:, low_end:low_end + group_width], precision=highest))
        expert_out = low_back(expert_out)
        gate_logits = low_back(jnp.einsum('bf,kfe->bke', features, gate_low, precision=highest))
        gate_probs = jax.nn.softmax(gate_logits, axis=-1)
        mixture = low(jnp.einsum('bke,bef->bkf', gate_probs, expert_out, precision=highest))
        tower_pre = low_back(jnp.einsum('bkf,kfc->bkc', mixture, tower_low, precision=highest))
        tower_act = jax.nn.gelu(tower_pre)
        logits = jnp.einsum('bkc,kc->bk', tower_act, tower_v, precision=highest)
        terms = task_scale * block_mask * (jax.nn.softplus(logits) - block_labels * logits)
        return (running + jnp.sum(terms), None)
    stepper = jax.checkpoint(one_block)
    shaped = (row_ids.reshape(blocks, B_DEV, TABLES, BAG), bag_counts.reshape(blocks, B_DEV, TABLES), labels_f.reshape(blocks, B_DEV, TASKS), mask_f.reshape(blocks, B_DEV, TASKS))
    loss_sum, _ = lax.scan(stepper, jnp.zeros((), jnp.float32), shaped)
    return loss_sum

def reference(row_ids, bag_counts, labels, label_mask, tables, table_mom, table_avg, w_in, w_in_mom, w_in_avg, w_out, w_out_mom, w_out_avg, gate_w, gate_mom, gate_avg, tower_w, tower_w_mom, tower_w_avg, tower_v, tower_v_mom, tower_v_avg):
    params = (tables, w_in, w_out, gate_w, tower_w, tower_v)
    moments = (table_mom, w_in_mom, w_out_mom, gate_mom, tower_w_mom, tower_v_mom)
    averages = (table_avg, w_in_avg, w_out_avg, gate_avg, tower_w_avg, tower_v_avg)
    labels_f = labels.astype(jnp.float32)
    mask_f = label_mask.astype(jnp.float32)
    loss_sum, pullback = jax.vjp(lambda values: forward(values, row_ids, bag_counts, labels_f, mask_f), params)
    grads = pullback(jnp.ones_like(loss_sum) / SAMPLES)[0]
    outputs = [loss_sum]
    for weight, moment, average, grad, rate in zip(params, moments, averages, grads, rates):
        moment_new = mu_rate * moment + grad
        weight_new = weight - rate * (grad + mu_rate * moment_new)
        average_new = avg_decay * average + (1.0 - avg_decay) * weight_new
        outputs += [weight_new, moment_new, average_new]
    return (outputs[0], outputs[1], outputs[2], outputs[3], outputs[4], outputs[5], outputs[6], outputs[7], outputs[8], outputs[9], outputs[10], outputs[11], outputs[12], outputs[13], outputs[14], outputs[15], outputs[16], outputs[17], outputs[18])
```

```python
import functools
import math

import jax
import jax.numpy as jnp
from jax import lax
from jax.experimental import pallas as pl
from jax.experimental.pallas import tpu as pltpu
from jax.sharding import PartitionSpec as P

highest = lax.Precision.HIGHEST
mu_rate = 0.5
avg_decay = 0.5
task_weights = (1.0, 0.6, 0.8, 0.4, 1.2)
rates = (5000000.0, 12000.0, 3500.0, 1000.0, 370.0, 200.0)
both = ("dp", "mp")
lanes = 128
group = 16
flag_bit = 20
f32, bf16, i32 = jnp.float32, jnp.bfloat16, jnp.int32
vmem_limit = 58 * 2**20


def bits_of(size):
    return int(size).bit_length() - 1


def params(limit=vmem_limit):
    return pltpu.CompilerParams(vmem_limit_bytes=limit)


def gelu_pair(h):
    scale = math.sqrt(2.0 / math.pi)
    square = h * h
    t = jnp.tanh(scale * h * (1.0 + 0.044715 * square))
    half = 0.5 * (1.0 + t)
    slope = half + 0.5 * h * (1.0 - t * t) * scale * (1.0 + 3.0 * 0.044715 * square)
    return h * half, slope


def gelu_grad(values_in):
    result, pullback = jax.vjp(jax.nn.gelu, values_in)
    return (result, pullback(jnp.ones_like(values_in))[0])


def nesterov(weight, moment, average, grad, rate):
    moment_new = mu_rate * moment + grad
    weight_new = weight - rate * (grad + mu_rate * moment_new)
    average_new = avg_decay * average + (1.0 - avg_decay) * weight_new
    return (weight_new, moment_new, average_new)


class Ring:
    def __init__(self, n_data, n_model):
        self.n_model = n_model
        self.sizes = (2, n_model // 2, 2, n_data // 2)
        self.steps = (("mp", 1), ("mp", 2), ("dp", 1), ("dp", 2))
        self.axis_sizes = {"dp": n_data, "mp": n_model}

    def offset_of(self, place):
        total = 0
        rest = place
        for size, (axis, stride) in reversed(list(zip(self.sizes, self.steps))):
            digit = rest & (size - 1)
            rest = rest >> bits_of(size)
            weight = stride * (self.n_model if axis == "dp" else 1)
            total = total + digit * weight
        return total

    def swap(self, value, stage, distance):
        axis, stride = self.steps[stage]
        count = self.axis_sizes[axis]
        return lax.ppermute(value, axis, [(i, i ^ (distance * stride)) for i in range(count)])

    def reduce_scatter(self, value):
        for stage, size in enumerate(self.sizes):
            if size == 1:
                continue
            parts = value.reshape((size, -1) + value.shape[1:])
            total = parts[0].astype(f32)
            for distance in range(1, size):
                total = total + self.swap(parts[distance], stage, distance).astype(f32)
            value = total.astype(bf16) if stage < 3 else total
        return value[0]

    def all_gather(self, value):
        value = value[None]
        for stage in reversed(range(4)):
            size = self.sizes[stage]
            if size == 1:
                continue
            pieces = [value] + [self.swap(value, stage, d) for d in range(1, size)]
            value = jnp.concatenate(pieces, axis=0)
        return value


def bucket_kernel(pairs, cap_rows, starts, keys, out):
    owners = out.shape[0]
    lane = lax.broadcasted_iota(i32, (1, lanes), 1)
    body_rows = -(-(cap_rows + 1) // 8) * 8

    def one(o, carry):
        off = starts[o * pairs]
        row = lax.shift_right_logical(off, 7)
        shift = off & (lanes - 1)
        block = keys[pl.ds(row, body_rows), :]
        turned = pltpu.roll(block, (lanes - shift) & (lanes - 1), 1)
        merged = jnp.where(lane < lanes - shift, turned[:cap_rows], turned[1 : cap_rows + 1])
        out[o, 0:cap_rows, :] = merged
        head = jnp.zeros((1, lanes), i32)
        for p in range(pairs + 1):
            head = jnp.where(lane == p, starts[o * pairs + p] - off, head)
        out[o, cap_rows : cap_rows + 1, :] = head
        return carry

    lax.fori_loop(0, owners, one, 0)


def prep_kernel(row_bits, sample_bits, entries, rows_out, samples_out):
    e = entries[...]
    rows = e & ((1 << row_bits) - 1)
    lane = lax.broadcasted_iota(i32, e.shape, 1)
    place = lane & (group - 1)
    clash = jnp.zeros(e.shape, i32)
    for d in range(1, group):
        other = pltpu.roll(rows, lanes - d, 1)
        clash = jnp.where((other == rows) & (place < group - d), 1, clash)
    step = 1
    while step < group:
        clash = clash | pltpu.roll(clash, lanes - step, 1)
        step *= 2
    rows_out[...] = jnp.where(place == 0, rows | (clash << flag_bit), rows)
    samples_out[...] = lax.shift_right_logical(e, row_bits) & ((1 << sample_bits) - 1)


def one_hot(samples_ref, first_row, base, low, high, per_device, width):
    parts = []
    for c in range(width // lanes):
        s = samples_ref[pl.ds(first_row + c, 1), :]
        k = lax.broadcasted_iota(i32, (1, lanes), 1) + (base + c * lanes)
        s = jnp.where((k >= low) & (k < high), s, -1)
        hit = lax.broadcasted_iota(i32, (per_device, lanes), 0) == s
        parts.append(jnp.where(hit, 1.0, 0.0).astype(bf16))
    return parts[0] if len(parts) == 1 else jnp.concatenate(parts, axis=1)


def gather_kernel(ring, pair, pairs, per_device, cap, me, bounds, rows, samples, table, out, rows_f, stage):
    devices = out.shape[0] // per_device
    rows_own = table.shape[2]
    width = min(256, cap)
    unroll = 32
    mask = 2 * rows_own - 1
    lane = lax.broadcasted_iota(i32, (lanes, lanes), 1)
    cap_rows = cap // lanes

    def turn(c, carry):
        at = pl.multiple_of(c * lanes, lanes)
        t = table[0, :, pl.ds(at, lanes)].T
        rows_f[pl.ds(at, lanes), :] = jnp.where(lane < lanes // 2, t, 0.0)
        at_odd = pl.multiple_of(c * lanes + rows_own, lanes)
        rows_f[pl.ds(at_odd, lanes), :] = jnp.where(lane < lanes // 2, 0.0, t)
        return carry

    lax.fori_loop(0, rows_own // lanes, turn, 0)
    stage[...] = jnp.zeros(stage.shape, f32)

    def one(a, carry):
        sender = me[0] ^ ring.offset_of(a)
        low = bounds[sender * 8 + pair]
        high = bounds[sender * 8 + pair + 1]

        def fetch(i, c):
            at = pl.multiple_of(i * unroll, unroll)
            first = sender * cap + at
            for u in range(unroll):
                r = rows[first + u]
                if u % group == 0:
                    r = r & mask
                stage[pl.ds(at + u, 1), :] = rows_f[pl.ds(r, 1), :]
            return c

        lax.fori_loop(lax.shift_right_logical(low, 5), lax.shift_right_logical(high + 31, 5), fetch, 0)

        def fold(i, total):
            at = pl.multiple_of(i * width, width)
            hot = one_hot(samples, sender * cap_rows + i * (width // lanes), at, low, high, per_device, width)
            return total + jnp.dot(hot, stage[pl.ds(at, width), :].astype(bf16), preferred_element_type=f32)

        shift = bits_of(width)
        total = lax.fori_loop(
            lax.shift_right_logical(low, shift),
            lax.shift_right_logical(high + width - 1, shift),
            fold,
            jnp.zeros((per_device, lanes), f32),
        )
        out[pl.ds(pl.multiple_of(a * per_device, per_device), per_device), :] = total.astype(bf16)
        return carry

    lax.fori_loop(0, devices, one, 0)


def scatter_kernel(
    ring, pair, per_device, cap, me, bounds, rows, samples, grads, w_in, m_in, a_in,
    w_out, m_out, a_out, sums, stage, w_buf, m_buf, a_buf, in_sem, out_sem,
):
    devices = grads.shape[0] // per_device
    rows_own = w_in.shape[2]
    width = min(256, cap)
    mask = 2 * rows_own - 1
    cap_rows = cap // lanes
    sources = (w_in, m_in, a_in)
    targets = (w_out, m_out, a_out)
    buffers = (w_buf, m_buf, a_buf)
    for i in range(3):
        pltpu.make_async_copy(sources[i].at[pair], buffers[i], in_sem.at[i]).start()

    def wipe(c, carry):
        sums[pl.ds(pl.multiple_of(c * lanes, lanes), lanes), :] = jnp.zeros((lanes, lanes), f32)
        return carry

    lax.fori_loop(0, 2 * rows_own // lanes, wipe, 0)

    def one(a, carry):
        sender = me[0] ^ ring.offset_of(a)
        low = bounds[sender * 8 + pair]
        high = bounds[sender * 8 + pair + 1]
        mine = grads[pl.ds(pl.multiple_of(a * per_device, per_device), per_device), :]

        def spread(i, c):
            at = pl.multiple_of(i * width, width)
            hot = one_hot(samples, sender * cap_rows + i * (width // lanes), at, low, high, per_device, width)
            stage[pl.ds(at, width), :] = lax.dot_general(
                hot, mine, (((0,), (0,)), ((), ())), preferred_element_type=f32
            )
            return c

        shift = bits_of(width)
        lax.fori_loop(
            lax.shift_right_logical(low, shift), lax.shift_right_logical(high + width - 1, shift), spread, 0
        )

        def add(i, c):
            at = pl.multiple_of(i * group, group)
            first = sender * cap + at
            places = [rows[first + u] for u in range(group)]
            clash = lax.shift_right_logical(places[0], flag_bit)
            places[0] = places[0] & mask

            @pl.when(clash == 0)
            def _():
                olds = [sums[pl.ds(r, 1), :] for r in places]
                news = [stage[pl.ds(at + u, 1), :] for u in range(group)]
                for r, old, new in zip(places, olds, news):
                    sums[pl.ds(r, 1), :] = old + new

            @pl.when(clash != 0)
            def _():
                for u, r in enumerate(places):
                    sums[pl.ds(r, 1), :] = sums[pl.ds(r, 1), :] + stage[pl.ds(at + u, 1), :]

            return c

        lax.fori_loop(
            lax.shift_right_logical(low, bits_of(group)),
            lax.shift_right_logical(high + group - 1, bits_of(group)),
            add,
            0,
        )
        return carry

    lax.fori_loop(0, devices, one, 0)
    for i in range(3):
        pltpu.make_async_copy(sources[i].at[pair], buffers[i], in_sem.at[i]).wait()
    lane = lax.broadcasted_iota(i32, (lanes, lanes), 1)
    chunks = out_sem.shape[0] // 3
    chunk = rows_own // chunks

    def copies(n):
        span = pl.ds(n * chunk, chunk)
        return [
            pltpu.make_async_copy(buffers[i].at[:, span], targets[i].at[pair, :, span], out_sem.at[n * 3 + i])
            for i in range(3)
        ]

    for n in range(chunks):

        def update(c, carry):
            at = pl.multiple_of(n * chunk + c * lanes, lanes)
            even = sums[pl.ds(at, lanes), :]
            odd = sums[pl.ds(pl.multiple_of(at + rows_own, lanes), lanes), :]
            grad = jnp.where(lane < lanes // 2, even, odd).T
            span = (slice(None), pl.ds(at, lanes))
            new = nesterov(w_buf[span], m_buf[span], a_buf[span], grad, rates[0])
            w_buf[span] = new[0]
            m_buf[span] = new[1]
            a_buf[span] = new[2]
            return carry

        lax.fori_loop(0, chunk // lanes, update, 0)
        for copy in copies(n):
            copy.start()
    for n in range(chunks):
        for copy in copies(n):
            copy.wait()


def experts_forward(x_ref, w_in_ref, w_out_ref, y_ref, act_ref, slope_ref):
    w_in = w_in_ref[:, 0, 0].reshape(-1, w_in_ref.shape[-1])
    w_out = w_out_ref[:, 0, 0].reshape(-1, w_out_ref.shape[-1])
    hidden = jnp.dot(x_ref[...], w_in, preferred_element_type=f32)
    act, slope = gelu_pair(hidden)
    act = act.astype(bf16)
    act_ref[0, 0] = act
    slope_ref[0, 0] = slope.astype(bf16)
    term = lax.dot_general(act, w_out, (((1,), (1,)), ((), ())), preferred_element_type=f32)

    @pl.when(pl.program_id(1) == 0)
    def _():
        y_ref[0] = term

    @pl.when(pl.program_id(1) != 0)
    def _():
        y_ref[0] += term


def experts_backward(x_ref, d_ref, w_in_ref, w_out_ref, act_ref, slope_ref, dw_in_ref, dw_out_ref, dx_ref):
    w_in = w_in_ref[:, 0, 0].reshape(-1, w_in_ref.shape[-1])
    w_out = w_out_ref[:, 0, 0].reshape(-1, w_out_ref.shape[-1])
    d_out = d_ref[0]
    d_act = jnp.dot(d_out, w_out, preferred_element_type=f32)
    d_hidden = (d_act * slope_ref[0, 0].astype(f32)).astype(bf16)
    shape = (dw_in_ref.shape[0],) + dw_in_ref.shape[3:]
    first = (((0,), (0,)), ((), ()))
    dw_out = lax.dot_general(d_out, act_ref[0, 0], first, preferred_element_type=f32)
    dw_out_ref[:, 0, 0] = dw_out.astype(bf16).reshape(shape)
    dw_in = lax.dot_general(x_ref[...], d_hidden, first, preferred_element_type=f32)
    dw_in_ref[:, 0, 0] = dw_in.astype(bf16).reshape(shape)
    dx = lax.dot_general(d_hidden, w_in, (((1,), (1,)), ((), ())), preferred_element_type=f32)
    start = (pl.program_id(0) == 0) & (pl.program_id(1) == 0)

    @pl.when(start)
    def _():
        dx_ref[...] = dx

    @pl.when(jnp.logical_not(start))
    def _():
        dx_ref[...] += dx


def head_backward(x_rows, y_rows, label_rows, mask_rows, gate_low, tower_low, tower_v, sample_total):
    gate_logits = jnp.einsum("rf,kfe->rke", x_rows, gate_low, preferred_element_type=f32)
    gate_probs = jax.nn.softmax(gate_logits, axis=-1)
    mixture = jnp.einsum("rke,erf->rkf", gate_probs, y_rows, precision=highest).astype(bf16)
    tower_pre = jnp.einsum("rkf,kfc->rkc", mixture, tower_low, preferred_element_type=f32)
    tower_act, slopes = gelu_grad(tower_pre)
    logits = jnp.einsum("rkc,kc->rk", tower_act, tower_v, precision=highest)
    label_f = label_rows.astype(f32)
    weighting = jnp.asarray(task_weights, f32) * mask_rows.astype(f32)
    loss_part = jnp.sum(weighting * (jax.nn.softplus(logits) - label_f * logits))
    d_logits = weighting * (jax.nn.sigmoid(logits) - label_f) / sample_total
    d_tower_v = jnp.einsum("rk,rkc->kc", d_logits, tower_act, precision=highest)
    d_pre = (d_logits[:, :, None] * tower_v[None] * slopes).astype(bf16)
    d_tower_w = jnp.einsum("rkf,rkc->kfc", mixture, d_pre, preferred_element_type=f32)
    d_mixture = jnp.einsum("rkc,kfc->rkf", d_pre, tower_low, preferred_element_type=f32)
    d_probs = jnp.einsum("rkf,erf->rke", d_mixture, y_rows, precision=highest)
    d_logit_gate = (gate_probs * (d_probs - jnp.sum(gate_probs * d_probs, axis=-1, keepdims=True))).astype(bf16)
    d_expert = jnp.einsum("rke,rkf->erf", gate_probs, d_mixture, precision=highest).astype(bf16)
    d_gate_w = jnp.einsum("rf,rke->kfe", x_rows, d_logit_gate, preferred_element_type=f32)
    d_x_gate = jnp.einsum("rke,kfe->rf", d_logit_gate, gate_low, preferred_element_type=f32)
    return (loss_part, d_gate_w, d_tower_w, d_tower_v, d_x_gate, d_expert)


def smem():
    return pl.BlockSpec(memory_space=pltpu.SMEM)


def vmem():
    return pl.BlockSpec(memory_space=pltpu.VMEM)


def body(
    row_ids, bag_counts, labels, label_mask, tables, table_mom, table_avg, w_in, w_in_mom, w_in_avg,
    w_out, w_out_mom, w_out_avg, gate_w, gate_mom, gate_avg, tower_w, tower_w_mom, tower_w_avg,
    tower_v, tower_v_mom, tower_v_avg,
):
    n_model = lax.axis_size("mp")
    n_data = lax.axis_size("dp")
    devices = n_data * n_model
    ring = Ring(n_data, n_model)
    mp_rank = lax.axis_index("mp")
    me = (lax.axis_index("dp") * n_model + mp_rank).astype(i32).reshape(1)
    per_group, table_count, bag_size = row_ids.shape
    per_device = per_group // n_model
    rows_own = tables.shape[1]
    emb_width = tables.shape[2]
    features = table_count * emb_width
    pairs = features // lanes
    sample_total = float(per_group * n_data)
    slot_total = per_device * table_count * bag_size
    cap = 2 * slot_total // devices
    cap_rows = cap // lanes

    w_out_t, w_out_mom_t, w_out_avg_t = (v.transpose(0, 2, 1) for v in (w_out, w_out_mom, w_out_avg))
    experts, f_own, h_own = w_in.shape
    w_in_all = lax.all_gather(w_in.astype(bf16), both, axis=0).reshape(n_data, n_model, experts, f_own, h_own)
    w_out_all = lax.all_gather(w_out_t.astype(bf16), both, axis=0).reshape(n_data, n_model, experts, f_own, h_own)

    row_bits = bits_of(rows_own) + 1
    sample_bits = bits_of(per_device)
    start = mp_rank * per_device
    ids = lax.dynamic_slice_in_dim(row_ids.transpose(1, 2, 0), start, per_device, 2)
    counts = lax.dynamic_slice_in_dim(bag_counts.T, start, per_device, 1)
    live = lax.broadcasted_iota(i32, ids.shape, 1) < counts[:, None, :]
    table_of = lax.broadcasted_iota(i32, ids.shape, 0)
    bucket = lax.shift_right_logical(ids, row_bits - 1) * pairs + lax.shift_right_logical(table_of, 1)
    key = (bucket << sample_bits) | lax.broadcasted_iota(i32, ids.shape, 2)
    key = (((key << 1) | (table_of & 1)) << (row_bits - 1)) | (ids & (rows_own - 1))
    key = jnp.where(live, key, 1 << 30).reshape(-1)
    ordered = lax.sort(key)
    bucket_sorted = lax.shift_right_logical(ordered, row_bits + sample_bits)
    starts = jnp.sum(
        (bucket_sorted[None, :] < jnp.arange(devices * pairs + 1, dtype=i32)[:, None]).astype(i32), axis=1
    )
    padded = jnp.concatenate([ordered.reshape(-1, lanes), jnp.zeros((cap_rows + 8, lanes), i32)], axis=0)
    out_rows = -(-(cap_rows + 1) // 8) * 8
    outgoing = pl.pallas_call(
        functools.partial(bucket_kernel, pairs, cap_rows),
        out_shape=jax.ShapeDtypeStruct((devices, out_rows, lanes), i32),
        in_specs=[smem(), vmem()],
        out_specs=vmem(),
        name="bucket",
    )(starts, padded)
    received = lax.all_to_all(outgoing, both, split_axis=0, concat_axis=0, tiled=True)
    bounds = received[:, cap_rows, :8].reshape(-1)
    entries = received[:, :cap_rows].reshape(devices * cap_rows, lanes)
    entry_shape = jax.ShapeDtypeStruct(entries.shape, i32)
    rows, samples = pl.pallas_call(
        functools.partial(prep_kernel, row_bits, sample_bits),
        out_shape=(entry_shape, entry_shape),
        in_specs=[vmem()],
        out_specs=(vmem(), vmem()),
        name="prep",
    )(entries)
    rows = rows.reshape(-1)

    paired = tuple(
        v.transpose(0, 2, 1).reshape(pairs, lanes, rows_own) for v in (tables, table_mom, table_avg)
    )
    pieces = []
    for pair in range(pairs):
        partial_sums = pl.pallas_call(
            functools.partial(gather_kernel, ring, pair, pairs, per_device, cap),
            grid=(1,),
            out_shape=jax.ShapeDtypeStruct((devices * per_device, lanes), bf16),
            in_specs=[
                smem(), smem(), smem(), vmem(),
                pl.BlockSpec((1, lanes, rows_own), lambda i, pair=pair: (pair, 0, 0)),
            ],
            out_specs=vmem(),
            scratch_shapes=[pltpu.VMEM((2 * rows_own, lanes), f32), pltpu.VMEM((cap, lanes), f32)],
            compiler_params=params(),
            name="gather",
        )(me, bounds, rows, samples, paired[0])
        pieces.append(ring.reduce_scatter(partial_sums.reshape(devices, per_device, lanes)))
    inverse = jnp.repeat(1.0 / counts.T.astype(f32), emb_width, axis=1)
    x = (jnp.concatenate(pieces, axis=1) * inverse).astype(bf16)

    hidden_shape = jax.ShapeDtypeStruct((experts, n_model, per_device, h_own), bf16)
    weight_spec = pl.BlockSpec((n_data, 1, 1, f_own, h_own), lambda e, m: (0, m, e, 0, 0))
    hidden_spec = pl.BlockSpec((1, 1, per_device, h_own), lambda e, m: (e, m, 0, 0))
    expert_spec = pl.BlockSpec((1, per_device, features), lambda e, m: (e, 0, 0))
    whole_spec = pl.BlockSpec((per_device, features), lambda e, m: (0, 0))
    y, act, slope = pl.pallas_call(
        experts_forward,
        grid=(experts, n_model),
        out_shape=(jax.ShapeDtypeStruct((experts, per_device, features), f32), hidden_shape, hidden_shape),
        in_specs=[whole_spec, weight_spec, weight_spec],
        out_specs=(expert_spec, hidden_spec, hidden_spec),
        compiler_params=params(),
        name="experts_forward",
    )(x, w_in_all, w_out_all)
    gate_low = gate_w.astype(bf16)
    tower_low = tower_w.astype(bf16)
    label_rows = lax.dynamic_slice_in_dim(labels, start, per_device, 0)
    mask_rows = lax.dynamic_slice_in_dim(label_mask, start, per_device, 0)
    loss_part, d_gate_w, d_tower_w, d_tower_v, d_x_gate, d_expert = head_backward(
        x, y, label_rows, mask_rows, gate_low, tower_low, tower_v, sample_total
    )
    weight_shape = jax.ShapeDtypeStruct((n_data, n_model, experts, f_own, h_own), bf16)
    dw_in, dw_out, d_x = pl.pallas_call(
        experts_backward,
        grid=(experts, n_model),
        out_shape=(weight_shape, weight_shape, jax.ShapeDtypeStruct((per_device, features), f32)),
        in_specs=[whole_spec, expert_spec, weight_spec, weight_spec, hidden_spec, hidden_spec],
        out_specs=(weight_spec, weight_spec, whole_spec),
        compiler_params=params(),
        name="experts_backward",
    )(x, d_expert, w_in_all, w_out_all, act, slope)
    outgoing_grads = ((d_x + d_x_gate) * inverse).astype(bf16)

    table_outs = None
    paired_shape = jax.ShapeDtypeStruct(paired[0].shape, f32)
    for pair in range(pairs):
        gathered = ring.all_gather(outgoing_grads[:, pair * lanes : (pair + 1) * lanes])
        gathered = gathered.reshape(devices * per_device, lanes)
        hbm = pl.BlockSpec(memory_space=pl.ANY)
        chunks = 4
        operands = (me, bounds, rows, samples, gathered) + paired
        call = functools.partial(scatter_kernel, ring, pair, per_device, cap)
        in_specs = [smem(), smem(), smem(), vmem(), vmem(), hbm, hbm, hbm]
        aliases = {}
        if table_outs is not None:
            operands = operands + table_outs
            in_specs = in_specs + [hbm, hbm, hbm]
            aliases = {8: 0, 9: 1, 10: 2}
            call = functools.partial(skip_old, call)
        table_outs = pl.pallas_call(
            call,
            out_shape=(paired_shape,) * 3,
            in_specs=in_specs,
            out_specs=(hbm, hbm, hbm),
            scratch_shapes=[
                pltpu.VMEM((2 * rows_own, lanes), f32),
                pltpu.VMEM((cap, lanes), f32),
                pltpu.VMEM((lanes, rows_own), f32),
                pltpu.VMEM((lanes, rows_own), f32),
                pltpu.VMEM((lanes, rows_own), f32),
                pltpu.SemaphoreType.DMA((3,)),
                pltpu.SemaphoreType.DMA((3 * chunks,)),
            ],
            input_output_aliases=aliases,
            compiler_params=params(),
            name="scatter",
        )(*operands)
    table_new = tuple(v.reshape(table_count, emb_width, rows_own).transpose(0, 2, 1) for v in table_outs)

    loss_sum, d_gate_w, d_tower_w, d_tower_v = lax.psum((loss_part, d_gate_w, d_tower_w, d_tower_v), both)
    own = (devices, experts, f_own, h_own)
    d_w_in = lax.psum_scatter(dw_in.reshape(own), both, scatter_dimension=0, tiled=True)[0].astype(f32)
    d_w_out = lax.psum_scatter(dw_out.reshape(own), both, scatter_dimension=0, tiled=True)[0].astype(f32)
    w_in_new = nesterov(w_in, w_in_mom, w_in_avg, d_w_in, rates[1])
    w_out_new = nesterov(w_out_t, w_out_mom_t, w_out_avg_t, d_w_out, rates[2])
    w_out_new = tuple(v.transpose(0, 2, 1) for v in w_out_new)
    gate_new = nesterov(gate_w, gate_mom, gate_avg, d_gate_w, rates[3])
    tower_new = nesterov(tower_w, tower_w_mom, tower_w_avg, d_tower_w, rates[4])
    vector_new = nesterov(tower_v, tower_v_mom, tower_v_avg, d_tower_v, rates[5])
    return (loss_sum,) + table_new + w_in_new + w_out_new + gate_new + tower_new + vector_new


def skip_old(call, me, bounds, rows, samples, grads, w, m, a, old_w, old_m, old_a, *rest):
    call(me, bounds, rows, samples, grads, w, m, a, *rest)


def solution(mesh):
    group_spec = P("dp", None)
    table_spec = P(None, both, None)
    placed = (
        (P("dp", None, None), group_spec, group_spec, group_spec)
        + (table_spec,) * 3
        + (P(None, "dp", "mp"),) * 3
        + (P(None, "mp", "dp"),) * 3
        + (P(),) * 9
    )
    return jax.shard_map(
        body,
        mesh=mesh,
        in_specs=placed,
        out_specs=(P(),)
        + (table_spec,) * 3
        + (P(None, "dp", "mp"),) * 3
        + (P(None, "mp", "dp"),) * 3
        + (P(),) * 9,
        check_vma=False,
    )
```

```python
import functools
import math

import jax
import jax.numpy as jnp
from jax import lax
from jax.experimental import pallas as pl
from jax.experimental.pallas import tpu as pltpu
from jax.sharding import PartitionSpec as P

mu_rate = 0.5
avg_decay = 0.5
task_weights = (1.0, 0.6, 0.8, 0.4, 1.2)
rates = (5000000.0, 12000.0, 3500.0, 1000.0, 370.0, 200.0)
both = ("dp", "mp")
lanes = 128
group = 32
window = 8
batch = 4
flag_bit = 20
f32, bf16, i32 = jnp.float32, jnp.bfloat16, jnp.int32
vmem_limit = 58 * 2**20


def bits_of(size):
    return int(size).bit_length() - 1


def cost(microseconds):
    return pl.CostEstimate(flops=int(microseconds * 1.1e9), bytes_accessed=int(microseconds * 3.0e6), transcendentals=0)


def params(limit=vmem_limit):
    return pltpu.CompilerParams(vmem_limit_bytes=limit)


def gelu_pair(h):
    scale = math.sqrt(2.0 / math.pi)
    square = h * h
    t = jnp.tanh(scale * h * (1.0 + 0.044715 * square))
    half = 0.5 * (1.0 + t)
    slope = half + 0.5 * h * (1.0 - t * t) * scale * (1.0 + 3.0 * 0.044715 * square)
    return h * half, slope


def nesterov(weight, moment, average, grad, rate):
    moment_new = mu_rate * moment + grad
    weight_new = weight - rate * (grad + mu_rate * moment_new)
    average_new = avg_decay * average + (1.0 - avg_decay) * weight_new
    return (weight_new, moment_new, average_new)


class Ring:
    def __init__(self, n_data, n_model):
        self.count = n_data * n_model
        tall = n_model // 2
        self.stages = (
            (0, 1),
            tuple(x * n_model + y * 2 for x in range(2) for y in range(tall)),
            tuple(z * 2 * n_model for z in range(n_data // 2)),
        )

    def offset_of(self, place):
        total = 0
        rest = place
        for stage in reversed(self.stages):
            digit = rest & (len(stage) - 1)
            rest = rest >> bits_of(len(stage))
            for bit in range(bits_of(len(stage))):
                total = total + ((digit >> bit) & 1) * stage[1 << bit]
        return total

    def device_at(self, me, place):
        return me ^ self.offset_of(place)

    def place_bits(self):
        places = {self.offset_of(place): place for place in range(self.count)}
        return [places[1 << bit] for bit in range(bits_of(self.count))]

    def swap(self, value, distance):
        return lax.ppermute(value, both, [(i, i ^ distance) for i in range(self.count)])

    def swap_pieces(self, stage, pieces):
        return [pieces[0]] + [self.swap(p, d) for p, d in zip(pieces[1:], self.stages[stage][1:])]

    def spread(self, stage, value):
        return [value] + [self.swap(value, d) for d in self.stages[stage][1:]]


def place_in(bits, offset):
    total = 0
    for bit, value in enumerate(bits):
        total = total + ((offset >> bit) & 1) * value
    return total


def sum_kernel(parts_in, parts_out, dtype, *refs):
    ins, outs = refs[:parts_in], refs[len(refs) - parts_out :]
    for k, out in enumerate(outs):
        total = ins[0][k].astype(f32)
        for ref in ins[1:]:
            total = total + ref[k].astype(f32)
        out[...] = total.astype(dtype)


def sum_pieces(parts, count, dtype, steps, after=(), name="sum"):
    length = parts[0].shape[0] // count
    rest = parts[0].shape[1:]
    fold = rest[:-2]
    blocks = length
    for size in fold:
        blocks = blocks * size
    steps = min(steps, blocks)
    each = blocks // steps
    tile = rest[-2:]
    views = [v.reshape((count, blocks) + tile) for v in parts]
    outs = pl.pallas_call(
        functools.partial(sum_kernel, len(parts), count, dtype),
        grid=(steps,),
        out_shape=[jax.ShapeDtypeStruct((blocks,) + tile, dtype)] * count,
        in_specs=[pl.BlockSpec((count, each) + tile, lambda i: (0, i, 0, 0))] * len(parts)
        + [pl.BlockSpec(memory_space=pl.ANY)] * len(after),
        out_specs=[pl.BlockSpec((each,) + tile, lambda i: (i, 0, 0))] * count,
        compiler_params=params(),
        name=name,
    )(*views, *after)
    return [v.reshape((length,) + rest) for v in outs]


def join_kernel(count, *refs):
    out = refs[-1]
    at = 0
    for ref in refs[:count]:
        out[at : at + ref.shape[0]] = ref[...]
        at += ref.shape[0]


def join(parts, after=()):
    total = sum(v.shape[0] for v in parts)
    anywhere = pl.BlockSpec(memory_space=pl.ANY)
    return pl.pallas_call(
        functools.partial(join_kernel, len(parts)),
        out_shape=jax.ShapeDtypeStruct((total,) + parts[0].shape[1:], parts[0].dtype),
        in_specs=[vmem()] * len(parts) + [anywhere] * len(after),
        out_specs=vmem(),
        compiler_params=params(),
        name="join",
    )(*parts, *after)


def held_until(value, after):
    anywhere = pl.BlockSpec(memory_space=pl.ANY)
    return pl.pallas_call(
        lambda *refs: None,
        out_shape=jax.ShapeDtypeStruct(value.shape, value.dtype),
        in_specs=[anywhere] * (1 + len(after)),
        out_specs=anywhere,
        input_output_aliases={0: 0},
        name="hold",
    )(value, *after)


def bucket_kernel(pairs, cap_rows, starts, keys, out):
    owners = out.shape[0]
    lane = lax.broadcasted_iota(i32, (1, lanes), 1)
    body_rows = -(-(cap_rows + 1) // 8) * 8

    def one(o, carry):
        off = starts[o * pairs]
        row = lax.shift_right_logical(off, 7)
        shift = off & (lanes - 1)
        block = keys[pl.ds(row, body_rows), :]
        turned = pltpu.roll(block, (lanes - shift) & (lanes - 1), 1)
        merged = jnp.where(lane < lanes - shift, turned[:cap_rows], turned[1 : cap_rows + 1])
        out[o, 0:cap_rows, :] = merged
        head = jnp.zeros((1, lanes), i32)
        for p in range(pairs + 1):
            head = jnp.where(lane == p, starts[o * pairs + p] - off, head)
        out[o, cap_rows : cap_rows + 1, :] = head
        return carry

    lax.fori_loop(0, owners, one, 0)


def prep_kernel(row_bits, sample_bits, entries, rows_out, samples_out):
    e = entries[...]
    rows = e & ((1 << row_bits) - 1)
    lane = lax.broadcasted_iota(i32, e.shape, 1)
    place = lane & (window - 1)
    clash = jnp.zeros(e.shape, i32)
    for d in range(1, window):
        other = pltpu.roll(rows, lanes - d, 1)
        clash = jnp.where((other == rows) & (place < window - d), 1, clash)
    step = 1
    while step < group:
        clash = clash | pltpu.roll(clash, lanes - step, 1)
        step *= 2
    rows_out[...] = jnp.where((lane & (group - 1)) == 0, rows | (clash << flag_bit), rows)
    samples_out[...] = lax.shift_right_logical(e, row_bits) & ((1 << sample_bits) - 1)


def one_hot(samples_ref, row, base, low, high, per_device, width):
    count = width // lanes
    s = jnp.concatenate([samples_ref[pl.ds(row + c, 1), :] for c in range(count)], axis=1)
    k = lax.broadcasted_iota(i32, (1, width), 1) + base
    s = jnp.where((k >= low) & (k < high), s, -1).astype(f32).astype(bf16)
    place = lax.broadcasted_iota(i32, (per_device, width), 0).astype(f32).astype(bf16)
    return jnp.where(place == s, jnp.ones((), bf16), jnp.zeros((), bf16))


class Lists:
    def __init__(self, ring, me, rows, held, sems):
        self.ring, self.me, self.rows, self.held, self.sems = ring, me, rows, held, sems
        self.length = held.shape[0] // (2 * batch)
        self.batches = rows.shape[0] // self.length // batch

    def copies(self, n):
        slot = n & 1
        found = []
        for b in range(batch):
            sender = self.ring.device_at(self.me[0], n * batch + b)
            source = self.rows.at[pl.ds(pl.multiple_of(sender * self.length, 1024), self.length)]
            held = self.held.at[pl.ds(pl.multiple_of((slot * batch + b) * self.length, 1024), self.length)]
            found.append(pltpu.make_async_copy(source, held, self.sems.at[slot, b]))
        return found

    def start(self, n):
        for copy in self.copies(n):
            copy.start()

    def wait(self, n):
        for copy in self.copies(n):
            copy.wait()

    def run(self, step):
        self.start(0)

        def one(n, carry):
            @pl.when(n + 1 < self.batches)
            def _():
                self.start(n + 1)

            self.wait(n)
            step(n)
            return carry

        lax.fori_loop(0, self.batches, one, 0)

    def first(self, n, b, at):
        return ((n & 1) * batch + b) * self.length + at

    def entry(self, place):
        return self.held[place] & ((1 << flag_bit) - 1)

    def clash(self, place):
        return lax.shift_right_logical(self.held[place], flag_bit)


def gather_kernel(ring, first_pair, at, per_device, cap, me, bounds, rows, samples, table, *refs):
    keep, send, rows_f, stage, pooled, held, sems, out_sem = refs[-8:]
    step = pl.program_id(0)
    pair = first_pair + step
    rows_own = table.shape[2]
    width = min(256, cap)
    cap_rows = cap // lanes
    blocks = cap // width
    span = 256
    lane = lax.broadcasted_iota(i32, (span, lanes), 1)
    same = lax.broadcasted_iota(i32, (span, span), 0) == lax.broadcasted_iota(i32, (span, span), 1)
    unit = jnp.where(same, 1.0, 0.0).astype(bf16)

    def turn(c, carry):
        at = pl.multiple_of(c * span, span)
        t = table[0, :, pl.ds(at, span)].astype(bf16)
        t = lax.dot_general(unit, t, (((1,), (1,)), ((), ())), preferred_element_type=f32)
        rows_f[pl.ds(at, span), :] = jnp.where(lane < lanes // 2, t, 0.0)
        at_odd = pl.multiple_of(c * span + rows_own, span)
        rows_f[pl.ds(at_odd, span), :] = jnp.where(lane < lanes // 2, 0.0, t)
        return carry

    lax.fori_loop(0, rows_own // span, turn, 0, unroll=8)
    stage[...] = jnp.zeros(stage.shape, f32)
    lists = Lists(ring, me, rows, held, sems)

    def some(n):
        senders = [ring.device_at(me[0], n * batch + b) for b in range(batch)]
        lows = [bounds[s * 8 + pair] for s in senders]
        highs = [bounds[s * 8 + pair + 1] for s in senders]
        for b in range(batch):

            def fetch(i, c):
                at = pl.multiple_of(i * group, group)
                first = lists.first(n, b, at)
                for u in range(group):
                    r = held[first + u] if u else lists.entry(first)
                    stage[b, pl.ds(at + u, 1), :] = rows_f[pl.ds(r, 1), :]
                return c

            lax.fori_loop(lax.div(lows[b], group), lax.div(highs[b] + group - 1, group), fetch, 0)

        def term(b, i):
            block = jnp.minimum(i, blocks - 1)
            row = senders[b] * cap_rows + block * (width // lanes)
            hot = one_hot(samples, row, i * width, lows[b], highs[b], per_device, width)
            fetched = stage[b, pl.ds(pl.multiple_of(block * width, width), width), :].astype(bf16)
            return jnp.dot(hot, fetched, preferred_element_type=f32)

        shift = bits_of(width)
        begins = [lax.shift_right_logical(low, shift) for low in lows]
        def put(b, total):
            pooled[pl.ds(n * batch + b, 1)] = total.astype(bf16)[None]

        for b in range(batch):
            put(b, term(b, begins[b]) + term(b, begins[b] + 1))
        for b in range(batch):

            @pl.when(highs[b] > (begins[b] + 2) * width)
            def _():
                total = lax.fori_loop(
                    begins[b],
                    lax.shift_right_logical(highs[b] + width - 1, shift),
                    lambda i, t: t + term(b, i),
                    jnp.zeros((per_device, lanes), f32),
                )
                put(b, total)

    lists.run(some)
    half = keep.shape[0]
    copies = [
        pltpu.make_async_copy(pooled.at[pl.ds(i * half, half)], ref.at[:, at + step], out_sem.at[i])
        for i, ref in enumerate((keep, send))
    ]
    for copy in copies:
        copy.start()
    for copy in copies:
        copy.wait()


def scatter_kernel(
    ring, pair, rows_at, per_device, cap, me, bounds, rows, samples, own, other, w_in, m_in, a_in, *refs
):
    w_out, m_out, a_out, sums, stage, grads, w_buf, m_buf, a_buf, held, sems, grad_sem, in_sem, out_sem = refs[-14:]
    blocks_each = own.shape[0]
    arrivals = [
        pltpu.make_async_copy(ref.at[:, pl.ds(rows_at, per_device)], grads.at[pl.ds(i * blocks_each, blocks_each)], grad_sem.at[i])
        for i, ref in enumerate((own, other))
    ]
    for arrival in arrivals:
        arrival.start()
    rows_own = w_in.shape[2]
    width = min(256, cap)
    cap_rows = cap // lanes
    blocks = cap // width
    sources = (w_in, m_in, a_in)
    targets = (w_out, m_out, a_out)
    buffers = (w_buf, m_buf, a_buf)
    sums[...] = jnp.zeros(sums.shape, f32)
    lists = Lists(ring, me, rows, held, sems)
    for arrival in arrivals:
        arrival.wait()
    for i in range(3):
        pltpu.make_async_copy(sources[i].at[pair], buffers[i], in_sem.at[i]).start()

    def some(n):
        senders = [ring.device_at(me[0], n * batch + b) for b in range(batch)]
        lows = [bounds[s * 8 + pair] for s in senders]
        highs = [bounds[s * 8 + pair + 1] for s in senders]

        def spread(b, i):
            block = jnp.minimum(i, blocks - 1)
            row = senders[b] * cap_rows + block * (width // lanes)
            hot = one_hot(samples, row, block * width, lows[b], highs[b], per_device, width)
            mine = grads[n * batch + b]
            stage[b, pl.ds(pl.multiple_of(block * width, width), width), :] = lax.dot_general(
                hot, mine, (((0,), (0,)), ((), ())), preferred_element_type=f32
            )

        shift = bits_of(width)
        begins = [lax.shift_right_logical(low, shift) for low in lows]
        for b in range(batch):
            spread(b, begins[b])
            spread(b, begins[b] + 1)
        for b in range(batch):

            @pl.when(highs[b] > (begins[b] + 2) * width)
            def _():
                def more(i, c):
                    spread(b, i)
                    return c

                lax.fori_loop(begins[b] + 2, lax.shift_right_logical(highs[b] + width - 1, shift), more, 0)

        for b in range(batch):

            def add(i, c):
                at = pl.multiple_of(i * group, group)
                first = lists.first(n, b, at)

                def apart():
                    for start in range(0, group, window):
                        places = [held[first + u] if u else lists.entry(first) for u in range(start, start + window)]
                        olds = [sums[pl.ds(r, 1), :] for r in places]
                        news = [stage[b, pl.ds(at + start + u, 1), :] for u in range(window)]
                        for r, old, new in zip(places, olds, news):
                            sums[pl.ds(r, 1), :] = old + new

                def in_turn():
                    def single(u, inner):
                        r = lists.entry(first + u)
                        sums[pl.ds(r, 1), :] = sums[pl.ds(r, 1), :] + stage[b, pl.ds(at + u, 1), :]
                        return inner

                    lax.fori_loop(0, group, single, 0)

                lax.cond(lists.clash(first) == 0, apart, in_turn)
                return c

            lax.fori_loop(lax.div(lows[b], group), lax.div(highs[b] + group - 1, group), add, 0)

    lists.run(some)
    for i in range(3):
        pltpu.make_async_copy(sources[i].at[pair], buffers[i], in_sem.at[i]).wait()
    chunks = out_sem.shape[0] // 3
    chunk = rows_own // chunks
    span = min(256, chunk)
    lane = lax.broadcasted_iota(i32, (span, lanes), 1)

    def copies(n):
        part = pl.ds(n * chunk, chunk)
        return [
            pltpu.make_async_copy(buffers[i].at[:, part], targets[i].at[pair, :, part], out_sem.at[n * 3 + i])
            for i in range(3)
        ]

    for n in range(chunks):

        def update(c, carry):
            at = pl.multiple_of(n * chunk + c * span, span)
            even = sums[pl.ds(at, span), :]
            odd = sums[pl.ds(pl.multiple_of(at + rows_own, span), span), :]
            grad = jnp.where(lane < lanes // 2, even, odd).T
            part = (slice(None), pl.ds(at, span))
            new = nesterov(w_buf[part], m_buf[part], a_buf[part], grad, rates[0])
            w_buf[part] = new[0]
            m_buf[part] = new[1]
            a_buf[part] = new[2]
            return carry

        lax.fori_loop(0, chunk // span, update, 0)
        for copy in copies(n):
            copy.start()
    for n in range(chunks):
        for copy in copies(n):
            copy.wait()


rows_first = (((0,), (0,)), ((), ()))
last_last = (((1,), (1,)), ((), ()))


def experts_forward(x_ref, weight_ref, y_ref, act_ref, slope_ref):
    x = x_ref[...]
    total = None
    for m in range(weight_ref.shape[1]):
        w_in, w_out = (weight_ref[:, m, i, 0].reshape(-1, weight_ref.shape[-1]) for i in range(2))
        act, slope = gelu_pair(jnp.dot(x, w_in, preferred_element_type=f32))
        act = act.astype(bf16)
        act_ref[0, m] = act
        slope_ref[0, m] = slope.astype(bf16)
        term = lax.dot_general(act, w_out, last_last, preferred_element_type=f32)
        total = term if total is None else total + term
    y_ref[0] = total


def experts_back_rows(pairs, d_ref, weight_ref, slope_ref, dxg_ref, inv_ref, d_hidden_ref, *refs):
    grads, dx = refs[:pairs], refs[pairs]
    d_out = d_ref[0]
    total = None
    for m in range(weight_ref.shape[1]):
        w_in, w_out = (weight_ref[:, m, i, 0].reshape(-1, weight_ref.shape[-1]) for i in range(2))
        d_act = jnp.dot(d_out, w_out, preferred_element_type=f32)
        d_hidden = (d_act * slope_ref[0, m].astype(f32)).astype(bf16)
        d_hidden_ref[0, m] = d_hidden
        term = lax.dot_general(d_hidden, w_in, last_last, preferred_element_type=f32)
        total = term if total is None else total + term

    @pl.when(pl.program_id(0) == 0)
    def _():
        dx[...] = dxg_ref[...] + total

    @pl.when(pl.program_id(0) != 0)
    def _():
        dx[...] += total

    @pl.when(pl.program_id(0) == pl.num_programs(0) - 1)
    def _():
        for p in range(pairs):
            part = (slice(None), slice(p * lanes, (p + 1) * lanes))
            grads[p][...] = (dx[part] * inv_ref[part]).astype(bf16)


def experts_back_weights(n_model, lhs_ref, rows_ref, *refs):
    dw_ref = refs[-1]
    devices, _, f_own, _ = dw_ref.shape
    lhs = lhs_ref[0]
    for m in range(n_model):
        out = jnp.dot(lhs, rows_ref[0, m], preferred_element_type=f32).astype(bf16)
        for d in range(devices // n_model):
            dw_ref[d * n_model + m, 0] = out[d * f_own : (d + 1) * f_own]


def experts_back_placed(bits, n_model, me, lhs_ref, rows_ref, *refs):
    keep, send = refs[-2:]
    half, _, f_own, h_own = keep.shape
    model = me[0] & (n_model - 1)
    data = me[0] ^ model
    bits = [0] + bits[1:]
    lhs = lhs_ref[0]
    for beside in range(n_model):
        out = jnp.dot(lhs, rows_ref[0, pl.ds(model ^ beside, 1)][0], preferred_element_type=f32).astype(bf16)
        to = send if beside & 1 else keep
        for d in range(2 * half // n_model):
            place = place_in(bits, (data ^ (d * n_model)) | (beside & (n_model - 2)))
            to[pl.ds(place, 1), 0] = out[d * f_own : (d + 1) * f_own][None]


def head_kernel(
    sample_total, x_ref, y_ref, gate_ref, tower_ref, v_ref, label_ref,
    d_expert_ref, d_expert_t_ref, dxg_ref, d_tower_ref, d_gate_ref, small_ref, probs, mixed, d_mixed, d_gate, inner,
):
    experts, rows, features = y_ref.shape
    tasks = tower_ref.shape[0]
    x = x_ref[...]
    gate = gate_ref[...]
    logits = jnp.dot(x, gate, preferred_element_type=f32)
    task_of = lax.shift_right_logical(lax.broadcasted_iota(i32, (1, lanes), 1), bits_of(experts))

    def by_task(fold, value, fill):
        total = jnp.zeros(value.shape, f32)
        for k in range(tasks):
            found = fold(jnp.where(task_of == k, value, fill), axis=1, keepdims=True)
            total = jnp.where(task_of == k, found, total)
        return total

    used = task_of < tasks
    raised = jnp.where(used, jnp.exp(logits - by_task(jnp.max, logits, -jnp.inf)), 0.0)
    probs[...] = raised / jnp.where(used, by_task(jnp.sum, raised, 0.0), 1.0)
    span = 16
    parts = 2
    wide = features // parts

    def mix(r, carry):
        part = pl.ds(pl.multiple_of(r * span, span), span)
        p = probs[part, :]
        for h in range(parts):
            across = slice(h * wide, (h + 1) * wide)
            totals = [None] * tasks
            for e in range(experts):
                y = y_ref[e, part, across]
                for k in range(tasks):
                    c = k * experts + e
                    more = p[:, c : c + 1] * y
                    totals[k] = more if e == 0 else totals[k] + more
            for k in range(tasks):
                mixed[k, part, across] = totals[k].astype(bf16)
        return carry

    lax.fori_loop(0, rows // span, mix, 0)
    loss = jnp.zeros((1, 1), f32)
    vectors = []
    for k in range(tasks):
        tower = tower_ref[k]
        act, slope = gelu_pair(jnp.dot(mixed[k], tower, preferred_element_type=f32))
        v = v_ref[k : k + 1, :]
        logit = jnp.sum(act * v, axis=1, keepdims=True)
        label = label_ref[:, k : k + 1]
        weighting = task_weights[k] * label_ref[:, tasks + k : tasks + k + 1]
        small_exp = jnp.exp(-jnp.abs(logit))
        softplus = jnp.maximum(logit, 0.0) + jnp.log1p(small_exp)
        loss = loss + jnp.sum(weighting * (softplus - label * logit), axis=0, keepdims=True)
        sigmoid = jnp.where(logit >= 0.0, 1.0, small_exp) / (1.0 + small_exp)
        d_logit = weighting * (sigmoid - label) / sample_total
        vectors.append(jnp.sum(d_logit * act, axis=0, keepdims=True))
        d_pre = (d_logit * v * slope).astype(bf16)
        d_mixed[k] = lax.dot_general(d_pre, tower, last_last, preferred_element_type=f32)
        d_tower_ref[k] = lax.dot_general(mixed[k], d_pre, rows_first, preferred_element_type=f32).astype(bf16)
    lane = lax.broadcasted_iota(i32, (span, lanes), 1)
    ones = jnp.ones((lanes, lanes), bf16)

    def back(r, carry):
        part = pl.ds(pl.multiple_of(r * span, span), span)
        p = probs[part, :]
        for e in range(experts):
            y = y_ref[e, part, :]
            total = None
            for k in range(tasks):
                c = k * experts + e
                d = d_mixed[k, part, :]
                product = d * y
                narrow = product[:, :lanes]
                for t in range(1, features // lanes):
                    narrow = narrow + product[:, t * lanes : (t + 1) * lanes]
                coarse = narrow.astype(bf16)
                inner[0, c * span : (c + 1) * span, :] = coarse
                inner[1, c * span : (c + 1) * span, :] = (narrow - coarse.astype(f32)).astype(bf16)
                more = p[:, c : c + 1] * d
                total = more if k == 0 else total + more
            d_expert_ref[e, part, :] = total.astype(bf16)
        row_sums = jnp.dot(inner[0], ones, preferred_element_type=f32)
        row_sums = row_sums + jnp.dot(inner[1], ones, preferred_element_type=f32)
        d_probs = jnp.zeros((span, lanes), f32)
        for c in range(tasks * experts):
            d_probs = jnp.where(lane == c, row_sums[c * span : (c + 1) * span], d_probs)
        d_gate[part, :] = (p * (d_probs - by_task(jnp.sum, p * d_probs, 0.0))).astype(bf16)
        return carry

    lax.fori_loop(0, rows // span, back, 0)
    for e in range(experts):
        d_expert_t_ref[e] = d_expert_ref[e].T
    dxg_ref[...] = lax.dot_general(d_gate[...], gate, last_last, preferred_element_type=f32)
    d_gate_ref[...] = lax.dot_general(x, d_gate[...], rows_first, preferred_element_type=f32).astype(bf16)
    line = lax.broadcasted_iota(i32, (8, lanes), 0)
    tile = jnp.where(line == tasks, loss, 0.0)
    for k in range(tasks):
        tile = jnp.where(line == k, vectors[k], tile)
    pieces = []
    for _ in range(4):
        piece = tile.astype(bf16)
        pieces.append(piece)
        tile = tile - piece.astype(f32)
    small_ref[...] = jnp.concatenate(pieces, axis=0)


def smem():
    return pl.BlockSpec(memory_space=pltpu.SMEM)


def vmem():
    return pl.BlockSpec(memory_space=pltpu.VMEM)


def body(
    row_ids, bag_counts, labels, label_mask, tables, table_mom, table_avg, w_in, w_in_mom, w_in_avg,
    w_out, w_out_mom, w_out_avg, gate_w, gate_mom, gate_avg, tower_w, tower_w_mom, tower_w_avg,
    tower_v, tower_v_mom, tower_v_avg,
):
    n_model = lax.axis_size("mp")
    n_data = lax.axis_size("dp")
    devices = n_data * n_model
    ring = Ring(n_data, n_model)
    mp_rank = lax.axis_index("mp")
    me = (lax.axis_index("dp") * n_model + mp_rank).astype(i32).reshape(1)
    per_group, table_count, bag_size = row_ids.shape
    per_device = per_group // n_model
    rows_own = tables.shape[1]
    emb_width = tables.shape[2]
    features = table_count * emb_width
    pairs = features // lanes
    sample_total = float(per_group * n_data)
    slot_total = per_device * table_count * bag_size
    cap = 2 * slot_total // devices
    cap_rows = cap // lanes

    w_out_t, w_out_mom_t, w_out_avg_t = (v.transpose(0, 2, 1) for v in (w_out, w_out_mom, w_out_avg))
    experts, f_own, h_own = w_in.shape
    weights = jnp.stack([w_in, w_out_t]).astype(bf16)
    weights = lax.all_gather(weights, both, axis=0).reshape(n_data, n_model, 2, experts, f_own, h_own)

    row_bits = bits_of(rows_own) + 1
    sample_bits = bits_of(per_device)
    start = mp_rank * per_device
    ids = lax.dynamic_slice_in_dim(row_ids.transpose(1, 2, 0), start, per_device, 2)
    counts = lax.dynamic_slice_in_dim(bag_counts.T, start, per_device, 1)
    live = lax.broadcasted_iota(i32, ids.shape, 1) < counts[:, None, :]
    table_of = lax.broadcasted_iota(i32, ids.shape, 0)
    bucket = lax.shift_right_logical(ids, row_bits - 1) * pairs + lax.shift_right_logical(table_of, 1)
    key = (bucket << sample_bits) | lax.broadcasted_iota(i32, ids.shape, 2)
    key = (((key << 1) | (table_of & 1)) << (row_bits - 1)) | (ids & (rows_own - 1))
    key = jnp.where(live, key, 1 << 30).reshape(-1)
    ordered = lax.sort(key)
    bucket_sorted = lax.shift_right_logical(ordered, row_bits + sample_bits)
    starts = jnp.sum(
        (bucket_sorted[None, :] < jnp.arange(devices * pairs + 1, dtype=i32)[:, None]).astype(i32), axis=1
    )
    padded = jnp.concatenate([ordered.reshape(-1, lanes), jnp.zeros((cap_rows + 8, lanes), i32)], axis=0)
    out_rows = -(-(cap_rows + 1) // 8) * 8
    outgoing = pl.pallas_call(
        functools.partial(bucket_kernel, pairs, cap_rows),
        out_shape=jax.ShapeDtypeStruct((devices, out_rows, lanes), i32),
        in_specs=[smem(), vmem()],
        out_specs=vmem(),
        name="bucket",
    )(starts, padded)
    received = lax.all_to_all(outgoing, both, split_axis=0, concat_axis=0, tiled=True)
    bounds = received[:, cap_rows, :8].reshape(-1)
    entries = received[:, :cap_rows].reshape(devices * cap_rows, lanes)
    entry_shape = jax.ShapeDtypeStruct(entries.shape, i32)
    rows, samples = pl.pallas_call(
        functools.partial(prep_kernel, row_bits, sample_bits),
        out_shape=(entry_shape, entry_shape),
        in_specs=[vmem()],
        out_specs=(vmem(), vmem()),
        name="prep",
    )(entries)
    length = max(cap, 1024)
    rows = jnp.pad(rows.reshape(devices, cap), ((0, 0), (0, length - cap))).reshape(-1)
    hbm = pl.BlockSpec(memory_space=pl.ANY)
    list_scratch = [pltpu.SMEM((2 * batch * length,), i32), pltpu.SemaphoreType.DMA((2, batch))]

    paired = tuple(
        v.transpose(0, 2, 1).reshape(pairs, lanes, rows_own) for v in (tables, table_mom, table_avg)
    )
    half = devices // 2
    half_shape = jax.ShapeDtypeStruct((half, per_device, lanes), bf16)

    def gather(first_pair, count, at, total, olds, after):
        out_shape = jax.ShapeDtypeStruct((half, total, per_device, lanes), bf16)
        return pl.pallas_call(
            functools.partial(gather_kernel, ring, first_pair, at, per_device, cap),
            grid=(count,),
            out_shape=(out_shape, out_shape),
            in_specs=[
                smem(), smem(), hbm, vmem(),
                pl.BlockSpec((1, lanes, rows_own), lambda i: (first_pair + i, 0, 0)),
            ] + [hbm] * (len(olds) + len(after)),
            out_specs=(hbm, hbm),
            scratch_shapes=[
                pltpu.VMEM((2 * rows_own, lanes), f32),
                pltpu.VMEM((batch, cap, lanes), f32),
                pltpu.VMEM((devices, per_device, lanes), bf16),
            ] + list_scratch + [pltpu.SemaphoreType.DMA((2,))],
            input_output_aliases={5: 0, 6: 1} if olds else {},
            compiler_params=params(),
            cost_estimate=cost(16 * count),
            name="gather",
        )(me, bounds, rows, samples, paired[0], *olds, *after)

    plane, line = len(ring.stages[1]), len(ring.stages[2])
    each = half // plane

    def core_sums(keep, send, steps, after=(), name="sum_core"):
        return sum_pieces([keep, ring.swap(send, 1)], plane, bf16, steps, after, name)

    def plane_sums(pieces, steps, after=(), name="sum_plane"):
        return sum_pieces(ring.swap_pieces(1, pieces), line, bf16, steps, after, name)

    def line_sum(pieces):
        total = None
        for piece in ring.swap_pieces(2, pieces):
            total = piece.astype(f32) if total is None else total + piece.astype(f32)
        return total

    early = pairs // 2
    rest = pairs - early
    cored_early = core_sums(*gather(0, early, 0, early, (), ()), 2)
    late = gather(early, rest - 1, 0, rest, (), ())
    late = gather(pairs - 1, 1, rest - 1, rest, late, (cored_early[0],))
    planed_early = plane_sums(cored_early, 1)
    cored_late = core_sums(late[0], held_until(late[1], (planed_early[0],)), 2)
    planed_late = plane_sums(cored_late, 1)
    pooled = jnp.concatenate([line_sum(planed_early)[0], line_sum(planed_late)[0]], axis=0)
    inverse = jnp.repeat(1.0 / counts.T.astype(f32), emb_width, axis=1)
    x = (pooled.transpose(1, 0, 2).reshape(per_device, features) * inverse).astype(bf16)

    hidden_shape = jax.ShapeDtypeStruct((experts, n_model, per_device, h_own), bf16)
    weight_spec = pl.BlockSpec((n_data, n_model, 2, 1, f_own, h_own), lambda e: (0, 0, 0, e, 0, 0))
    hidden_spec = pl.BlockSpec((1, n_model, per_device, h_own), lambda e: (e, 0, 0, 0))
    expert_spec = pl.BlockSpec((1, per_device, features), lambda e: (e, 0, 0))
    whole_spec = pl.BlockSpec((per_device, features), lambda e: (0, 0))
    y, act, slope = pl.pallas_call(
        experts_forward,
        grid=(experts,),
        out_shape=(jax.ShapeDtypeStruct((experts, per_device, features), f32), hidden_shape, hidden_shape),
        in_specs=[whole_spec, weight_spec],
        out_specs=(expert_spec, hidden_spec, hidden_spec),
        compiler_params=params(),
        cost_estimate=cost(16),
        name="experts_forward",
    )(x, weights)
    tasks, _, tower_width = tower_w.shape
    spare = lanes - tasks * experts
    gate_low = jnp.pad(gate_w.transpose(1, 0, 2).reshape(features, tasks * experts), ((0, 0), (0, spare))).astype(bf16)
    label_rows = lax.dynamic_slice_in_dim(labels, start, per_device, 0)
    mask_rows = lax.dynamic_slice_in_dim(label_mask, start, per_device, 0)
    marks = jnp.concatenate([label_rows, mask_rows], axis=1).astype(f32)
    d_expert, d_expert_t, d_x_gate, d_tower_part, d_gate_part, tiny = pl.pallas_call(
        functools.partial(head_kernel, sample_total),
        out_shape=(
            jax.ShapeDtypeStruct((experts, per_device, features), bf16),
            jax.ShapeDtypeStruct((experts, features, per_device), bf16),
            jax.ShapeDtypeStruct((per_device, features), f32),
            jax.ShapeDtypeStruct(tower_w.shape, bf16),
            jax.ShapeDtypeStruct((features, lanes), bf16),
            jax.ShapeDtypeStruct((32, lanes), bf16),
        ),
        in_specs=[vmem()] * 6,
        out_specs=(vmem(),) * 6,
        scratch_shapes=[
            pltpu.VMEM((per_device, lanes), f32),
            pltpu.VMEM((tasks, per_device, features), bf16),
            pltpu.VMEM((tasks, per_device, features), f32),
            pltpu.VMEM((per_device, lanes), bf16),
            pltpu.VMEM((2, 16 * tasks * experts, lanes), bf16),
        ],
        compiler_params=params(),
        cost_estimate=cost(12),
        name="towers",
    )(x, y, gate_low, tower_w.astype(bf16), tower_v, marks)
    grads_shape = jax.ShapeDtypeStruct((per_device, lanes), bf16)
    d_hidden, *grads = pl.pallas_call(
        functools.partial(experts_back_rows, pairs),
        grid=(experts,),
        out_shape=(hidden_shape,) + (grads_shape,) * pairs,
        in_specs=[expert_spec, weight_spec, hidden_spec, whole_spec, whole_spec],
        out_specs=(hidden_spec,) + (pl.BlockSpec((per_device, lanes), lambda e: (0, 0)),) * pairs,
        scratch_shapes=[pltpu.VMEM((per_device, features), f32)],
        compiler_params=params(),
        cost_estimate=cost(14),
        name="experts_back_rows",
    )(d_expert, weights, slope, d_x_gate, inverse)
    grads = jnp.concatenate([grads[0], tiny] + grads[1:], axis=0)[None]

    lhs_spec = [
        pl.BlockSpec((1, features, per_device), lambda e, single=single: (0 if single else e, 0, 0))
        for single in (False, True)
    ]
    rows_spec = pl.BlockSpec((1, n_model, per_device, h_own), lambda e: (e, 0, 0, 0))
    half_weights = jax.ShapeDtypeStruct((half, experts, f_own, h_own), bf16)
    half_spec = pl.BlockSpec((half, 1, f_own, h_own), lambda e: (0, e, 0, 0))

    paired_shape = jax.ShapeDtypeStruct(paired[0].shape, f32)
    chunks = 4

    def scatter(pair, at, own, other, olds, after):
        in_specs = [smem(), smem(), hbm, vmem()] + [hbm] * (5 + len(olds) + len(after))
        return pl.pallas_call(
            functools.partial(scatter_kernel, ring, pair, at, per_device, cap),
            out_shape=(paired_shape,) * 3,
            in_specs=in_specs,
            out_specs=(hbm, hbm, hbm),
            scratch_shapes=[
                pltpu.VMEM((2 * rows_own, lanes), f32),
                pltpu.VMEM((batch, cap, lanes), f32),
                pltpu.VMEM((devices, per_device, lanes), bf16),
                pltpu.VMEM((lanes, rows_own), f32),
                pltpu.VMEM((lanes, rows_own), f32),
                pltpu.VMEM((lanes, rows_own), f32),
                *list_scratch,
                pltpu.SemaphoreType.DMA((2,)),
                pltpu.SemaphoreType.DMA((3,)),
                pltpu.SemaphoreType.DMA((3 * chunks,)),
            ],
            input_output_aliases={9: 0, 10: 1, 11: 2} if olds else {},
            compiler_params=params(),
            cost_estimate=cost(26),
            name="scatter",
        )(me, bounds, rows, samples, own, other, *paired, *olds, *after)

    small_rows = tasks * features + features
    small = jnp.concatenate([d_tower_part.reshape(-1, lanes), d_gate_part], axis=0).reshape(2, 1, small_rows // 2, lanes)
    side = me[0] & 1
    give = lax.dynamic_index_in_dim(small, 1 - side, 0, keepdims=False)
    take = lax.dynamic_index_in_dim(small, side, 0, keepdims=False)
    distances = [1 << bit for bit in range(bits_of(devices))]

    def add_small(after):
        got = ring.swap(give, distances.pop(0)) if distances else None
        return take if got is None else sum_pieces([take, got], 1, bf16, 1, after, "sum_small")[0]

    dw_out = pl.pallas_call(
        functools.partial(experts_back_weights, n_model),
        grid=(experts,),
        out_shape=jax.ShapeDtypeStruct((devices, experts, f_own, h_own), bf16),
        in_specs=[lhs_spec[0], rows_spec],
        out_specs=pl.BlockSpec((devices, 1, f_own, h_own), lambda e: (0, e, 0, 0)),
        compiler_params=params(),
        cost_estimate=cost(9),
        name="experts_back_out",
    )(d_expert_t, act)
    lined = join(ring.spread(2, grads), (dw_out,))
    give = take = add_small((dw_out,))
    d_w_out = lax.psum_scatter(dw_out, both, scatter_dimension=0, tiled=True)[0].astype(f32)
    keep, send = pl.pallas_call(
        functools.partial(experts_back_placed, ring.place_bits(), n_model),
        grid=(experts,),
        out_shape=(half_weights, half_weights),
        in_specs=[smem(), lhs_spec[1], rows_spec, hbm, hbm],
        out_specs=(half_spec, half_spec),
        compiler_params=params(),
        cost_estimate=cost(9),
        name="experts_back_in",
    )(me, x.T[None], d_hidden, lined, dw_out)
    give = take = add_small((keep,))
    with_tiny = per_device + tiny.shape[0]
    edges = (0, with_tiny, with_tiny + per_device, lined.shape[1])
    spread = [ring.spread(1, lined[:, low:high]) for low, high in zip(edges, edges[1:])]
    cored = core_sums(keep, send, 8, (give,), "sum_core_w")
    own = join(spread[0], (cored[0],))
    other = ring.swap(own, 1)
    give = take = add_small((own,))
    tiny_sum = jnp.sum(jnp.concatenate([own[:, per_device:], other[:, per_device:]]).astype(f32), axis=0)
    table_outs = scatter(0, 0, own, other, (), (give,))
    own = join(spread[1], (table_outs[0],))
    other = ring.swap(own, 1)
    give = take = add_small((own,))
    table_outs = scatter(1, 0, own, other, table_outs, (give,))
    own = join(spread[2], (table_outs[0],))
    other = ring.swap(own, 1)
    while distances:
        give = take = add_small((own,))
    table_outs = scatter(2, 0, own, other, table_outs, (give,))
    for pair in range(3, pairs):
        after = ()
        if pair == pairs - 1:
            planed = plane_sums(cored, 4, (table_outs[0],), "sum_plane_w")
            after = (planed[0],)
        table_outs = scatter(pair, (pair - 2) * per_device, own, other, table_outs, after)
    got = ring.swap(take, 1)
    small = jnp.concatenate([jnp.where(side == 0, take, got), jnp.where(side == 0, got, take)]).astype(f32)
    small = small.reshape(small_rows, lanes)
    d_tower_w = small[: tasks * features].reshape(tower_w.shape)
    d_gate_w = small[tasks * features :, : tasks * experts]
    d_gate_w = d_gate_w.reshape(features, tasks, experts).transpose(1, 0, 2)
    d_w_in = line_sum(planed)[0]
    tiny_sum = jnp.sum(tiny_sum.reshape(4, 8, lanes), axis=0)
    d_tower_v, loss_sum = tiny_sum[:tasks], tiny_sum[tasks, 0]
    table_new = tuple(v.reshape(table_count, emb_width, rows_own).transpose(0, 2, 1) for v in table_outs)
    w_in_new = nesterov(w_in, w_in_mom, w_in_avg, d_w_in, rates[1])
    w_out_new = nesterov(w_out_t, w_out_mom_t, w_out_avg_t, d_w_out, rates[2])
    w_out_new = tuple(v.transpose(0, 2, 1) for v in w_out_new)
    gate_new = nesterov(gate_w, gate_mom, gate_avg, d_gate_w, rates[3])
    tower_new = nesterov(tower_w, tower_w_mom, tower_w_avg, d_tower_w, rates[4])
    vector_new = nesterov(tower_v, tower_v_mom, tower_v_avg, d_tower_v, rates[5])
    return (loss_sum,) + table_new + w_in_new + w_out_new + gate_new + tower_new + vector_new


def solution(mesh):
    group_spec = P("dp", None)
    table_spec = P(None, both, None)
    placed = (
        (P("dp", None, None), group_spec, group_spec, group_spec)
        + (table_spec,) * 3
        + (P(None, "dp", "mp"),) * 3
        + (P(None, "mp", "dp"),) * 3
        + (P(),) * 9
    )
    return jax.shard_map(
        body,
        mesh=mesh,
        in_specs=placed,
        out_specs=(P(),)
        + (table_spec,) * 3
        + (P(None, "dp", "mp"),) * 3
        + (P(None, "mp", "dp"),) * 3
        + (P(),) * 9,
        check_vma=False,
    )
```

```python
import functools
import math

import jax
import jax.numpy as jnp
from jax import lax
from jax.experimental import pallas as pl
from jax.experimental.pallas import tpu as pltpu
from jax.sharding import PartitionSpec as P

mu_rate = 0.5
avg_decay = 0.5
task_weights = (1.0, 0.6, 0.8, 0.4, 1.2)
rates = (5000000.0, 12000.0, 3500.0, 1000.0, 370.0, 200.0)
both = ("dp", "mp")
lanes = 128
group = 32
window = 8
batch = 4
flag_bit = 20
f32, bf16, i32 = jnp.float32, jnp.bfloat16, jnp.int32
vmem_limit = 58 * 2**20


def bits_of(size):
    return int(size).bit_length() - 1


def cost(microseconds):
    return pl.CostEstimate(flops=int(microseconds * 1.1e9), bytes_accessed=int(microseconds * 3.0e6), transcendentals=0)


def params(limit=vmem_limit):
    return pltpu.CompilerParams(vmem_limit_bytes=limit)


def gelu_pair(h):
    scale = math.sqrt(2.0 / math.pi)
    square = h * h
    t = jnp.tanh(scale * h * (1.0 + 0.044715 * square))
    half = 0.5 * (1.0 + t)
    slope = half + 0.5 * h * (1.0 - t * t) * scale * (1.0 + 3.0 * 0.044715 * square)
    return h * half, slope


def nesterov(weight, moment, average, grad, rate):
    moment_new = mu_rate * moment + grad
    weight_new = weight - rate * (grad + mu_rate * moment_new)
    average_new = avg_decay * average + (1.0 - avg_decay) * weight_new
    return (weight_new, moment_new, average_new)


class Ring:
    def __init__(self, n_data, n_model):
        self.count = n_data * n_model
        tall = n_model // 2
        self.stages = (
            (0, 1),
            tuple(x * n_model + y * 2 for x in range(2) for y in range(tall)),
            tuple(z * 2 * n_model for z in range(n_data // 2)),
        )

    def offset_of(self, place):
        total = 0
        rest = place
        for stage in reversed(self.stages):
            digit = rest & (len(stage) - 1)
            rest = rest >> bits_of(len(stage))
            for bit in range(bits_of(len(stage))):
                total = total + ((digit >> bit) & 1) * stage[1 << bit]
        return total

    def device_at(self, me, place):
        return me ^ self.offset_of(place)

    def place_bits(self):
        places = {self.offset_of(place): place for place in range(self.count)}
        return [places[1 << bit] for bit in range(bits_of(self.count))]

    def swap(self, value, distance):
        return lax.ppermute(value, both, [(i, i ^ distance) for i in range(self.count)])

    def swap_pieces(self, stage, pieces):
        return [pieces[0]] + [self.swap(p, d) for p, d in zip(pieces[1:], self.stages[stage][1:])]

    def spread(self, stage, value):
        return [value] + [self.swap(value, d) for d in self.stages[stage][1:]]


def place_in(bits, offset):
    total = 0
    for bit, value in enumerate(bits):
        total = total + ((offset >> bit) & 1) * value
    return total


def sum_kernel(parts_in, parts_out, dtype, *refs):
    ins, outs = refs[:parts_in], refs[len(refs) - parts_out :]
    for k, out in enumerate(outs):
        total = ins[0][k].astype(f32)
        for ref in ins[1:]:
            total = total + ref[k].astype(f32)
        out[...] = total.astype(dtype)


def sum_pieces(parts, count, dtype, steps, after=(), name="sum"):
    length = parts[0].shape[0] // count
    rest = parts[0].shape[1:]
    fold = rest[:-2]
    blocks = length
    for size in fold:
        blocks = blocks * size
    steps = min(steps, blocks)
    each = blocks // steps
    tile = rest[-2:]
    views = [v.reshape((count, blocks) + tile) for v in parts]
    outs = pl.pallas_call(
        functools.partial(sum_kernel, len(parts), count, dtype),
        grid=(steps,),
        out_shape=[jax.ShapeDtypeStruct((blocks,) + tile, dtype)] * count,
        in_specs=[pl.BlockSpec((count, each) + tile, lambda i: (0, i, 0, 0))] * len(parts)
        + [pl.BlockSpec(memory_space=pl.ANY)] * len(after),
        out_specs=[pl.BlockSpec((each,) + tile, lambda i: (i, 0, 0))] * count,
        compiler_params=params(),
        name=name,
    )(*views, *after)
    return [v.reshape((length,) + rest) for v in outs]


def join_kernel(count, *refs):
    out = refs[-1]
    at = 0
    for ref in refs[:count]:
        out[at : at + ref.shape[0]] = ref[...]
        at += ref.shape[0]


def join(parts, after=()):
    total = sum(v.shape[0] for v in parts)
    anywhere = pl.BlockSpec(memory_space=pl.ANY)
    return pl.pallas_call(
        functools.partial(join_kernel, len(parts)),
        out_shape=jax.ShapeDtypeStruct((total,) + parts[0].shape[1:], parts[0].dtype),
        in_specs=[vmem()] * len(parts) + [anywhere] * len(after),
        out_specs=vmem(),
        compiler_params=params(),
        name="join",
    )(*parts, *after)


def held_until(value, after):
    anywhere = pl.BlockSpec(memory_space=pl.ANY)
    return pl.pallas_call(
        lambda *refs: None,
        out_shape=jax.ShapeDtypeStruct(value.shape, value.dtype),
        in_specs=[anywhere] * (1 + len(after)),
        out_specs=anywhere,
        input_output_aliases={0: 0},
        name="hold",
    )(value, *after)


def bucket_kernel(pairs, cap_rows, starts, keys, out):
    owners = out.shape[0]
    lane = lax.broadcasted_iota(i32, (1, lanes), 1)
    body_rows = -(-(cap_rows + 1) // 8) * 8

    def one(o, carry):
        off = starts[o * pairs]
        row = lax.shift_right_logical(off, 7)
        shift = off & (lanes - 1)
        block = keys[pl.ds(row, body_rows), :]
        turned = pltpu.roll(block, (lanes - shift) & (lanes - 1), 1)
        merged = jnp.where(lane < lanes - shift, turned[:cap_rows], turned[1 : cap_rows + 1])
        out[o, 0:cap_rows, :] = merged
        head = jnp.zeros((1, lanes), i32)
        for p in range(pairs + 1):
            head = jnp.where(lane == p, starts[o * pairs + p] - off, head)
        out[o, cap_rows : cap_rows + 1, :] = head
        return carry

    lax.fori_loop(0, owners, one, 0)


def prep_kernel(row_bits, sample_bits, entries, rows_out, samples_out):
    e = entries[...]
    rows = e & ((1 << row_bits) - 1)
    lane = lax.broadcasted_iota(i32, e.shape, 1)
    place = lane & (window - 1)
    clash = jnp.zeros(e.shape, i32)
    for d in range(1, window):
        other = pltpu.roll(rows, lanes - d, 1)
        clash = jnp.where((other == rows) & (place < window - d), 1, clash)
    step = 1
    while step < group:
        clash = clash | pltpu.roll(clash, lanes - step, 1)
        step *= 2
    rows_out[...] = jnp.where((lane & (group - 1)) == 0, rows | (clash << flag_bit), rows)
    samples_out[...] = lax.shift_right_logical(e, row_bits) & ((1 << sample_bits) - 1)


def one_hot(samples_ref, row, base, low, high, per_device, width):
    count = width // lanes
    s = jnp.concatenate([samples_ref[pl.ds(row + c, 1), :] for c in range(count)], axis=1)
    k = lax.broadcasted_iota(i32, (1, width), 1) + base
    s = jnp.where((k >= low) & (k < high), s, -1).astype(f32).astype(bf16)
    place = lax.broadcasted_iota(i32, (per_device, width), 0).astype(f32).astype(bf16)
    return jnp.where(place == s, jnp.ones((), bf16), jnp.zeros((), bf16))


class Lists:
    def __init__(self, ring, me, rows, held, sems):
        self.ring, self.me, self.rows, self.held, self.sems = ring, me, rows, held, sems
        self.length = held.shape[0] // (2 * batch)
        self.batches = rows.shape[0] // self.length // batch

    def copies(self, n):
        slot = n & 1
        found = []
        for b in range(batch):
            sender = self.ring.device_at(self.me[0], n * batch + b)
            source = self.rows.at[pl.ds(pl.multiple_of(sender * self.length, 1024), self.length)]
            held = self.held.at[pl.ds(pl.multiple_of((slot * batch + b) * self.length, 1024), self.length)]
            found.append(pltpu.make_async_copy(source, held, self.sems.at[slot, b]))
        return found

    def start(self, n):
        for copy in self.copies(n):
            copy.start()

    def wait(self, n):
        for copy in self.copies(n):
            copy.wait()

    def run(self, step):
        self.start(0)

        def one(n, carry):
            @pl.when(n + 1 < self.batches)
            def _():
                self.start(n + 1)

            self.wait(n)
            step(n)
            return carry

        lax.fori_loop(0, self.batches, one, 0)

    def first(self, n, b, at):
        return ((n & 1) * batch + b) * self.length + at

    def entry(self, place):
        return self.held[place] & ((1 << flag_bit) - 1)

    def clash(self, place):
        return lax.shift_right_logical(self.held[place], flag_bit)


def gather_kernel(ring, first_pair, at, per_device, cap, me, bounds, rows, samples, table, *refs):
    keep, send, rows_f, stage, pooled, held, sems, out_sem = refs[-8:]
    step = pl.program_id(0)
    pair = first_pair + step
    rows_own = table.shape[2]
    width = min(256, cap)
    cap_rows = cap // lanes
    blocks = cap // width
    span = 256
    lane = lax.broadcasted_iota(i32, (span, lanes), 1)
    same = lax.broadcasted_iota(i32, (span, span), 0) == lax.broadcasted_iota(i32, (span, span), 1)
    unit = jnp.where(same, 1.0, 0.0).astype(bf16)

    def turn(c, carry):
        at = pl.multiple_of(c * span, span)
        t = table[0, :, pl.ds(at, span)].astype(bf16)
        t = lax.dot_general(unit, t, (((1,), (1,)), ((), ())), preferred_element_type=f32)
        rows_f[pl.ds(at, span), :] = jnp.where(lane < lanes // 2, t, 0.0)
        at_odd = pl.multiple_of(c * span + rows_own, span)
        rows_f[pl.ds(at_odd, span), :] = jnp.where(lane < lanes // 2, 0.0, t)
        return carry

    lax.fori_loop(0, rows_own // span, turn, 0, unroll=8)
    stage[...] = jnp.zeros(stage.shape, f32)
    lists = Lists(ring, me, rows, held, sems)

    def some(n):
        senders = [ring.device_at(me[0], n * batch + b) for b in range(batch)]
        lows = [bounds[s * 8 + pair] for s in senders]
        highs = [bounds[s * 8 + pair + 1] for s in senders]
        for b in range(batch):

            def fetch(i, c):
                at = pl.multiple_of(i * group, group)
                first = lists.first(n, b, at)
                for u in range(group):
                    r = held[first + u] if u else lists.entry(first)
                    stage[b, pl.ds(at + u, 1), :] = rows_f[pl.ds(r, 1), :]
                return c

            lax.fori_loop(lax.div(lows[b], group), lax.div(highs[b] + group - 1, group), fetch, 0)

        def term(b, i):
            block = jnp.minimum(i, blocks - 1)
            row = senders[b] * cap_rows + block * (width // lanes)
            hot = one_hot(samples, row, i * width, lows[b], highs[b], per_device, width)
            fetched = stage[b, pl.ds(pl.multiple_of(block * width, width), width), :].astype(bf16)
            return jnp.dot(hot, fetched, preferred_element_type=f32)

        shift = bits_of(width)
        begins = [lax.shift_right_logical(low, shift) for low in lows]
        def put(b, total):
            pooled[pl.ds(n * batch + b, 1)] = total.astype(bf16)[None]

        for b in range(batch):
            put(b, term(b, begins[b]) + term(b, begins[b] + 1))
        for b in range(batch):

            @pl.when(highs[b] > (begins[b] + 2) * width)
            def _():
                total = lax.fori_loop(
                    begins[b],
                    lax.shift_right_logical(highs[b] + width - 1, shift),
                    lambda i, t: t + term(b, i),
                    jnp.zeros((per_device, lanes), f32),
                )
                put(b, total)

    lists.run(some)
    half = keep.shape[0]
    copies = [
        pltpu.make_async_copy(pooled.at[pl.ds(i * half, half)], ref.at[:, at + step], out_sem.at[i])
        for i, ref in enumerate((keep, send))
    ]
    for copy in copies:
        copy.start()
    for copy in copies:
        copy.wait()


def scatter_kernel(
    ring, pair, rows_at, per_device, cap, me, bounds, rows, samples, own, other, w_in, m_in, a_in, *refs
):
    w_out, m_out, a_out, sums, stage, grads, w_buf, m_buf, a_buf, held, sems, grad_sem, in_sem, out_sem = refs[-14:]
    blocks_each = own.shape[0]
    arrivals = [
        pltpu.make_async_copy(ref.at[:, pl.ds(rows_at, per_device)], grads.at[pl.ds(i * blocks_each, blocks_each)], grad_sem.at[i])
        for i, ref in enumerate((own, other))
    ]
    for arrival in arrivals:
        arrival.start()
    rows_own = w_in.shape[2]
    width = min(256, cap)
    cap_rows = cap // lanes
    blocks = cap // width
    sources = (w_in, m_in, a_in)
    targets = (w_out, m_out, a_out)
    buffers = (w_buf, m_buf, a_buf)
    sums[...] = jnp.zeros(sums.shape, f32)
    lists = Lists(ring, me, rows, held, sems)
    for arrival in arrivals:
        arrival.wait()
    for i in range(3):
        pltpu.make_async_copy(sources[i].at[pair], buffers[i], in_sem.at[i]).start()

    def some(n):
        senders = [ring.device_at(me[0], n * batch + b) for b in range(batch)]
        lows = [bounds[s * 8 + pair] for s in senders]
        highs = [bounds[s * 8 + pair + 1] for s in senders]

        def spread(b, i):
            block = jnp.minimum(i, blocks - 1)
            row = senders[b] * cap_rows + block * (width // lanes)
            hot = one_hot(samples, row, block * width, lows[b], highs[b], per_device, width)
            mine = grads[n * batch + b]
            stage[b, pl.ds(pl.multiple_of(block * width, width), width), :] = lax.dot_general(
                hot, mine, (((0,), (0,)), ((), ())), preferred_element_type=f32
            )

        shift = bits_of(width)
        begins = [lax.shift_right_logical(low, shift) for low in lows]
        for b in range(batch):
            spread(b, begins[b])
            spread(b, begins[b] + 1)
        for b in range(batch):

            @pl.when(highs[b] > (begins[b] + 2) * width)
            def _():
                def more(i, c):
                    spread(b, i)
                    return c

                lax.fori_loop(begins[b] + 2, lax.shift_right_logical(highs[b] + width - 1, shift), more, 0)

        for b in range(batch):

            def add(i, c):
                at = pl.multiple_of(i * group, group)
                first = lists.first(n, b, at)

                def apart():
                    for start in range(0, group, window):
                        places = [held[first + u] if u else lists.entry(first) for u in range(start, start + window)]
                        olds = [sums[pl.ds(r, 1), :] for r in places]
                        news = [stage[b, pl.ds(at + start + u, 1), :] for u in range(window)]
                        for r, old, new in zip(places, olds, news):
                            sums[pl.ds(r, 1), :] = old + new

                def in_turn():
                    def single(u, inner):
                        r = lists.entry(first + u)
                        sums[pl.ds(r, 1), :] = sums[pl.ds(r, 1), :] + stage[b, pl.ds(at + u, 1), :]
                        return inner

                    lax.fori_loop(0, group, single, 0)

                lax.cond(lists.clash(first) == 0, apart, in_turn)
                return c

            lax.fori_loop(lax.div(lows[b], group), lax.div(highs[b] + group - 1, group), add, 0)

    lists.run(some)
    for i in range(3):
        pltpu.make_async_copy(sources[i].at[pair], buffers[i], in_sem.at[i]).wait()
    chunks = out_sem.shape[0] // 3
    chunk = rows_own // chunks
    span = min(256, chunk)
    lane = lax.broadcasted_iota(i32, (span, lanes), 1)

    def copies(n):
        part = pl.ds(n * chunk, chunk)
        return [
            pltpu.make_async_copy(buffers[i].at[:, part], targets[i].at[pair, :, part], out_sem.at[n * 3 + i])
            for i in range(3)
        ]

    for n in range(chunks):

        def update(c, carry):
            at = pl.multiple_of(n * chunk + c * span, span)
            even = sums[pl.ds(at, span), :]
            odd = sums[pl.ds(pl.multiple_of(at + rows_own, span), span), :]
            grad = jnp.where(lane < lanes // 2, even, odd).T
            part = (slice(None), pl.ds(at, span))
            new = nesterov(w_buf[part], m_buf[part], a_buf[part], grad, rates[0])
            w_buf[part] = new[0]
            m_buf[part] = new[1]
            a_buf[part] = new[2]
            return carry

        lax.fori_loop(0, chunk // span, update, 0)
        for copy in copies(n):
            copy.start()
    for n in range(chunks):
        for copy in copies(n):
            copy.wait()


rows_first = (((0,), (0,)), ((), ()))
last_last = (((1,), (1,)), ((), ()))


def experts_forward(x_ref, weight_ref, y_ref, act_ref, slope_ref):
    x = x_ref[...]
    total = None
    for m in range(weight_ref.shape[1]):
        w_in, w_out = (weight_ref[:, m, i, 0].reshape(-1, weight_ref.shape[-1]) for i in range(2))
        act, slope = gelu_pair(jnp.dot(x, w_in, preferred_element_type=f32))
        act = act.astype(bf16)
        act_ref[0, m] = act
        slope_ref[0, m] = slope.astype(bf16)
        term = lax.dot_general(act, w_out, last_last, preferred_element_type=f32)
        total = term if total is None else total + term
    y_ref[0] = total


def experts_back_rows(pairs, d_ref, weight_ref, slope_ref, dxg_ref, inv_ref, d_hidden_ref, *refs):
    grads, dx = refs[:pairs], refs[pairs]
    d_out = d_ref[0]
    total = None
    for m in range(weight_ref.shape[1]):
        w_in, w_out = (weight_ref[:, m, i, 0].reshape(-1, weight_ref.shape[-1]) for i in range(2))
        d_act = jnp.dot(d_out, w_out, preferred_element_type=f32)
        d_hidden = (d_act * slope_ref[0, m].astype(f32)).astype(bf16)
        d_hidden_ref[0, m] = d_hidden
        term = lax.dot_general(d_hidden, w_in, last_last, preferred_element_type=f32)
        total = term if total is None else total + term

    @pl.when(pl.program_id(0) == 0)
    def _():
        dx[...] = dxg_ref[...] + total

    @pl.when(pl.program_id(0) != 0)
    def _():
        dx[...] += total

    @pl.when(pl.program_id(0) == pl.num_programs(0) - 1)
    def _():
        for p in range(pairs):
            part = (slice(None), slice(p * lanes, (p + 1) * lanes))
            grads[p][...] = (dx[part] * inv_ref[part]).astype(bf16)


def experts_back_weights(n_model, lhs_ref, rows_ref, *refs):
    dw_ref = refs[-1]
    devices, _, f_own, _ = dw_ref.shape
    lhs = lhs_ref[0]
    for m in range(n_model):
        out = jnp.dot(lhs, rows_ref[0, m], preferred_element_type=f32).astype(bf16)
        for d in range(devices // n_model):
            dw_ref[d * n_model + m, 0] = out[d * f_own : (d + 1) * f_own]


def experts_back_placed(bits, n_model, me, lhs_ref, rows_ref, *refs):
    keep, send = refs[-2:]
    half, _, f_own, h_own = keep.shape
    model = me[0] & (n_model - 1)
    data = me[0] ^ model
    bits = [0] + bits[1:]
    lhs = lhs_ref[0]
    for beside in range(n_model):
        out = jnp.dot(lhs, rows_ref[0, pl.ds(model ^ beside, 1)][0], preferred_element_type=f32).astype(bf16)
        to = send if beside & 1 else keep
        for d in range(2 * half // n_model):
            place = place_in(bits, (data ^ (d * n_model)) | (beside & (n_model - 2)))
            to[pl.ds(place, 1), 0] = out[d * f_own : (d + 1) * f_own][None]


def head_kernel(
    sample_total, x_ref, y_ref, gate_ref, tower_ref, v_ref, label_ref,
    d_expert_ref, d_expert_t_ref, dxg_ref, d_tower_ref, d_gate_ref, small_ref, probs, mixed, d_mixed, d_gate, inner,
):
    experts, rows, features = y_ref.shape
    tasks = tower_ref.shape[0]
    x = x_ref[...]
    gate = gate_ref[...]
    logits = jnp.dot(x, gate, preferred_element_type=f32)
    task_of = lax.shift_right_logical(lax.broadcasted_iota(i32, (1, lanes), 1), bits_of(experts))

    def by_task(fold, value, fill):
        total = jnp.zeros(value.shape, f32)
        for k in range(tasks):
            found = fold(jnp.where(task_of == k, value, fill), axis=1, keepdims=True)
            total = jnp.where(task_of == k, found, total)
        return total

    used = task_of < tasks
    raised = jnp.where(used, jnp.exp(logits - by_task(jnp.max, logits, -jnp.inf)), 0.0)
    probs[...] = raised / jnp.where(used, by_task(jnp.sum, raised, 0.0), 1.0)
    span = 16
    parts = 2
    wide = features // parts

    def mix(r, carry):
        part = pl.ds(pl.multiple_of(r * span, span), span)
        p = probs[part, :]
        for h in range(parts):
            across = slice(h * wide, (h + 1) * wide)
            totals = [None] * tasks
            for e in range(experts):
                y = y_ref[e, part, across]
                for k in range(tasks):
                    c = k * experts + e
                    more = p[:, c : c + 1] * y
                    totals[k] = more if e == 0 else totals[k] + more
            for k in range(tasks):
                mixed[k, part, across] = totals[k].astype(bf16)
        return carry

    lax.fori_loop(0, rows // span, mix, 0)
    loss = jnp.zeros((1, 1), f32)
    vectors = []
    for k in range(tasks):
        tower = tower_ref[k]
        act, slope = gelu_pair(jnp.dot(mixed[k], tower, preferred_element_type=f32))
        v = v_ref[k : k + 1, :]
        logit = jnp.sum(act * v, axis=1, keepdims=True)
        label = label_ref[:, k : k + 1]
        weighting = task_weights[k] * label_ref[:, tasks + k : tasks + k + 1]
        small_exp = jnp.exp(-jnp.abs(logit))
        softplus = jnp.maximum(logit, 0.0) + jnp.log1p(small_exp)
        loss = loss + jnp.sum(weighting * (softplus - label * logit), axis=0, keepdims=True)
        sigmoid = jnp.where(logit >= 0.0, 1.0, small_exp) / (1.0 + small_exp)
        d_logit = weighting * (sigmoid - label) / sample_total
        vectors.append(jnp.sum(d_logit * act, axis=0, keepdims=True))
        d_pre = (d_logit * v * slope).astype(bf16)
        d_mixed[k] = lax.dot_general(d_pre, tower, last_last, preferred_element_type=f32)
        d_tower_ref[k] = lax.dot_general(mixed[k], d_pre, rows_first, preferred_element_type=f32).astype(bf16)
    lane = lax.broadcasted_iota(i32, (span, lanes), 1)
    ones = jnp.ones((lanes, lanes), bf16)

    def back(r, carry):
        part = pl.ds(pl.multiple_of(r * span, span), span)
        p = probs[part, :]
        for e in range(experts):
            y = y_ref[e, part, :]
            total = None
            for k in range(tasks):
                c = k * experts + e
                d = d_mixed[k, part, :]
                product = d * y
                narrow = product[:, :lanes]
                for t in range(1, features // lanes):
                    narrow = narrow + product[:, t * lanes : (t + 1) * lanes]
                coarse = narrow.astype(bf16)
                inner[0, c * span : (c + 1) * span, :] = coarse
                inner[1, c * span : (c + 1) * span, :] = (narrow - coarse.astype(f32)).astype(bf16)
                more = p[:, c : c + 1] * d
                total = more if k == 0 else total + more
            d_expert_ref[e, part, :] = total.astype(bf16)
        row_sums = jnp.dot(inner[0], ones, preferred_element_type=f32)
        row_sums = row_sums + jnp.dot(inner[1], ones, preferred_element_type=f32)
        d_probs = jnp.zeros((span, lanes), f32)
        for c in range(tasks * experts):
            d_probs = jnp.where(lane == c, row_sums[c * span : (c + 1) * span], d_probs)
        d_gate[part, :] = (p * (d_probs - by_task(jnp.sum, p * d_probs, 0.0))).astype(bf16)
        return carry

    lax.fori_loop(0, rows // span, back, 0)
    for e in range(experts):
        d_expert_t_ref[e] = d_expert_ref[e].T
    dxg_ref[...] = lax.dot_general(d_gate[...], gate, last_last, preferred_element_type=f32)
    d_gate_ref[...] = lax.dot_general(x, d_gate[...], rows_first, preferred_element_type=f32).astype(bf16)
    line = lax.broadcasted_iota(i32, (8, lanes), 0)
    tile = jnp.where(line == tasks, loss, 0.0)
    for k in range(tasks):
        tile = jnp.where(line == k, vectors[k], tile)
    pieces = []
    for _ in range(4):
        piece = tile.astype(bf16)
        pieces.append(piece)
        tile = tile - piece.astype(f32)
    small_ref[...] = jnp.concatenate(pieces, axis=0)


def smem():
    return pl.BlockSpec(memory_space=pltpu.SMEM)


def vmem():
    return pl.BlockSpec(memory_space=pltpu.VMEM)


def body(
    row_ids, bag_counts, labels, label_mask, tables, table_mom, table_avg, w_in, w_in_mom, w_in_avg,
    w_out, w_out_mom, w_out_avg, gate_w, gate_mom, gate_avg, tower_w, tower_w_mom, tower_w_avg,
    tower_v, tower_v_mom, tower_v_avg,
):
    n_model = lax.axis_size("mp")
    n_data = lax.axis_size("dp")
    devices = n_data * n_model
    ring = Ring(n_data, n_model)
    mp_rank = lax.axis_index("mp")
    me = (lax.axis_index("dp") * n_model + mp_rank).astype(i32).reshape(1)
    per_group, table_count, bag_size = row_ids.shape
    per_device = per_group // n_model
    rows_own = tables.shape[1]
    emb_width = tables.shape[2]
    features = table_count * emb_width
    pairs = features // lanes
    sample_total = float(per_group * n_data)
    slot_total = per_device * table_count * bag_size
    cap = 2 * slot_total // devices
    cap_rows = cap // lanes

    w_out_t, w_out_mom_t, w_out_avg_t = (v.transpose(0, 2, 1) for v in (w_out, w_out_mom, w_out_avg))
    experts, f_own, h_own = w_in.shape
    weights = jnp.stack([w_in, w_out_t]).astype(bf16)
    weights = lax.all_gather(weights, both, axis=0).reshape(n_data, n_model, 2, experts, f_own, h_own)

    row_bits = bits_of(rows_own) + 1
    sample_bits = bits_of(per_device)
    start = mp_rank * per_device
    ids = lax.dynamic_slice_in_dim(row_ids.transpose(1, 2, 0), start, per_device, 2)
    counts = lax.dynamic_slice_in_dim(bag_counts.T, start, per_device, 1)
    live = lax.broadcasted_iota(i32, ids.shape, 1) < counts[:, None, :]
    table_of = lax.broadcasted_iota(i32, ids.shape, 0)
    bucket = lax.shift_right_logical(ids, row_bits - 1) * pairs + lax.shift_right_logical(table_of, 1)
    key = (bucket << sample_bits) | lax.broadcasted_iota(i32, ids.shape, 2)
    key = (((key << 1) | (table_of & 1)) << (row_bits - 1)) | (ids & (rows_own - 1))
    key = jnp.where(live, key, 1 << 30).reshape(-1)
    ordered = lax.sort(key)
    bucket_sorted = lax.shift_right_logical(ordered, row_bits + sample_bits)
    starts = jnp.sum(
        (bucket_sorted[None, :] < jnp.arange(devices * pairs + 1, dtype=i32)[:, None]).astype(i32), axis=1
    )
    padded = jnp.concatenate([ordered.reshape(-1, lanes), jnp.zeros((cap_rows + 8, lanes), i32)], axis=0)
    out_rows = -(-(cap_rows + 1) // 8) * 8
    outgoing = pl.pallas_call(
        functools.partial(bucket_kernel, pairs, cap_rows),
        out_shape=jax.ShapeDtypeStruct((devices, out_rows, lanes), i32),
        in_specs=[smem(), vmem()],
        out_specs=vmem(),
        name="bucket",
    )(starts, padded)
    received = lax.all_to_all(outgoing, both, split_axis=0, concat_axis=0, tiled=True)
    bounds = received[:, cap_rows, :8].reshape(-1)
    entries = received[:, :cap_rows].reshape(devices * cap_rows, lanes)
    entry_shape = jax.ShapeDtypeStruct(entries.shape, i32)
    rows, samples = pl.pallas_call(
        functools.partial(prep_kernel, row_bits, sample_bits),
        out_shape=(entry_shape, entry_shape),
        in_specs=[vmem()],
        out_specs=(vmem(), vmem()),
        name="prep",
    )(entries)
    length = max(cap, 1024)
    rows = jnp.pad(rows.reshape(devices, cap), ((0, 0), (0, length - cap))).reshape(-1)
    hbm = pl.BlockSpec(memory_space=pl.ANY)
    list_scratch = [pltpu.SMEM((2 * batch * length,), i32), pltpu.SemaphoreType.DMA((2, batch))]

    paired = tuple(
        v.transpose(0, 2, 1).reshape(pairs, lanes, rows_own) for v in (tables, table_mom, table_avg)
    )
    half = devices // 2
    half_shape = jax.ShapeDtypeStruct((half, per_device, lanes), bf16)

    def gather(first_pair, count, at, total, olds, after):
        out_shape = jax.ShapeDtypeStruct((half, total, per_device, lanes), bf16)
        return pl.pallas_call(
            functools.partial(gather_kernel, ring, first_pair, at, per_device, cap),
            grid=(count,),
            out_shape=(out_shape, out_shape),
            in_specs=[
                smem(), smem(), hbm, vmem(),
                pl.BlockSpec((1, lanes, rows_own), lambda i: (first_pair + i, 0, 0)),
            ] + [hbm] * (len(olds) + len(after)),
            out_specs=(hbm, hbm),
            scratch_shapes=[
                pltpu.VMEM((2 * rows_own, lanes), f32),
                pltpu.VMEM((batch, cap, lanes), f32),
                pltpu.VMEM((devices, per_device, lanes), bf16),
            ] + list_scratch + [pltpu.SemaphoreType.DMA((2,))],
            input_output_aliases={5: 0, 6: 1} if olds else {},
            compiler_params=params(),
            cost_estimate=cost(16 * count),
            name="gather",
        )(me, bounds, rows, samples, paired[0], *olds, *after)

    plane, line = len(ring.stages[1]), len(ring.stages[2])
    each = half // plane

    def core_sums(keep, send, steps, after=(), name="sum_core"):
        return sum_pieces([keep, ring.swap(send, 1)], plane, bf16, steps, after, name)

    def plane_sums(pieces, steps, after=(), name="sum_plane"):
        return sum_pieces(ring.swap_pieces(1, pieces), line, bf16, steps, after, name)

    def line_sum(pieces):
        total = None
        for piece in ring.swap_pieces(2, pieces):
            total = piece.astype(f32) if total is None else total + piece.astype(f32)
        return total

    early = pairs // 2
    rest = pairs - early
    cored_early = core_sums(*gather(0, early, 0, early, (), ()), 2)
    late = gather(early, rest - 1, 0, rest, (), ())
    late = gather(pairs - 1, 1, rest - 1, rest, late, (cored_early[0],))
    planed_early = plane_sums(cored_early, 1)
    cored_late = core_sums(late[0], held_until(late[1], (planed_early[0],)), 2)
    planed_late = plane_sums(cored_late, 1)
    pooled = jnp.concatenate([line_sum(planed_early)[0], line_sum(planed_late)[0]], axis=0)
    inverse = jnp.repeat(1.0 / counts.T.astype(f32), emb_width, axis=1)
    x = (pooled.transpose(1, 0, 2).reshape(per_device, features) * inverse).astype(bf16)

    hidden_shape = jax.ShapeDtypeStruct((experts, n_model, per_device, h_own), bf16)
    weight_spec = pl.BlockSpec((n_data, n_model, 2, 1, f_own, h_own), lambda e: (0, 0, 0, e, 0, 0))
    hidden_spec = pl.BlockSpec((1, n_model, per_device, h_own), lambda e: (e, 0, 0, 0))
    expert_spec = pl.BlockSpec((1, per_device, features), lambda e: (e, 0, 0))
    whole_spec = pl.BlockSpec((per_device, features), lambda e: (0, 0))
    y, act, slope = pl.pallas_call(
        experts_forward,
        grid=(experts,),
        out_shape=(jax.ShapeDtypeStruct((experts, per_device, features), f32), hidden_shape, hidden_shape),
        in_specs=[whole_spec, weight_spec],
        out_specs=(expert_spec, hidden_spec, hidden_spec),
        compiler_params=params(),
        cost_estimate=cost(16),
        name="experts_forward",
    )(x, weights)
    tasks, _, tower_width = tower_w.shape
    spare = lanes - tasks * experts
    gate_low = jnp.pad(gate_w.transpose(1, 0, 2).reshape(features, tasks * experts), ((0, 0), (0, spare))).astype(bf16)
    label_rows = lax.dynamic_slice_in_dim(labels, start, per_device, 0)
    mask_rows = lax.dynamic_slice_in_dim(label_mask, start, per_device, 0)
    marks = jnp.concatenate([label_rows, mask_rows], axis=1).astype(f32)
    d_expert, d_expert_t, d_x_gate, d_tower_part, d_gate_part, tiny = pl.pallas_call(
        functools.partial(head_kernel, sample_total),
        out_shape=(
            jax.ShapeDtypeStruct((experts, per_device, features), bf16),
            jax.ShapeDtypeStruct((experts, features, per_device), bf16),
            jax.ShapeDtypeStruct((per_device, features), f32),
            jax.ShapeDtypeStruct(tower_w.shape, bf16),
            jax.ShapeDtypeStruct((features, lanes), bf16),
            jax.ShapeDtypeStruct((32, lanes), bf16),
        ),
        in_specs=[vmem()] * 6,
        out_specs=(vmem(),) * 6,
        scratch_shapes=[
            pltpu.VMEM((per_device, lanes), f32),
            pltpu.VMEM((tasks, per_device, features), bf16),
            pltpu.VMEM((tasks, per_device, features), f32),
            pltpu.VMEM((per_device, lanes), bf16),
            pltpu.VMEM((2, 16 * tasks * experts, lanes), bf16),
        ],
        compiler_params=params(),
        cost_estimate=cost(12),
        name="towers",
    )(x, y, gate_low, tower_w.astype(bf16), tower_v, marks)
    grads_shape = jax.ShapeDtypeStruct((per_device, lanes), bf16)
    d_hidden, *grads = pl.pallas_call(
        functools.partial(experts_back_rows, pairs),
        grid=(experts,),
        out_shape=(hidden_shape,) + (grads_shape,) * pairs,
        in_specs=[expert_spec, weight_spec, hidden_spec, whole_spec, whole_spec],
        out_specs=(hidden_spec,) + (pl.BlockSpec((per_device, lanes), lambda e: (0, 0)),) * pairs,
        scratch_shapes=[pltpu.VMEM((per_device, features), f32)],
        compiler_params=params(),
        cost_estimate=cost(14),
        name="experts_back_rows",
    )(d_expert, weights, slope, d_x_gate, inverse)
    grads = jnp.concatenate([grads[0], tiny] + grads[1:], axis=0)[None]

    lhs_spec = [
        pl.BlockSpec((1, features, per_device), lambda e, single=single: (0 if single else e, 0, 0))
        for single in (False, True)
    ]
    rows_spec = pl.BlockSpec((1, n_model, per_device, h_own), lambda e: (e, 0, 0, 0))
    half_weights = jax.ShapeDtypeStruct((half, experts, f_own, h_own), bf16)
    half_spec = pl.BlockSpec((half, 1, f_own, h_own), lambda e: (0, e, 0, 0))

    paired_shape = jax.ShapeDtypeStruct(paired[0].shape, f32)
    chunks = 4

    def scatter(pair, at, own, other, olds, after):
        in_specs = [smem(), smem(), hbm, vmem()] + [hbm] * (5 + len(olds) + len(after))
        return pl.pallas_call(
            functools.partial(scatter_kernel, ring, pair, at, per_device, cap),
            out_shape=(paired_shape,) * 3,
            in_specs=in_specs,
            out_specs=(hbm, hbm, hbm),
            scratch_shapes=[
                pltpu.VMEM((2 * rows_own, lanes), f32),
                pltpu.VMEM((batch, cap, lanes), f32),
                pltpu.VMEM((devices, per_device, lanes), bf16),
                pltpu.VMEM((lanes, rows_own), f32),
                pltpu.VMEM((lanes, rows_own), f32),
                pltpu.VMEM((lanes, rows_own), f32),
                *list_scratch,
                pltpu.SemaphoreType.DMA((2,)),
                pltpu.SemaphoreType.DMA((3,)),
                pltpu.SemaphoreType.DMA((3 * chunks,)),
            ],
            input_output_aliases={9: 0, 10: 1, 11: 2} if olds else {},
            compiler_params=params(),
            cost_estimate=cost(26),
            name="scatter",
        )(me, bounds, rows, samples, own, other, *paired, *olds, *after)

    small_rows = tasks * features + features
    small = jnp.concatenate([d_tower_part.reshape(-1, lanes), d_gate_part], axis=0).reshape(2, 1, small_rows // 2, lanes)
    side = me[0] & 1
    give = lax.dynamic_index_in_dim(small, 1 - side, 0, keepdims=False)
    take = lax.dynamic_index_in_dim(small, side, 0, keepdims=False)
    dw_out = pl.pallas_call(
        functools.partial(experts_back_weights, n_model),
        grid=(experts,),
        out_shape=jax.ShapeDtypeStruct((devices, experts, f_own, h_own), bf16),
        in_specs=[lhs_spec[0], rows_spec],
        out_specs=pl.BlockSpec((devices, 1, f_own, h_own), lambda e: (0, e, 0, 0)),
        compiler_params=params(),
        cost_estimate=cost(9),
        name="experts_back_out",
    )(d_expert_t, act)
    lined = join(ring.spread(2, grads), (dw_out,))
    small = sum_pieces([take, ring.swap(give, 1)], 1, bf16, 1, (dw_out,), "sum_small")[0]
    d_w_out = lax.psum_scatter(dw_out, both, scatter_dimension=0, tiled=True)[0].astype(f32)
    keep, send = pl.pallas_call(
        functools.partial(experts_back_placed, ring.place_bits(), n_model),
        grid=(experts,),
        out_shape=(half_weights, half_weights),
        in_specs=[smem(), lhs_spec[1], rows_spec, hbm, hbm],
        out_specs=(half_spec, half_spec),
        compiler_params=params(),
        cost_estimate=cost(9),
        name="experts_back_in",
    )(me, x.T[None], d_hidden, lined, small)
    with_tiny = per_device + tiny.shape[0]
    edges = (0, with_tiny, lined.shape[1])
    spread = [ring.spread(1, lined[:, low:high]) for low, high in zip(edges, edges[1:])]
    far = [1 << bit for bit in range(3, bits_of(devices))] + [2, 4]

    def add_small(small, after, count=1):
        for distance in far[:count]:
            small = sum_pieces([small, ring.swap(small, distance)], 1, bf16, 1, after, "sum_small")[0]
        del far[:count]
        return small

    small = add_small(small, (keep,))
    own = join(spread[0], (small,))
    other = ring.swap(own, 1)
    send = held_until(send, (own,))
    sent = ring.swap(send, 1)
    tiny_sum = jnp.sum(jnp.concatenate([own[:, per_device:], other[:, per_device:]]).astype(f32), axis=0)
    table_outs = scatter(0, 0, own, other, (), ())
    small = add_small(small, (table_outs[0],))
    own = join(spread[1], (small,))
    other = ring.swap(own, 1)
    cored = sum_pieces([keep, sent], plane, bf16, 8, (own,), "sum_core_w")
    for pair in range(1, pairs):
        if pair == pairs - 1:
            planed = plane_sums(cored, 4, (table_outs[0],), "sum_plane_w")
            small = add_small(small, (planed[0],), len(far))
            after = (small,)
        elif pair == 1:
            after = (cored[0],)
        else:
            small = add_small(small, (table_outs[0],))
            after = (small,)
        table_outs = scatter(pair, (pair - 1) * per_device, own, other, table_outs, after)
    take = small
    got = ring.swap(take, 1)
    small = jnp.concatenate([jnp.where(side == 0, take, got), jnp.where(side == 0, got, take)]).astype(f32)
    small = small.reshape(small_rows, lanes)
    d_tower_w = small[: tasks * features].reshape(tower_w.shape)
    d_gate_w = small[tasks * features :, : tasks * experts]
    d_gate_w = d_gate_w.reshape(features, tasks, experts).transpose(1, 0, 2)
    d_w_in = line_sum(planed)[0]
    tiny_sum = jnp.sum(tiny_sum.reshape(4, 8, lanes), axis=0)
    d_tower_v, loss_sum = tiny_sum[:tasks], tiny_sum[tasks, 0]
    table_new = tuple(v.reshape(table_count, emb_width, rows_own).transpose(0, 2, 1) for v in table_outs)
    w_in_new = nesterov(w_in, w_in_mom, w_in_avg, d_w_in, rates[1])
    w_out_new = nesterov(w_out_t, w_out_mom_t, w_out_avg_t, d_w_out, rates[2])
    w_out_new = tuple(v.transpose(0, 2, 1) for v in w_out_new)
    gate_new = nesterov(gate_w, gate_mom, gate_avg, d_gate_w, rates[3])
    tower_new = nesterov(tower_w, tower_w_mom, tower_w_avg, d_tower_w, rates[4])
    vector_new = nesterov(tower_v, tower_v_mom, tower_v_avg, d_tower_v, rates[5])
    return (loss_sum,) + table_new + w_in_new + w_out_new + gate_new + tower_new + vector_new


def solution(mesh):
    group_spec = P("dp", None)
    table_spec = P(None, both, None)
    placed = (
        (P("dp", None, None), group_spec, group_spec, group_spec)
        + (table_spec,) * 3
        + (P(None, "dp", "mp"),) * 3
        + (P(None, "mp", "dp"),) * 3
        + (P(),) * 9
    )
    return jax.shard_map(
        body,
        mesh=mesh,
        in_specs=placed,
        out_specs=(P(),)
        + (table_spec,) * 3
        + (P(None, "dp", "mp"),) * 3
        + (P(None, "mp", "dp"),) * 3
        + (P(),) * 9,
        check_vma=False,
    )
```

```python
import functools
import math

import jax
import jax.numpy as jnp
from jax import lax
from jax.experimental import pallas as pl
from jax.experimental.pallas import tpu as pltpu
from jax.sharding import PartitionSpec as P

mu_rate = 0.5
avg_decay = 0.5
task_weights = (1.0, 0.6, 0.8, 0.4, 1.2)
rates = (5000000.0, 12000.0, 3500.0, 1000.0, 370.0, 200.0)
both = ("dp", "mp")
lanes = 128
group = 64
window = 8
batch = 4
flag_bit = 20
f32, bf16, i32 = jnp.float32, jnp.bfloat16, jnp.int32
vmem_limit = 58 * 2**20


def bits_of(size):
    return int(size).bit_length() - 1


def cost(microseconds):
    return pl.CostEstimate(flops=int(microseconds * 1.1e9), bytes_accessed=int(microseconds * 3.0e6), transcendentals=0)


def params(limit=vmem_limit):
    return pltpu.CompilerParams(vmem_limit_bytes=limit)


def gelu_pair(h):
    scale = math.sqrt(2.0 / math.pi)
    square = h * h
    t = jnp.tanh(scale * h * (1.0 + 0.044715 * square))
    half = 0.5 * (1.0 + t)
    slope = half + 0.5 * h * (1.0 - t * t) * scale * (1.0 + 3.0 * 0.044715 * square)
    return h * half, slope


def nesterov(weight, moment, average, grad, rate):
    moment_new = mu_rate * moment + grad
    weight_new = weight - rate * (grad + mu_rate * moment_new)
    average_new = avg_decay * average + (1.0 - avg_decay) * weight_new
    return (weight_new, moment_new, average_new)


class Ring:
    def __init__(self, n_data, n_model):
        self.count = n_data * n_model
        tall = n_model // 2
        self.stages = (
            (0, 1),
            tuple(x * n_model + y * 2 for x in range(2) for y in range(tall)),
            tuple(z * 2 * n_model for z in range(n_data // 2)),
        )

    def offset_of(self, place):
        total = 0
        rest = place
        for stage in reversed(self.stages):
            digit = rest & (len(stage) - 1)
            rest = rest >> bits_of(len(stage))
            for bit in range(bits_of(len(stage))):
                total = total + ((digit >> bit) & 1) * stage[1 << bit]
        return total

    def device_at(self, me, place):
        return me ^ self.offset_of(place)

    def place_bits(self):
        places = {self.offset_of(place): place for place in range(self.count)}
        return [places[1 << bit] for bit in range(bits_of(self.count))]

    def swap(self, value, distance):
        return lax.ppermute(value, both, [(i, i ^ distance) for i in range(self.count)])

    def swap_pieces(self, stage, pieces):
        return [pieces[0]] + [self.swap(p, d) for p, d in zip(pieces[1:], self.stages[stage][1:])]

    def spread(self, stage, value):
        return [value] + [self.swap(value, d) for d in self.stages[stage][1:]]


def place_in(bits, offset):
    total = 0
    for bit, value in enumerate(bits):
        total = total + ((offset >> bit) & 1) * value
    return total


def sum_kernel(parts_in, parts_out, dtype, *refs):
    ins, outs = refs[:parts_in], refs[len(refs) - parts_out :]
    for k, out in enumerate(outs):
        total = ins[0][k].astype(f32)
        for ref in ins[1:]:
            total = total + ref[k].astype(f32)
        out[...] = total.astype(dtype)


def sum_pieces(parts, count, dtype, steps, after=(), name="sum"):
    length = parts[0].shape[0] // count
    rest = parts[0].shape[1:]
    fold = rest[:-2]
    blocks = length
    for size in fold:
        blocks = blocks * size
    steps = min(steps, blocks)
    each = blocks // steps
    tile = rest[-2:]
    views = [v.reshape((count, blocks) + tile) for v in parts]
    outs = pl.pallas_call(
        functools.partial(sum_kernel, len(parts), count, dtype),
        grid=(steps,),
        out_shape=[jax.ShapeDtypeStruct((blocks,) + tile, dtype)] * count,
        in_specs=[pl.BlockSpec((count, each) + tile, lambda i: (0, i, 0, 0))] * len(parts)
        + [pl.BlockSpec(memory_space=pl.ANY)] * len(after),
        out_specs=[pl.BlockSpec((each,) + tile, lambda i: (i, 0, 0))] * count,
        compiler_params=params(),
        name=name,
    )(*views, *after)
    return [v.reshape((length,) + rest) for v in outs]


def join_kernel(count, *refs):
    out = refs[-1]
    at = 0
    for ref in refs[:count]:
        out[at : at + ref.shape[0]] = ref[...]
        at += ref.shape[0]


def join(parts, after=()):
    total = sum(v.shape[0] for v in parts)
    anywhere = pl.BlockSpec(memory_space=pl.ANY)
    return pl.pallas_call(
        functools.partial(join_kernel, len(parts)),
        out_shape=jax.ShapeDtypeStruct((total,) + parts[0].shape[1:], parts[0].dtype),
        in_specs=[vmem()] * len(parts) + [anywhere] * len(after),
        out_specs=vmem(),
        compiler_params=params(),
        name="join",
    )(*parts, *after)


def held_until(value, after):
    anywhere = pl.BlockSpec(memory_space=pl.ANY)
    return pl.pallas_call(
        lambda *refs: None,
        out_shape=jax.ShapeDtypeStruct(value.shape, value.dtype),
        in_specs=[anywhere] * (1 + len(after)),
        out_specs=anywhere,
        input_output_aliases={0: 0},
        name="hold",
    )(value, *after)


def bucket_kernel(pairs, cap_rows, starts, keys, out):
    owners = out.shape[0]
    lane = lax.broadcasted_iota(i32, (1, lanes), 1)
    body_rows = -(-(cap_rows + 1) // 8) * 8

    def one(o, carry):
        off = starts[o * pairs]
        row = lax.shift_right_logical(off, 7)
        shift = off & (lanes - 1)
        block = keys[pl.ds(row, body_rows), :]
        turned = pltpu.roll(block, (lanes - shift) & (lanes - 1), 1)
        merged = jnp.where(lane < lanes - shift, turned[:cap_rows], turned[1 : cap_rows + 1])
        out[o, 0:cap_rows, :] = merged
        head = jnp.zeros((1, lanes), i32)
        for p in range(pairs + 1):
            head = jnp.where(lane == p, starts[o * pairs + p] - off, head)
        out[o, cap_rows : cap_rows + 1, :] = head
        return carry

    lax.fori_loop(0, owners, one, 0)


def prep_kernel(row_bits, sample_bits, entries, rows_out, samples_out):
    e = entries[...]
    rows = e & ((1 << row_bits) - 1)
    lane = lax.broadcasted_iota(i32, e.shape, 1)
    place = lane & (window - 1)
    clash = jnp.zeros(e.shape, i32)
    for d in range(1, window):
        other = pltpu.roll(rows, lanes - d, 1)
        clash = jnp.where((other == rows) & (place < window - d), 1, clash)
    step = 1
    while step < group:
        clash = clash | pltpu.roll(clash, lanes - step, 1)
        step *= 2
    rows_out[...] = jnp.where((lane & (group - 1)) == 0, rows | (clash << flag_bit), rows)
    samples_out[...] = lax.shift_right_logical(e, row_bits) & ((1 << sample_bits) - 1)


def one_hot(samples_ref, row, base, low, high, per_device, width):
    count = width // lanes
    s = jnp.concatenate([samples_ref[pl.ds(row + c, 1), :] for c in range(count)], axis=1)
    k = lax.broadcasted_iota(i32, (1, width), 1) + base
    s = jnp.where((k >= low) & (k < high), s, -1).astype(f32).astype(bf16)
    place = lax.broadcasted_iota(i32, (per_device, width), 0).astype(f32).astype(bf16)
    return jnp.where(place == s, jnp.ones((), bf16), jnp.zeros((), bf16))


class Lists:
    def __init__(self, ring, me, rows, held, sems):
        self.ring, self.me, self.rows, self.held, self.sems = ring, me, rows, held, sems
        self.length = held.shape[0] // (2 * batch)
        self.batches = rows.shape[0] // self.length // batch

    def copies(self, n):
        slot = n & 1
        found = []
        for b in range(batch):
            sender = self.ring.device_at(self.me[0], n * batch + b)
            source = self.rows.at[pl.ds(pl.multiple_of(sender * self.length, 1024), self.length)]
            held = self.held.at[pl.ds(pl.multiple_of((slot * batch + b) * self.length, 1024), self.length)]
            found.append(pltpu.make_async_copy(source, held, self.sems.at[slot, b]))
        return found

    def start(self, n):
        for copy in self.copies(n):
            copy.start()

    def wait(self, n):
        for copy in self.copies(n):
            copy.wait()

    def run(self, step):
        self.start(0)

        def one(n, carry):
            @pl.when(n + 1 < self.batches)
            def _():
                self.start(n + 1)

            self.wait(n)
            step(n)
            return carry

        lax.fori_loop(0, self.batches, one, 0)

    def first(self, n, b, at):
        return ((n & 1) * batch + b) * self.length + at

    def entry(self, place):
        return self.held[place] & ((1 << flag_bit) - 1)

    def clash(self, place):
        return lax.shift_right_logical(self.held[place], flag_bit)


def gather_kernel(ring, first_pair, at, per_device, cap, me, bounds, rows, samples, table, *refs):
    keep, send, rows_f, stage, pooled, held, sems, out_sem = refs[-8:]
    step = pl.program_id(0)
    pair = first_pair + step
    rows_own = table.shape[2]
    width = min(256, cap)
    cap_rows = cap // lanes
    blocks = cap // width
    span = 256
    lane = lax.broadcasted_iota(i32, (span, lanes), 1)
    same = lax.broadcasted_iota(i32, (span, span), 0) == lax.broadcasted_iota(i32, (span, span), 1)
    unit = jnp.where(same, 1.0, 0.0).astype(bf16)

    def turn(c, carry):
        at = pl.multiple_of(c * span, span)
        t = table[0, :, pl.ds(at, span)].astype(bf16)
        t = lax.dot_general(unit, t, (((1,), (1,)), ((), ())), preferred_element_type=f32)
        rows_f[pl.ds(at, span), :] = jnp.where(lane < lanes // 2, t, 0.0)
        at_odd = pl.multiple_of(c * span + rows_own, span)
        rows_f[pl.ds(at_odd, span), :] = jnp.where(lane < lanes // 2, 0.0, t)
        return carry

    lax.fori_loop(0, rows_own // span, turn, 0, unroll=8)
    stage[...] = jnp.zeros(stage.shape, f32)
    lists = Lists(ring, me, rows, held, sems)

    def some(n):
        senders = [ring.device_at(me[0], n * batch + b) for b in range(batch)]
        lows = [bounds[s * 8 + pair] for s in senders]
        highs = [bounds[s * 8 + pair + 1] for s in senders]
        for b in range(batch):

            def fetch(i, c):
                at = pl.multiple_of(i * group, group)
                first = lists.first(n, b, at)
                for u in range(group):
                    r = held[first + u] if u else lists.entry(first)
                    stage[b, pl.ds(at + u, 1), :] = rows_f[pl.ds(r, 1), :]
                return c

            lax.fori_loop(lax.div(lows[b], group), lax.div(highs[b] + group - 1, group), fetch, 0)

        def term(b, i):
            block = jnp.minimum(i, blocks - 1)
            row = senders[b] * cap_rows + block * (width // lanes)
            hot = one_hot(samples, row, i * width, lows[b], highs[b], per_device, width)
            fetched = stage[b, pl.ds(pl.multiple_of(block * width, width), width), :].astype(bf16)
            return jnp.dot(hot, fetched, preferred_element_type=f32)

        shift = bits_of(width)
        begins = [lax.shift_right_logical(low, shift) for low in lows]
        def put(b, total):
            pooled[pl.ds(n * batch + b, 1)] = total.astype(bf16)[None]

        for b in range(batch):
            put(b, term(b, begins[b]) + term(b, begins[b] + 1))
        for b in range(batch):

            @pl.when(highs[b] > (begins[b] + 2) * width)
            def _():
                total = lax.fori_loop(
                    begins[b],
                    lax.shift_right_logical(highs[b] + width - 1, shift),
                    lambda i, t: t + term(b, i),
                    jnp.zeros((per_device, lanes), f32),
                )
                put(b, total)

    lists.run(some)
    half = keep.shape[0]
    copies = [
        pltpu.make_async_copy(pooled.at[pl.ds(i * half, half)], ref.at[:, at + step], out_sem.at[i])
        for i, ref in enumerate((keep, send))
    ]
    for copy in copies:
        copy.start()
    for copy in copies:
        copy.wait()


def scatter_kernel(
    ring, pair, rows_at, per_device, cap, me, bounds, rows, samples, own, other, w_in, m_in, a_in, *refs
):
    w_out, m_out, a_out, sums, stage, grads, w_buf, m_buf, a_buf, held, sems, grad_sem, in_sem, out_sem = refs[-14:]
    blocks_each = own.shape[0]
    arrivals = [
        pltpu.make_async_copy(ref.at[:, pl.ds(rows_at, per_device)], grads.at[pl.ds(i * blocks_each, blocks_each)], grad_sem.at[i])
        for i, ref in enumerate((own, other))
    ]
    for arrival in arrivals:
        arrival.start()
    rows_own = w_in.shape[2]
    width = min(256, cap)
    cap_rows = cap // lanes
    blocks = cap // width
    sources = (w_in, m_in, a_in)
    targets = (w_out, m_out, a_out)
    buffers = (w_buf, m_buf, a_buf)
    sums[...] = jnp.zeros(sums.shape, f32)
    lists = Lists(ring, me, rows, held, sems)
    for arrival in arrivals:
        arrival.wait()
    for i in range(3):
        pltpu.make_async_copy(sources[i].at[pair], buffers[i], in_sem.at[i]).start()

    def some(n):
        senders = [ring.device_at(me[0], n * batch + b) for b in range(batch)]
        lows = [bounds[s * 8 + pair] for s in senders]
        highs = [bounds[s * 8 + pair + 1] for s in senders]

        def spread(b, i):
            block = jnp.minimum(i, blocks - 1)
            row = senders[b] * cap_rows + block * (width // lanes)
            hot = one_hot(samples, row, block * width, lows[b], highs[b], per_device, width)
            mine = grads[n * batch + b]
            stage[b, pl.ds(pl.multiple_of(block * width, width), width), :] = lax.dot_general(
                hot, mine, (((0,), (0,)), ((), ())), preferred_element_type=f32
            )

        shift = bits_of(width)
        begins = [lax.shift_right_logical(low, shift) for low in lows]
        for b in range(batch):
            spread(b, begins[b])
            spread(b, begins[b] + 1)
        for b in range(batch):

            @pl.when(highs[b] > (begins[b] + 2) * width)
            def _():
                def more(i, c):
                    spread(b, i)
                    return c

                lax.fori_loop(begins[b] + 2, lax.shift_right_logical(highs[b] + width - 1, shift), more, 0)

        for b in range(batch):

            def add(i, c):
                at = pl.multiple_of(i * group, group)
                first = lists.first(n, b, at)

                def apart():
                    for start in range(0, group, window):
                        places = [held[first + u] if u else lists.entry(first) for u in range(start, start + window)]
                        olds = [sums[pl.ds(r, 1), :] for r in places]
                        news = [stage[b, pl.ds(at + start + u, 1), :] for u in range(window)]
                        for r, old, new in zip(places, olds, news):
                            sums[pl.ds(r, 1), :] = old + new

                def in_turn():
                    def single(u, inner):
                        r = lists.entry(first + u)
                        sums[pl.ds(r, 1), :] = sums[pl.ds(r, 1), :] + stage[b, pl.ds(at + u, 1), :]
                        return inner

                    lax.fori_loop(0, group, single, 0)

                lax.cond(lists.clash(first) == 0, apart, in_turn)
                return c

            lax.fori_loop(lax.div(lows[b], group), lax.div(highs[b] + group - 1, group), add, 0)

    lists.run(some)
    for i in range(3):
        pltpu.make_async_copy(sources[i].at[pair], buffers[i], in_sem.at[i]).wait()
    chunks = out_sem.shape[0] // 3
    chunk = rows_own // chunks
    span = min(256, chunk)
    lane = lax.broadcasted_iota(i32, (span, lanes), 1)

    def copies(n):
        part = pl.ds(n * chunk, chunk)
        return [
            pltpu.make_async_copy(buffers[i].at[:, part], targets[i].at[pair, :, part], out_sem.at[n * 3 + i])
            for i in range(3)
        ]

    for n in range(chunks):

        def update(c, carry):
            at = pl.multiple_of(n * chunk + c * span, span)
            even = sums[pl.ds(at, span), :]
            odd = sums[pl.ds(pl.multiple_of(at + rows_own, span), span), :]
            grad = jnp.where(lane < lanes // 2, even, odd).T
            part = (slice(None), pl.ds(at, span))
            new = nesterov(w_buf[part], m_buf[part], a_buf[part], grad, rates[0])
            w_buf[part] = new[0]
            m_buf[part] = new[1]
            a_buf[part] = new[2]
            return carry

        lax.fori_loop(0, chunk // span, update, 0)
        for copy in copies(n):
            copy.start()
    for n in range(chunks):
        for copy in copies(n):
            copy.wait()


rows_first = (((0,), (0,)), ((), ()))
last_last = (((1,), (1,)), ((), ()))


def experts_forward(x_ref, weight_ref, y_ref, act_ref, slope_ref):
    x = x_ref[...]
    total = None
    for m in range(weight_ref.shape[1]):
        w_in, w_out = (weight_ref[:, m, i, 0].reshape(-1, weight_ref.shape[-1]) for i in range(2))
        act, slope = gelu_pair(jnp.dot(x, w_in, preferred_element_type=f32))
        act = act.astype(bf16)
        act_ref[0, m] = act
        slope_ref[0, m] = slope.astype(bf16)
        term = lax.dot_general(act, w_out, last_last, preferred_element_type=f32)
        total = term if total is None else total + term
    y_ref[0] = total


def experts_back_rows(pairs, d_ref, weight_ref, slope_ref, dxg_ref, inv_ref, d_hidden_ref, *refs):
    grads, dx = refs[:pairs], refs[pairs]
    d_out = d_ref[0]
    total = None
    for m in range(weight_ref.shape[1]):
        w_in, w_out = (weight_ref[:, m, i, 0].reshape(-1, weight_ref.shape[-1]) for i in range(2))
        d_act = jnp.dot(d_out, w_out, preferred_element_type=f32)
        d_hidden = (d_act * slope_ref[0, m].astype(f32)).astype(bf16)
        d_hidden_ref[0, m] = d_hidden
        term = lax.dot_general(d_hidden, w_in, last_last, preferred_element_type=f32)
        total = term if total is None else total + term

    @pl.when(pl.program_id(0) == 0)
    def _():
        dx[...] = dxg_ref[...] + total

    @pl.when(pl.program_id(0) != 0)
    def _():
        dx[...] += total

    @pl.when(pl.program_id(0) == pl.num_programs(0) - 1)
    def _():
        for p in range(pairs):
            part = (slice(None), slice(p * lanes, (p + 1) * lanes))
            grads[p][...] = (dx[part] * inv_ref[part]).astype(bf16)


def experts_back_weights(n_model, lhs_ref, rows_ref, *refs):
    dw_ref = refs[-1]
    devices, _, f_own, _ = dw_ref.shape
    lhs = lhs_ref[0]
    for m in range(n_model):
        out = jnp.dot(lhs, rows_ref[0, m], preferred_element_type=f32).astype(bf16)
        for d in range(devices // n_model):
            dw_ref[d * n_model + m, 0] = out[d * f_own : (d + 1) * f_own]


def experts_back_placed(bits, n_model, me, lhs_ref, rows_ref, *refs):
    keep, send = refs[-2:]
    half, _, f_own, h_own = keep.shape
    model = me[0] & (n_model - 1)
    data = me[0] ^ model
    bits = [0] + bits[1:]
    lhs = lhs_ref[0]
    for beside in range(n_model):
        out = jnp.dot(lhs, rows_ref[0, pl.ds(model ^ beside, 1)][0], preferred_element_type=f32).astype(bf16)
        to = send if beside & 1 else keep
        for d in range(2 * half // n_model):
            place = place_in(bits, (data ^ (d * n_model)) | (beside & (n_model - 2)))
            to[pl.ds(place, 1), 0] = out[d * f_own : (d + 1) * f_own][None]


def head_kernel(
    sample_total, x_ref, y_ref, gate_ref, tower_ref, v_ref, label_ref,
    d_expert_ref, d_expert_t_ref, dxg_ref, d_tower_ref, d_gate_ref, small_ref, probs, mixed, d_mixed, d_gate, inner,
):
    experts, rows, features = y_ref.shape
    tasks = tower_ref.shape[0]
    x = x_ref[...]
    gate = gate_ref[...]
    logits = jnp.dot(x, gate, preferred_element_type=f32)
    task_of = lax.shift_right_logical(lax.broadcasted_iota(i32, (1, lanes), 1), bits_of(experts))

    def by_task(fold, value, fill):
        total = jnp.zeros(value.shape, f32)
        for k in range(tasks):
            found = fold(jnp.where(task_of == k, value, fill), axis=1, keepdims=True)
            total = jnp.where(task_of == k, found, total)
        return total

    used = task_of < tasks
    raised = jnp.where(used, jnp.exp(logits - by_task(jnp.max, logits, -jnp.inf)), 0.0)
    probs[...] = raised / jnp.where(used, by_task(jnp.sum, raised, 0.0), 1.0)
    span = 16
    parts = 2
    wide = features // parts

    def mix(r, carry):
        part = pl.ds(pl.multiple_of(r * span, span), span)
        p = probs[part, :]
        for h in range(parts):
            across = slice(h * wide, (h + 1) * wide)
            totals = [None] * tasks
            for e in range(experts):
                y = y_ref[e, part, across]
                for k in range(tasks):
                    c = k * experts + e
                    more = p[:, c : c + 1] * y
                    totals[k] = more if e == 0 else totals[k] + more
            for k in range(tasks):
                mixed[k, part, across] = totals[k].astype(bf16)
        return carry

    lax.fori_loop(0, rows // span, mix, 0)
    loss = jnp.zeros((1, 1), f32)
    vectors = []
    for k in range(tasks):
        tower = tower_ref[k]
        act, slope = gelu_pair(jnp.dot(mixed[k], tower, preferred_element_type=f32))
        v = v_ref[k : k + 1, :]
        logit = jnp.sum(act * v, axis=1, keepdims=True)
        label = label_ref[:, k : k + 1]
        weighting = task_weights[k] * label_ref[:, tasks + k : tasks + k + 1]
        small_exp = jnp.exp(-jnp.abs(logit))
        softplus = jnp.maximum(logit, 0.0) + jnp.log1p(small_exp)
        loss = loss + jnp.sum(weighting * (softplus - label * logit), axis=0, keepdims=True)
        sigmoid = jnp.where(logit >= 0.0, 1.0, small_exp) / (1.0 + small_exp)
        d_logit = weighting * (sigmoid - label) / sample_total
        vectors.append(jnp.sum(d_logit * act, axis=0, keepdims=True))
        d_pre = (d_logit * v * slope).astype(bf16)
        d_mixed[k] = lax.dot_general(d_pre, tower, last_last, preferred_element_type=f32)
        d_tower_ref[k] = lax.dot_general(mixed[k], d_pre, rows_first, preferred_element_type=f32).astype(bf16)
    lane = lax.broadcasted_iota(i32, (span, lanes), 1)
    ones = jnp.ones((lanes, lanes), bf16)

    def back(r, carry):
        part = pl.ds(pl.multiple_of(r * span, span), span)
        p = probs[part, :]
        for e in range(experts):
            y = y_ref[e, part, :]
            total = None
            for k in range(tasks):
                c = k * experts + e
                d = d_mixed[k, part, :]
                product = d * y
                narrow = product[:, :lanes]
                for t in range(1, features // lanes):
                    narrow = narrow + product[:, t * lanes : (t + 1) * lanes]
                coarse = narrow.astype(bf16)
                inner[0, c * span : (c + 1) * span, :] = coarse
                inner[1, c * span : (c + 1) * span, :] = (narrow - coarse.astype(f32)).astype(bf16)
                more = p[:, c : c + 1] * d
                total = more if k == 0 else total + more
            d_expert_ref[e, part, :] = total.astype(bf16)
        row_sums = jnp.dot(inner[0], ones, preferred_element_type=f32)
        row_sums = row_sums + jnp.dot(inner[1], ones, preferred_element_type=f32)
        d_probs = jnp.zeros((span, lanes), f32)
        for c in range(tasks * experts):
            d_probs = jnp.where(lane == c, row_sums[c * span : (c + 1) * span], d_probs)
        d_gate[part, :] = (p * (d_probs - by_task(jnp.sum, p * d_probs, 0.0))).astype(bf16)
        return carry

    lax.fori_loop(0, rows // span, back, 0)
    for e in range(experts):
        d_expert_t_ref[e] = d_expert_ref[e].T
    dxg_ref[...] = lax.dot_general(d_gate[...], gate, last_last, preferred_element_type=f32)
    d_gate_ref[...] = lax.dot_general(x, d_gate[...], rows_first, preferred_element_type=f32).astype(bf16)
    line = lax.broadcasted_iota(i32, (8, lanes), 0)
    tile = jnp.where(line == tasks, loss, 0.0)
    for k in range(tasks):
        tile = jnp.where(line == k, vectors[k], tile)
    pieces = []
    for _ in range(4):
        piece = tile.astype(bf16)
        pieces.append(piece)
        tile = tile - piece.astype(f32)
    small_ref[...] = jnp.concatenate(pieces, axis=0)


def smem():
    return pl.BlockSpec(memory_space=pltpu.SMEM)


def vmem():
    return pl.BlockSpec(memory_space=pltpu.VMEM)


def body(
    row_ids, bag_counts, labels, label_mask, tables, table_mom, table_avg, w_in, w_in_mom, w_in_avg,
    w_out, w_out_mom, w_out_avg, gate_w, gate_mom, gate_avg, tower_w, tower_w_mom, tower_w_avg,
    tower_v, tower_v_mom, tower_v_avg,
):
    n_model = lax.axis_size("mp")
    n_data = lax.axis_size("dp")
    devices = n_data * n_model
    ring = Ring(n_data, n_model)
    mp_rank = lax.axis_index("mp")
    me = (lax.axis_index("dp") * n_model + mp_rank).astype(i32).reshape(1)
    per_group, table_count, bag_size = row_ids.shape
    per_device = per_group // n_model
    rows_own = tables.shape[1]
    emb_width = tables.shape[2]
    features = table_count * emb_width
    pairs = features // lanes
    sample_total = float(per_group * n_data)
    slot_total = per_device * table_count * bag_size
    cap = 2 * slot_total // devices
    cap_rows = cap // lanes

    w_out_t, w_out_mom_t, w_out_avg_t = (v.transpose(0, 2, 1) for v in (w_out, w_out_mom, w_out_avg))
    experts, f_own, h_own = w_in.shape
    weights = jnp.stack([w_in, w_out_t]).astype(bf16)
    weights = lax.all_gather(weights, both, axis=0).reshape(n_data, n_model, 2, experts, f_own, h_own)

    row_bits = bits_of(rows_own) + 1
    sample_bits = bits_of(per_device)
    start = mp_rank * per_device
    ids = lax.dynamic_slice_in_dim(row_ids.transpose(1, 2, 0), start, per_device, 2)
    counts = lax.dynamic_slice_in_dim(bag_counts.T, start, per_device, 1)
    live = lax.broadcasted_iota(i32, ids.shape, 1) < counts[:, None, :]
    table_of = lax.broadcasted_iota(i32, ids.shape, 0)
    bucket = lax.shift_right_logical(ids, row_bits - 1) * pairs + lax.shift_right_logical(table_of, 1)
    key = (bucket << sample_bits) | lax.broadcasted_iota(i32, ids.shape, 2)
    key = (((key << 1) | (table_of & 1)) << (row_bits - 1)) | (ids & (rows_own - 1))
    key = jnp.where(live, key, 1 << 30).reshape(-1)
    ordered = lax.sort(key)
    bucket_sorted = lax.shift_right_logical(ordered, row_bits + sample_bits)
    starts = jnp.sum(
        (bucket_sorted[None, :] < jnp.arange(devices * pairs + 1, dtype=i32)[:, None]).astype(i32), axis=1
    )
    padded = jnp.concatenate([ordered.reshape(-1, lanes), jnp.zeros((cap_rows + 8, lanes), i32)], axis=0)
    out_rows = -(-(cap_rows + 1) // 8) * 8
    outgoing = pl.pallas_call(
        functools.partial(bucket_kernel, pairs, cap_rows),
        out_shape=jax.ShapeDtypeStruct((devices, out_rows, lanes), i32),
        in_specs=[smem(), vmem()],
        out_specs=vmem(),
        name="bucket",
    )(starts, padded)
    received = lax.all_to_all(outgoing, both, split_axis=0, concat_axis=0, tiled=True)
    bounds = received[:, cap_rows, :8].reshape(-1)
    entries = received[:, :cap_rows].reshape(devices * cap_rows, lanes)
    entry_shape = jax.ShapeDtypeStruct(entries.shape, i32)
    rows, samples = pl.pallas_call(
        functools.partial(prep_kernel, row_bits, sample_bits),
        out_shape=(entry_shape, entry_shape),
        in_specs=[vmem()],
        out_specs=(vmem(), vmem()),
        name="prep",
    )(entries)
    length = max(cap, 1024)
    rows = jnp.pad(rows.reshape(devices, cap), ((0, 0), (0, length - cap))).reshape(-1)
    hbm = pl.BlockSpec(memory_space=pl.ANY)
    list_scratch = [pltpu.SMEM((2 * batch * length,), i32), pltpu.SemaphoreType.DMA((2, batch))]

    paired = tuple(
        v.transpose(0, 2, 1).reshape(pairs, lanes, rows_own) for v in (tables, table_mom, table_avg)
    )
    half = devices // 2
    half_shape = jax.ShapeDtypeStruct((half, per_device, lanes), bf16)

    def gather(first_pair, count, at, total, olds, after):
        out_shape = jax.ShapeDtypeStruct((half, total, per_device, lanes), bf16)
        return pl.pallas_call(
            functools.partial(gather_kernel, ring, first_pair, at, per_device, cap),
            grid=(count,),
            out_shape=(out_shape, out_shape),
            in_specs=[
                smem(), smem(), hbm, vmem(),
                pl.BlockSpec((1, lanes, rows_own), lambda i: (first_pair + i, 0, 0)),
            ] + [hbm] * (len(olds) + len(after)),
            out_specs=(hbm, hbm),
            scratch_shapes=[
                pltpu.VMEM((2 * rows_own, lanes), f32),
                pltpu.VMEM((batch, cap, lanes), f32),
                pltpu.VMEM((devices, per_device, lanes), bf16),
            ] + list_scratch + [pltpu.SemaphoreType.DMA((2,))],
            input_output_aliases={5: 0, 6: 1} if olds else {},
            compiler_params=params(),
            cost_estimate=cost(16 * count),
            name="gather",
        )(me, bounds, rows, samples, paired[0], *olds, *after)

    plane, line = len(ring.stages[1]), len(ring.stages[2])
    each = half // plane

    def core_sums(keep, send, steps, after=(), name="sum_core"):
        return sum_pieces([keep, ring.swap(send, 1)], plane, bf16, steps, after, name)

    def plane_sums(pieces, steps, after=(), name="sum_plane"):
        return sum_pieces(ring.swap_pieces(1, pieces), line, bf16, steps, after, name)

    def line_sum(pieces):
        total = None
        for piece in ring.swap_pieces(2, pieces):
            total = piece.astype(f32) if total is None else total + piece.astype(f32)
        return total

    early = pairs // 2
    rest = pairs - early
    cored_early = core_sums(*gather(0, early, 0, early, (), ()), 2)
    late = gather(early, rest - 1, 0, rest, (), ())
    late = gather(pairs - 1, 1, rest - 1, rest, late, (cored_early[0],))
    planed_early = plane_sums(cored_early, 1)
    cored_late = core_sums(late[0], held_until(late[1], (planed_early[0],)), 2)
    planed_late = plane_sums(cored_late, 1)
    pooled = jnp.concatenate([line_sum(planed_early)[0], line_sum(planed_late)[0]], axis=0)
    inverse = jnp.repeat(1.0 / counts.T.astype(f32), emb_width, axis=1)
    x = (pooled.transpose(1, 0, 2).reshape(per_device, features) * inverse).astype(bf16)

    hidden_shape = jax.ShapeDtypeStruct((experts, n_model, per_device, h_own), bf16)
    weight_spec = pl.BlockSpec((n_data, n_model, 2, 1, f_own, h_own), lambda e: (0, 0, 0, e, 0, 0))
    hidden_spec = pl.BlockSpec((1, n_model, per_device, h_own), lambda e: (e, 0, 0, 0))
    expert_spec = pl.BlockSpec((1, per_device, features), lambda e: (e, 0, 0))
    whole_spec = pl.BlockSpec((per_device, features), lambda e: (0, 0))
    y, act, slope = pl.pallas_call(
        experts_forward,
        grid=(experts,),
        out_shape=(jax.ShapeDtypeStruct((experts, per_device, features), f32), hidden_shape, hidden_shape),
        in_specs=[whole_spec, weight_spec],
        out_specs=(expert_spec, hidden_spec, hidden_spec),
        compiler_params=params(),
        cost_estimate=cost(16),
        name="experts_forward",
    )(x, weights)
    tasks, _, tower_width = tower_w.shape
    spare = lanes - tasks * experts
    gate_low = jnp.pad(gate_w.transpose(1, 0, 2).reshape(features, tasks * experts), ((0, 0), (0, spare))).astype(bf16)
    label_rows = lax.dynamic_slice_in_dim(labels, start, per_device, 0)
    mask_rows = lax.dynamic_slice_in_dim(label_mask, start, per_device, 0)
    marks = jnp.concatenate([label_rows, mask_rows], axis=1).astype(f32)
    d_expert, d_expert_t, d_x_gate, d_tower_part, d_gate_part, tiny = pl.pallas_call(
        functools.partial(head_kernel, sample_total),
        out_shape=(
            jax.ShapeDtypeStruct((experts, per_device, features), bf16),
            jax.ShapeDtypeStruct((experts, features, per_device), bf16),
            jax.ShapeDtypeStruct((per_device, features), f32),
            jax.ShapeDtypeStruct(tower_w.shape, bf16),
            jax.ShapeDtypeStruct((features, lanes), bf16),
            jax.ShapeDtypeStruct((32, lanes), bf16),
        ),
        in_specs=[vmem()] * 6,
        out_specs=(vmem(),) * 6,
        scratch_shapes=[
            pltpu.VMEM((per_device, lanes), f32),
            pltpu.VMEM((tasks, per_device, features), bf16),
            pltpu.VMEM((tasks, per_device, features), f32),
            pltpu.VMEM((per_device, lanes), bf16),
            pltpu.VMEM((2, 16 * tasks * experts, lanes), bf16),
        ],
        compiler_params=params(),
        cost_estimate=cost(12),
        name="towers",
    )(x, y, gate_low, tower_w.astype(bf16), tower_v, marks)
    grads_shape = jax.ShapeDtypeStruct((per_device, lanes), bf16)
    d_hidden, *grads = pl.pallas_call(
        functools.partial(experts_back_rows, pairs),
        grid=(experts,),
        out_shape=(hidden_shape,) + (grads_shape,) * pairs,
        in_specs=[expert_spec, weight_spec, hidden_spec, whole_spec, whole_spec],
        out_specs=(hidden_spec,) + (pl.BlockSpec((per_device, lanes), lambda e: (0, 0)),) * pairs,
        scratch_shapes=[pltpu.VMEM((per_device, features), f32)],
        compiler_params=params(),
        cost_estimate=cost(14),
        name="experts_back_rows",
    )(d_expert, weights, slope, d_x_gate, inverse)
    grads = jnp.concatenate([grads[0], tiny] + grads[1:], axis=0)[None]

    lhs_spec = [
        pl.BlockSpec((1, features, per_device), lambda e, single=single: (0 if single else e, 0, 0))
        for single in (False, True)
    ]
    rows_spec = pl.BlockSpec((1, n_model, per_device, h_own), lambda e: (e, 0, 0, 0))
    half_weights = jax.ShapeDtypeStruct((half, experts, f_own, h_own), bf16)
    half_spec = pl.BlockSpec((half, 1, f_own, h_own), lambda e: (0, e, 0, 0))

    paired_shape = jax.ShapeDtypeStruct(paired[0].shape, f32)
    chunks = 4

    def scatter(pair, at, own, other, olds, after):
        in_specs = [smem(), smem(), hbm, vmem()] + [hbm] * (5 + len(olds) + len(after))
        return pl.pallas_call(
            functools.partial(scatter_kernel, ring, pair, at, per_device, cap),
            out_shape=(paired_shape,) * 3,
            in_specs=in_specs,
            out_specs=(hbm, hbm, hbm),
            scratch_shapes=[
                pltpu.VMEM((2 * rows_own, lanes), f32),
                pltpu.VMEM((batch, cap, lanes), f32),
                pltpu.VMEM((devices, per_device, lanes), bf16),
                pltpu.VMEM((lanes, rows_own), f32),
                pltpu.VMEM((lanes, rows_own), f32),
                pltpu.VMEM((lanes, rows_own), f32),
                *list_scratch,
                pltpu.SemaphoreType.DMA((2,)),
                pltpu.SemaphoreType.DMA((3,)),
                pltpu.SemaphoreType.DMA((3 * chunks,)),
            ],
            input_output_aliases={9: 0, 10: 1, 11: 2} if olds else {},
            compiler_params=params(),
            cost_estimate=cost(26),
            name="scatter",
        )(me, bounds, rows, samples, own, other, *paired, *olds, *after)

    small_rows = tasks * features + features
    small = jnp.concatenate([d_tower_part.reshape(-1, lanes), d_gate_part], axis=0).reshape(2, 1, small_rows // 2, lanes)
    side = me[0] & 1
    give = lax.dynamic_index_in_dim(small, 1 - side, 0, keepdims=False)
    take = lax.dynamic_index_in_dim(small, side, 0, keepdims=False)
    dw_out = pl.pallas_call(
        functools.partial(experts_back_weights, n_model),
        grid=(experts,),
        out_shape=jax.ShapeDtypeStruct((devices, experts, f_own, h_own), bf16),
        in_specs=[lhs_spec[0], rows_spec],
        out_specs=pl.BlockSpec((devices, 1, f_own, h_own), lambda e: (0, e, 0, 0)),
        compiler_params=params(),
        cost_estimate=cost(9),
        name="experts_back_out",
    )(d_expert_t, act)
    lined = join(ring.spread(2, grads), (dw_out,))
    small = sum_pieces([take, ring.swap(give, 1)], 1, bf16, 1, (dw_out,), "sum_small")[0]
    d_w_out = lax.psum_scatter(dw_out, both, scatter_dimension=0, tiled=True)[0].astype(f32)
    keep, send = pl.pallas_call(
        functools.partial(experts_back_placed, ring.place_bits(), n_model),
        grid=(experts,),
        out_shape=(half_weights, half_weights),
        in_specs=[smem(), lhs_spec[1], rows_spec, hbm, hbm],
        out_specs=(half_spec, half_spec),
        compiler_params=params(),
        cost_estimate=cost(9),
        name="experts_back_in",
    )(me, x.T[None], d_hidden, lined, small)
    with_tiny = per_device + tiny.shape[0]
    edges = (0, with_tiny, lined.shape[1])
    spread = [ring.spread(1, lined[:, low:high]) for low, high in zip(edges, edges[1:])]
    far = [1 << bit for bit in range(3, bits_of(devices))] + [2, 4]

    def add_small(small, after, count=1):
        for distance in far[:count]:
            small = sum_pieces([small, ring.swap(small, distance)], 1, bf16, 1, after, "sum_small")[0]
        del far[:count]
        return small

    small = add_small(small, (keep,))
    own = join(spread[0], (small,))
    other = ring.swap(own, 1)
    send = held_until(send, (own,))
    sent = ring.swap(send, 1)
    tiny_sum = jnp.sum(jnp.concatenate([own[:, per_device:], other[:, per_device:]]).astype(f32), axis=0)
    table_outs = scatter(0, 0, own, other, (), ())
    small = add_small(small, (table_outs[0],))
    own = join(spread[1], (small,))
    other = ring.swap(own, 1)
    cored = sum_pieces([keep, sent], plane, bf16, 8, (own,), "sum_core_w")
    for pair in range(1, pairs):
        if pair == pairs - 1:
            planed = plane_sums(cored, 4, (table_outs[0],), "sum_plane_w")
            small = add_small(small, (planed[0],), len(far))
            after = (small,)
        elif pair == 1:
            after = (cored[0],)
        else:
            small = add_small(small, (table_outs[0],))
            after = (small,)
        table_outs = scatter(pair, (pair - 1) * per_device, own, other, table_outs, after)
    take = small
    got = ring.swap(take, 1)
    small = jnp.concatenate([jnp.where(side == 0, take, got), jnp.where(side == 0, got, take)]).astype(f32)
    small = small.reshape(small_rows, lanes)
    d_tower_w = small[: tasks * features].reshape(tower_w.shape)
    d_gate_w = small[tasks * features :, : tasks * experts]
    d_gate_w = d_gate_w.reshape(features, tasks, experts).transpose(1, 0, 2)
    d_w_in = line_sum(planed)[0]
    tiny_sum = jnp.sum(tiny_sum.reshape(4, 8, lanes), axis=0)
    d_tower_v, loss_sum = tiny_sum[:tasks], tiny_sum[tasks, 0]
    table_new = tuple(v.reshape(table_count, emb_width, rows_own).transpose(0, 2, 1) for v in table_outs)
    w_in_new = nesterov(w_in, w_in_mom, w_in_avg, d_w_in, rates[1])
    w_out_new = nesterov(w_out_t, w_out_mom_t, w_out_avg_t, d_w_out, rates[2])
    w_out_new = tuple(v.transpose(0, 2, 1) for v in w_out_new)
    gate_new = nesterov(gate_w, gate_mom, gate_avg, d_gate_w, rates[3])
    tower_new = nesterov(tower_w, tower_w_mom, tower_w_avg, d_tower_w, rates[4])
    vector_new = nesterov(tower_v, tower_v_mom, tower_v_avg, d_tower_v, rates[5])
    return (loss_sum,) + table_new + w_in_new + w_out_new + gate_new + tower_new + vector_new


def solution(mesh):
    group_spec = P("dp", None)
    table_spec = P(None, both, None)
    placed = (
        (P("dp", None, None), group_spec, group_spec, group_spec)
        + (table_spec,) * 3
        + (P(None, "dp", "mp"),) * 3
        + (P(None, "mp", "dp"),) * 3
        + (P(),) * 9
    )
    return jax.shard_map(
        body,
        mesh=mesh,
        in_specs=placed,
        out_specs=(P(),)
        + (table_spec,) * 3
        + (P(None, "dp", "mp"),) * 3
        + (P(None, "mp", "dp"),) * 3
        + (P(),) * 9,
        check_vma=False,
    )
```

```python
import functools
import math

import jax
import jax.numpy as jnp
from jax import lax
from jax.experimental import pallas as pl
from jax.experimental.pallas import tpu as pltpu
from jax.sharding import PartitionSpec as P

mu_rate = 0.5
avg_decay = 0.5
task_weights = (1.0, 0.6, 0.8, 0.4, 1.2)
rates = (5000000.0, 12000.0, 3500.0, 1000.0, 370.0, 200.0)
both = ("dp", "mp")
lanes = 128
group = 64
window = 8
batch = 4
flag_bit = 20
f32, bf16, i32 = jnp.float32, jnp.bfloat16, jnp.int32
vmem_limit = 58 * 2**20


def bits_of(size):
    return int(size).bit_length() - 1


def cost(microseconds):
    return pl.CostEstimate(flops=int(microseconds * 1.1e9), bytes_accessed=int(microseconds * 3.0e6), transcendentals=0)


def params(limit=vmem_limit):
    return pltpu.CompilerParams(vmem_limit_bytes=limit)


def gelu_pair(h):
    scale = math.sqrt(2.0 / math.pi)
    square = h * h
    t = jnp.tanh(scale * h * (1.0 + 0.044715 * square))
    half = 0.5 * (1.0 + t)
    slope = half + 0.5 * h * (1.0 - t * t) * scale * (1.0 + 3.0 * 0.044715 * square)
    return h * half, slope


def nesterov(weight, moment, average, grad, rate):
    moment_new = mu_rate * moment + grad
    weight_new = weight - rate * (grad + mu_rate * moment_new)
    average_new = avg_decay * average + (1.0 - avg_decay) * weight_new
    return (weight_new, moment_new, average_new)


class Ring:
    def __init__(self, n_data, n_model):
        self.count = n_data * n_model
        tall = n_model // 2
        self.stages = (
            (0, 1),
            tuple(x * n_model + y * 2 for x in range(2) for y in range(tall)),
            tuple(z * 2 * n_model for z in range(n_data // 2)),
        )

    def offset_of(self, place):
        total = 0
        rest = place
        for stage in reversed(self.stages):
            digit = rest & (len(stage) - 1)
            rest = rest >> bits_of(len(stage))
            for bit in range(bits_of(len(stage))):
                total = total + ((digit >> bit) & 1) * stage[1 << bit]
        return total

    def device_at(self, me, place):
        return me ^ self.offset_of(place)

    def place_bits(self):
        places = {self.offset_of(place): place for place in range(self.count)}
        return [places[1 << bit] for bit in range(bits_of(self.count))]

    def swap(self, value, distance):
        return lax.ppermute(value, both, [(i, i ^ distance) for i in range(self.count)])

    def swap_pieces(self, stage, pieces):
        return [pieces[0]] + [self.swap(p, d) for p, d in zip(pieces[1:], self.stages[stage][1:])]

    def spread(self, stage, value):
        return [value] + [self.swap(value, d) for d in self.stages[stage][1:]]


def place_in(bits, offset):
    total = 0
    for bit, value in enumerate(bits):
        total = total + ((offset >> bit) & 1) * value
    return total


def sum_kernel(parts_in, parts_out, dtype, *refs):
    ins, outs = refs[:parts_in], refs[len(refs) - parts_out :]
    for k, out in enumerate(outs):
        total = ins[0][k].astype(f32)
        for ref in ins[1:]:
            total = total + ref[k].astype(f32)
        out[...] = total.astype(dtype)


def sum_pieces(parts, count, dtype, steps, after=(), name="sum"):
    length = parts[0].shape[0] // count
    rest = parts[0].shape[1:]
    fold = rest[:-2]
    blocks = length
    for size in fold:
        blocks = blocks * size
    steps = min(steps, blocks)
    each = blocks // steps
    tile = rest[-2:]
    views = [v.reshape((count, blocks) + tile) for v in parts]
    outs = pl.pallas_call(
        functools.partial(sum_kernel, len(parts), count, dtype),
        grid=(steps,),
        out_shape=[jax.ShapeDtypeStruct((blocks,) + tile, dtype)] * count,
        in_specs=[pl.BlockSpec((count, each) + tile, lambda i: (0, i, 0, 0))] * len(parts)
        + [pl.BlockSpec(memory_space=pl.ANY)] * len(after),
        out_specs=[pl.BlockSpec((each,) + tile, lambda i: (i, 0, 0))] * count,
        compiler_params=params(),
        name=name,
    )(*views, *after)
    return [v.reshape((length,) + rest) for v in outs]


def join_kernel(count, *refs):
    out = refs[-1]
    at = 0
    for ref in refs[:count]:
        out[at : at + ref.shape[0]] = ref[...]
        at += ref.shape[0]


def join(parts, after=()):
    total = sum(v.shape[0] for v in parts)
    anywhere = pl.BlockSpec(memory_space=pl.ANY)
    return pl.pallas_call(
        functools.partial(join_kernel, len(parts)),
        out_shape=jax.ShapeDtypeStruct((total,) + parts[0].shape[1:], parts[0].dtype),
        in_specs=[vmem()] * len(parts) + [anywhere] * len(after),
        out_specs=vmem(),
        compiler_params=params(),
        name="join",
    )(*parts, *after)


def held_until(value, after):
    anywhere = pl.BlockSpec(memory_space=pl.ANY)
    return pl.pallas_call(
        lambda *refs: None,
        out_shape=jax.ShapeDtypeStruct(value.shape, value.dtype),
        in_specs=[anywhere] * (1 + len(after)),
        out_specs=anywhere,
        input_output_aliases={0: 0},
        name="hold",
    )(value, *after)


def bucket_kernel(pairs, cap_rows, starts, keys, out):
    owners = out.shape[0]
    lane = lax.broadcasted_iota(i32, (1, lanes), 1)
    body_rows = -(-(cap_rows + 1) // 8) * 8

    def one(o, carry):
        off = starts[o * pairs]
        row = lax.shift_right_logical(off, 7)
        shift = off & (lanes - 1)
        block = keys[pl.ds(row, body_rows), :]
        turned = pltpu.roll(block, (lanes - shift) & (lanes - 1), 1)
        merged = jnp.where(lane < lanes - shift, turned[:cap_rows], turned[1 : cap_rows + 1])
        out[o, 0:cap_rows, :] = merged
        head = jnp.zeros((1, lanes), i32)
        for p in range(pairs + 1):
            head = jnp.where(lane == p, starts[o * pairs + p] - off, head)
        out[o, cap_rows : cap_rows + 1, :] = head
        return carry

    lax.fori_loop(0, owners, one, 0)


def prep_kernel(row_bits, sample_bits, entries, rows_out, samples_out):
    e = entries[...]
    rows = e & ((1 << row_bits) - 1)
    lane = lax.broadcasted_iota(i32, e.shape, 1)
    place = lane & (window - 1)
    clash = jnp.zeros(e.shape, i32)
    for d in range(1, window):
        other = pltpu.roll(rows, lanes - d, 1)
        clash = jnp.where((other == rows) & (place < window - d), 1, clash)
    step = 1
    while step < group:
        clash = clash | pltpu.roll(clash, lanes - step, 1)
        step *= 2
    rows_out[...] = jnp.where((lane & (group - 1)) == 0, rows | (clash << flag_bit), rows)
    samples_out[...] = lax.shift_right_logical(e, row_bits) & ((1 << sample_bits) - 1)


def one_hot(samples_ref, row, base, low, high, per_device, width):
    count = width // lanes
    s = jnp.concatenate([samples_ref[pl.ds(row + c, 1), :] for c in range(count)], axis=1)
    k = lax.broadcasted_iota(i32, (1, width), 1) + base
    s = jnp.where((k >= low) & (k < high), s, -1).astype(f32).astype(bf16)
    place = lax.broadcasted_iota(i32, (per_device, width), 0).astype(f32).astype(bf16)
    return jnp.where(place == s, jnp.ones((), bf16), jnp.zeros((), bf16))


class Lists:
    def __init__(self, ring, me, rows, held, sems):
        self.ring, self.me, self.rows, self.held, self.sems = ring, me, rows, held, sems
        self.length = held.shape[0] // (2 * batch)
        self.batches = rows.shape[0] // self.length // batch

    def copies(self, n):
        slot = n & 1
        found = []
        for b in range(batch):
            sender = self.ring.device_at(self.me[0], n * batch + b)
            source = self.rows.at[pl.ds(pl.multiple_of(sender * self.length, 1024), self.length)]
            held = self.held.at[pl.ds(pl.multiple_of((slot * batch + b) * self.length, 1024), self.length)]
            found.append(pltpu.make_async_copy(source, held, self.sems.at[slot, b]))
        return found

    def start(self, n):
        for copy in self.copies(n):
            copy.start()

    def wait(self, n):
        for copy in self.copies(n):
            copy.wait()

    def run(self, step):
        self.start(0)

        def one(n, carry):
            @pl.when(n + 1 < self.batches)
            def _():
                self.start(n + 1)

            self.wait(n)
            step(n)
            return carry

        lax.fori_loop(0, self.batches, one, 0)

    def first(self, n, b, at):
        return ((n & 1) * batch + b) * self.length + at

    def entry(self, place):
        return self.held[place] & ((1 << flag_bit) - 1)

    def clash(self, place):
        return lax.shift_right_logical(self.held[place], flag_bit)


def gather_kernel(ring, first_pair, at, per_device, cap, me, bounds, rows, samples, table, *refs):
    keep, send, rows_f, stage, pooled, held, sems, out_sem = refs[-8:]
    step = pl.program_id(0)
    pair = first_pair + step
    rows_own = table.shape[2]
    width = min(256, cap)
    cap_rows = cap // lanes
    blocks = cap // width
    span = 256
    lane = lax.broadcasted_iota(i32, (span, lanes), 1)
    same = lax.broadcasted_iota(i32, (span, span), 0) == lax.broadcasted_iota(i32, (span, span), 1)
    unit = jnp.where(same, 1.0, 0.0).astype(bf16)

    def turn(c, carry):
        at = pl.multiple_of(c * span, span)
        t = table[0, :, pl.ds(at, span)].astype(bf16)
        t = lax.dot_general(unit, t, (((1,), (1,)), ((), ())), preferred_element_type=f32)
        rows_f[pl.ds(at, span), :] = jnp.where(lane < lanes // 2, t, 0.0)
        at_odd = pl.multiple_of(c * span + rows_own, span)
        rows_f[pl.ds(at_odd, span), :] = jnp.where(lane < lanes // 2, 0.0, t)
        return carry

    lax.fori_loop(0, rows_own // span, turn, 0, unroll=8)
    stage[...] = jnp.zeros(stage.shape, f32)
    lists = Lists(ring, me, rows, held, sems)

    def some(n):
        senders = [ring.device_at(me[0], n * batch + b) for b in range(batch)]
        lows = [bounds[s * 8 + pair] for s in senders]
        highs = [bounds[s * 8 + pair + 1] for s in senders]
        for b in range(batch):

            def fetch(i, c):
                at = pl.multiple_of(i * group, group)
                first = lists.first(n, b, at)
                for u in range(group):
                    r = held[first + u] if u else lists.entry(first)
                    stage[b, pl.ds(at + u, 1), :] = rows_f[pl.ds(r, 1), :]
                return c

            lax.fori_loop(lax.div(lows[b], group), lax.div(highs[b] + group - 1, group), fetch, 0)

        def term(b, i):
            block = jnp.minimum(i, blocks - 1)
            row = senders[b] * cap_rows + block * (width // lanes)
            hot = one_hot(samples, row, i * width, lows[b], highs[b], per_device, width)
            fetched = stage[b, pl.ds(pl.multiple_of(block * width, width), width), :].astype(bf16)
            return jnp.dot(hot, fetched, preferred_element_type=f32)

        shift = bits_of(width)
        begins = [lax.shift_right_logical(low, shift) for low in lows]
        def put(b, total):
            pooled[pl.ds(n * batch + b, 1)] = total.astype(bf16)[None]

        for b in range(batch):
            put(b, term(b, begins[b]) + term(b, begins[b] + 1))
        for b in range(batch):

            @pl.when(highs[b] > (begins[b] + 2) * width)
            def _():
                total = lax.fori_loop(
                    begins[b],
                    lax.shift_right_logical(highs[b] + width - 1, shift),
                    lambda i, t: t + term(b, i),
                    jnp.zeros((per_device, lanes), f32),
                )
                put(b, total)

    lists.run(some)
    half = keep.shape[0]
    copies = [
        pltpu.make_async_copy(pooled.at[pl.ds(i * half, half)], ref.at[:, at + step], out_sem.at[i])
        for i, ref in enumerate((keep, send))
    ]
    for copy in copies:
        copy.start()
    for copy in copies:
        copy.wait()


def scatter_kernel(
    ring, pair, rows_at, per_device, cap, me, bounds, rows, samples, own, other, w_in, m_in, a_in, *refs
):
    w_out, m_out, a_out, sums, stage, grads, w_buf, m_buf, a_buf, held, sems, grad_sem, in_sem, out_sem = refs[-14:]
    blocks_each = own.shape[0]
    arrivals = [
        pltpu.make_async_copy(ref.at[:, pl.ds(rows_at, per_device)], grads.at[pl.ds(i * blocks_each, blocks_each)], grad_sem.at[i])
        for i, ref in enumerate((own, other))
    ]
    for arrival in arrivals:
        arrival.start()
    rows_own = w_in.shape[2]
    width = min(256, cap)
    cap_rows = cap // lanes
    blocks = cap // width
    sources = (w_in, m_in, a_in)
    targets = (w_out, m_out, a_out)
    buffers = (w_buf, m_buf, a_buf)
    sums[...] = jnp.zeros(sums.shape, f32)
    lists = Lists(ring, me, rows, held, sems)
    for arrival in arrivals:
        arrival.wait()
    for i in range(3):
        pltpu.make_async_copy(sources[i].at[pair], buffers[i], in_sem.at[i]).start()

    def some(n):
        senders = [ring.device_at(me[0], n * batch + b) for b in range(batch)]
        lows = [bounds[s * 8 + pair] for s in senders]
        highs = [bounds[s * 8 + pair + 1] for s in senders]

        def spread(b, i):
            block = jnp.minimum(i, blocks - 1)
            row = senders[b] * cap_rows + block * (width // lanes)
            hot = one_hot(samples, row, block * width, lows[b], highs[b], per_device, width)
            mine = grads[n * batch + b]
            stage[b, pl.ds(pl.multiple_of(block * width, width), width), :] = lax.dot_general(
                hot, mine, (((0,), (0,)), ((), ())), preferred_element_type=f32
            )

        shift = bits_of(width)
        begins = [lax.shift_right_logical(low, shift) for low in lows]
        for b in range(batch):
            spread(b, begins[b])
            spread(b, begins[b] + 1)
        for b in range(batch):

            @pl.when(highs[b] > (begins[b] + 2) * width)
            def _():
                def more(i, c):
                    spread(b, i)
                    return c

                lax.fori_loop(begins[b] + 2, lax.shift_right_logical(highs[b] + width - 1, shift), more, 0)

        for b in range(batch):

            def add(i, c):
                at = pl.multiple_of(i * group, group)
                first = lists.first(n, b, at)

                def apart():
                    for start in range(0, group, window):
                        places = [held[first + u] if u else lists.entry(first) for u in range(start, start + window)]
                        olds = [sums[pl.ds(r, 1), :] for r in places]
                        news = [stage[b, pl.ds(at + start + u, 1), :] for u in range(window)]
                        for r, old, new in zip(places, olds, news):
                            sums[pl.ds(r, 1), :] = old + new

                def in_turn():
                    def single(u, inner):
                        r = lists.entry(first + u)
                        sums[pl.ds(r, 1), :] = sums[pl.ds(r, 1), :] + stage[b, pl.ds(at + u, 1), :]
                        return inner

                    lax.fori_loop(0, group, single, 0)

                lax.cond(lists.clash(first) == 0, apart, in_turn)
                return c

            lax.fori_loop(lax.div(lows[b], group), lax.div(highs[b] + group - 1, group), add, 0)

    lists.run(some)
    for i in range(3):
        pltpu.make_async_copy(sources[i].at[pair], buffers[i], in_sem.at[i]).wait()
    chunks = out_sem.shape[0] // 3
    chunk = rows_own // chunks
    span = min(256, chunk)
    lane = lax.broadcasted_iota(i32, (span, lanes), 1)

    def copies(n):
        part = pl.ds(n * chunk, chunk)
        return [
            pltpu.make_async_copy(buffers[i].at[:, part], targets[i].at[pair, :, part], out_sem.at[n * 3 + i])
            for i in range(3)
        ]

    for n in range(chunks):

        def update(c, carry):
            at = pl.multiple_of(n * chunk + c * span, span)
            even = sums[pl.ds(at, span), :]
            odd = sums[pl.ds(pl.multiple_of(at + rows_own, span), span), :]
            grad = jnp.where(lane < lanes // 2, even, odd).T
            part = (slice(None), pl.ds(at, span))
            new = nesterov(w_buf[part], m_buf[part], a_buf[part], grad, rates[0])
            w_buf[part] = new[0]
            m_buf[part] = new[1]
            a_buf[part] = new[2]
            return carry

        lax.fori_loop(0, chunk // span, update, 0)
        for copy in copies(n):
            copy.start()
    for n in range(chunks):
        for copy in copies(n):
            copy.wait()


rows_first = (((0,), (0,)), ((), ()))
last_last = (((1,), (1,)), ((), ()))


def experts_forward(x_ref, weight_ref, y_ref, act_ref, slope_ref):
    x = x_ref[...]
    total = None
    for m in range(weight_ref.shape[1]):
        w_in, w_out = (weight_ref[:, m, i, 0].reshape(-1, weight_ref.shape[-1]) for i in range(2))
        act, slope = gelu_pair(jnp.dot(x, w_in, preferred_element_type=f32))
        act = act.astype(bf16)
        act_ref[0, m] = act
        slope_ref[0, m] = slope.astype(bf16)
        term = lax.dot_general(act, w_out, last_last, preferred_element_type=f32)
        total = term if total is None else total + term
    y_ref[0] = total


def experts_back_rows(pairs, d_ref, weight_ref, slope_ref, dxg_ref, inv_ref, d_hidden_ref, *refs):
    grads, dx = refs[:pairs], refs[pairs]
    d_out = d_ref[0]
    total = None
    for m in range(weight_ref.shape[1]):
        w_in, w_out = (weight_ref[:, m, i, 0].reshape(-1, weight_ref.shape[-1]) for i in range(2))
        d_act = jnp.dot(d_out, w_out, preferred_element_type=f32)
        d_hidden = (d_act * slope_ref[0, m].astype(f32)).astype(bf16)
        d_hidden_ref[0, m] = d_hidden
        term = lax.dot_general(d_hidden, w_in, last_last, preferred_element_type=f32)
        total = term if total is None else total + term

    @pl.when(pl.program_id(0) == 0)
    def _():
        dx[...] = dxg_ref[...] + total

    @pl.when(pl.program_id(0) != 0)
    def _():
        dx[...] += total

    @pl.when(pl.program_id(0) == pl.num_programs(0) - 1)
    def _():
        for p in range(pairs):
            part = (slice(None), slice(p * lanes, (p + 1) * lanes))
            grads[p][...] = (dx[part] * inv_ref[part]).astype(bf16)


def experts_back_weights(n_model, lhs_ref, rows_ref, *refs):
    dw_ref = refs[-1]
    devices, _, f_own, _ = dw_ref.shape
    lhs = lhs_ref[0]
    for m in range(n_model):
        out = jnp.dot(lhs, rows_ref[0, m], preferred_element_type=f32).astype(bf16)
        for d in range(devices // n_model):
            dw_ref[d * n_model + m, 0] = out[d * f_own : (d + 1) * f_own]


def experts_back_placed(bits, n_model, me, lhs_ref, rows_ref, *refs):
    keep, send = refs[-2:]
    half, _, f_own, h_own = keep.shape
    model = me[0] & (n_model - 1)
    data = me[0] ^ model
    bits = [0] + bits[1:]
    lhs = lhs_ref[0]
    for beside in range(n_model):
        out = jnp.dot(lhs, rows_ref[0, pl.ds(model ^ beside, 1)][0], preferred_element_type=f32).astype(bf16)
        to = send if beside & 1 else keep
        for d in range(2 * half // n_model):
            place = place_in(bits, (data ^ (d * n_model)) | (beside & (n_model - 2)))
            to[pl.ds(place, 1), 0] = out[d * f_own : (d + 1) * f_own][None]


def head_kernel(
    sample_total, x_ref, y_ref, gate_ref, tower_ref, v_ref, label_ref,
    d_expert_ref, d_expert_t_ref, dxg_ref, d_tower_ref, d_gate_ref, small_ref, probs, mixed, d_mixed, d_gate, inner,
):
    experts, rows, features = y_ref.shape
    tasks = tower_ref.shape[0]
    x = x_ref[...]
    gate = gate_ref[...]
    logits = jnp.dot(x, gate, preferred_element_type=f32)
    task_of = lax.shift_right_logical(lax.broadcasted_iota(i32, (1, lanes), 1), bits_of(experts))

    def by_task(fold, value, fill):
        total = jnp.zeros(value.shape, f32)
        for k in range(tasks):
            found = fold(jnp.where(task_of == k, value, fill), axis=1, keepdims=True)
            total = jnp.where(task_of == k, found, total)
        return total

    used = task_of < tasks
    raised = jnp.where(used, jnp.exp(logits - by_task(jnp.max, logits, -jnp.inf)), 0.0)
    probs[...] = raised / jnp.where(used, by_task(jnp.sum, raised, 0.0), 1.0)
    span = 16
    parts = 2
    wide = features // parts

    def mix(r, carry):
        part = pl.ds(pl.multiple_of(r * span, span), span)
        p = probs[part, :]
        for h in range(parts):
            across = slice(h * wide, (h + 1) * wide)
            totals = [None] * tasks
            for e in range(experts):
                y = y_ref[e, part, across]
                for k in range(tasks):
                    c = k * experts + e
                    more = p[:, c : c + 1] * y
                    totals[k] = more if e == 0 else totals[k] + more
            for k in range(tasks):
                mixed[k, part, across] = totals[k].astype(bf16)
        return carry

    lax.fori_loop(0, rows // span, mix, 0)
    loss = jnp.zeros((1, 1), f32)
    vectors = []
    for k in range(tasks):
        tower = tower_ref[k]
        act, slope = gelu_pair(jnp.dot(mixed[k], tower, preferred_element_type=f32))
        v = v_ref[k : k + 1, :]
        logit = jnp.sum(act * v, axis=1, keepdims=True)
        label = label_ref[:, k : k + 1]
        weighting = task_weights[k] * label_ref[:, tasks + k : tasks + k + 1]
        small_exp = jnp.exp(-jnp.abs(logit))
        softplus = jnp.maximum(logit, 0.0) + jnp.log1p(small_exp)
        loss = loss + jnp.sum(weighting * (softplus - label * logit), axis=0, keepdims=True)
        sigmoid = jnp.where(logit >= 0.0, 1.0, small_exp) / (1.0 + small_exp)
        d_logit = weighting * (sigmoid - label) / sample_total
        vectors.append(jnp.sum(d_logit * act, axis=0, keepdims=True))
        d_pre = (d_logit * v * slope).astype(bf16)
        d_mixed[k] = lax.dot_general(d_pre, tower, last_last, preferred_element_type=f32)
        d_tower_ref[k] = lax.dot_general(mixed[k], d_pre, rows_first, preferred_element_type=f32).astype(bf16)
    lane = lax.broadcasted_iota(i32, (span, lanes), 1)
    ones = jnp.ones((lanes, lanes), bf16)

    def back(r, carry):
        part = pl.ds(pl.multiple_of(r * span, span), span)
        p = probs[part, :]
        for e in range(experts):
            y = y_ref[e, part, :]
            total = None
            for k in range(tasks):
                c = k * experts + e
                d = d_mixed[k, part, :]
                product = d * y
                narrow = product[:, :lanes]
                for t in range(1, features // lanes):
                    narrow = narrow + product[:, t * lanes : (t + 1) * lanes]
                coarse = narrow.astype(bf16)
                inner[0, c * span : (c + 1) * span, :] = coarse
                inner[1, c * span : (c + 1) * span, :] = (narrow - coarse.astype(f32)).astype(bf16)
                more = p[:, c : c + 1] * d
                total = more if k == 0 else total + more
            d_expert_ref[e, part, :] = total.astype(bf16)
        row_sums = jnp.dot(inner[0], ones, preferred_element_type=f32)
        row_sums = row_sums + jnp.dot(inner[1], ones, preferred_element_type=f32)
        d_probs = jnp.zeros((span, lanes), f32)
        for c in range(tasks * experts):
            d_probs = jnp.where(lane == c, row_sums[c * span : (c + 1) * span], d_probs)
        d_gate[part, :] = (p * (d_probs - by_task(jnp.sum, p * d_probs, 0.0))).astype(bf16)
        return carry

    lax.fori_loop(0, rows // span, back, 0)
    for e in range(experts):
        d_expert_t_ref[e] = d_expert_ref[e].T
    dxg_ref[...] = lax.dot_general(d_gate[...], gate, last_last, preferred_element_type=f32)
    d_gate_ref[...] = lax.dot_general(x, d_gate[...], rows_first, preferred_element_type=f32).astype(bf16)
    line = lax.broadcasted_iota(i32, (8, lanes), 0)
    tile = jnp.where(line == tasks, loss, 0.0)
    for k in range(tasks):
        tile = jnp.where(line == k, vectors[k], tile)
    pieces = []
    for _ in range(4):
        piece = tile.astype(bf16)
        pieces.append(piece)
        tile = tile - piece.astype(f32)
    small_ref[...] = jnp.concatenate(pieces, axis=0)


def smem():
    return pl.BlockSpec(memory_space=pltpu.SMEM)


def vmem():
    return pl.BlockSpec(memory_space=pltpu.VMEM)


def body(
    row_ids, bag_counts, labels, label_mask, tables, table_mom, table_avg, w_in, w_in_mom, w_in_avg,
    w_out, w_out_mom, w_out_avg, gate_w, gate_mom, gate_avg, tower_w, tower_w_mom, tower_w_avg,
    tower_v, tower_v_mom, tower_v_avg,
):
    n_model = lax.axis_size("mp")
    n_data = lax.axis_size("dp")
    devices = n_data * n_model
    ring = Ring(n_data, n_model)
    mp_rank = lax.axis_index("mp")
    me = (lax.axis_index("dp") * n_model + mp_rank).astype(i32).reshape(1)
    per_group, table_count, bag_size = row_ids.shape
    per_device = per_group // n_model
    rows_own = tables.shape[1]
    emb_width = tables.shape[2]
    features = table_count * emb_width
    pairs = features // lanes
    sample_total = float(per_group * n_data)
    slot_total = per_device * table_count * bag_size
    cap = 2 * slot_total // devices
    cap_rows = cap // lanes

    w_out_t, w_out_mom_t, w_out_avg_t = (v.transpose(0, 2, 1) for v in (w_out, w_out_mom, w_out_avg))
    experts, f_own, h_own = w_in.shape
    weights = jnp.stack([w_in, w_out_t]).astype(bf16)
    weights = lax.all_gather(weights, both, axis=0).reshape(n_data, n_model, 2, experts, f_own, h_own)

    row_bits = bits_of(rows_own) + 1
    sample_bits = bits_of(per_device)
    start = mp_rank * per_device
    ids = lax.dynamic_slice_in_dim(row_ids.transpose(1, 2, 0), start, per_device, 2)
    counts = lax.dynamic_slice_in_dim(bag_counts.T, start, per_device, 1)
    live = lax.broadcasted_iota(i32, ids.shape, 1) < counts[:, None, :]
    table_of = lax.broadcasted_iota(i32, ids.shape, 0)
    bucket = lax.shift_right_logical(ids, row_bits - 1) * pairs + lax.shift_right_logical(table_of, 1)
    key = (bucket << sample_bits) | lax.broadcasted_iota(i32, ids.shape, 2)
    key = (((key << 1) | (table_of & 1)) << (row_bits - 1)) | (ids & (rows_own - 1))
    key = jnp.where(live, key, 1 << 30).reshape(-1)
    ordered = lax.sort(key)
    bucket_sorted = lax.shift_right_logical(ordered, row_bits + sample_bits)
    starts = jnp.sum(
        (bucket_sorted[None, :] < jnp.arange(devices * pairs + 1, dtype=i32)[:, None]).astype(i32), axis=1
    )
    padded = jnp.concatenate([ordered.reshape(-1, lanes), jnp.zeros((cap_rows + 8, lanes), i32)], axis=0)
    out_rows = -(-(cap_rows + 1) // 8) * 8
    outgoing = pl.pallas_call(
        functools.partial(bucket_kernel, pairs, cap_rows),
        out_shape=jax.ShapeDtypeStruct((devices, out_rows, lanes), i32),
        in_specs=[smem(), vmem()],
        out_specs=vmem(),
        name="bucket",
    )(starts, padded)
    received = lax.all_to_all(outgoing, both, split_axis=0, concat_axis=0, tiled=True)
    bounds = received[:, cap_rows, :8].reshape(-1)
    entries = received[:, :cap_rows].reshape(devices * cap_rows, lanes)
    entry_shape = jax.ShapeDtypeStruct(entries.shape, i32)
    rows, samples = pl.pallas_call(
        functools.partial(prep_kernel, row_bits, sample_bits),
        out_shape=(entry_shape, entry_shape),
        in_specs=[vmem()],
        out_specs=(vmem(), vmem()),
        name="prep",
    )(entries)
    length = max(cap, 1024)
    rows = jnp.pad(rows.reshape(devices, cap), ((0, 0), (0, length - cap))).reshape(-1)
    hbm = pl.BlockSpec(memory_space=pl.ANY)
    list_scratch = [pltpu.SMEM((2 * batch * length,), i32), pltpu.SemaphoreType.DMA((2, batch))]

    paired = tuple(
        v.transpose(0, 2, 1).reshape(pairs, lanes, rows_own) for v in (tables, table_mom, table_avg)
    )
    half = devices // 2
    half_shape = jax.ShapeDtypeStruct((half, per_device, lanes), bf16)

    def gather(first_pair, count, at, total, olds, after):
        out_shape = jax.ShapeDtypeStruct((half, total, per_device, lanes), bf16)
        return pl.pallas_call(
            functools.partial(gather_kernel, ring, first_pair, at, per_device, cap),
            grid=(count,),
            out_shape=(out_shape, out_shape),
            in_specs=[
                smem(), smem(), hbm, vmem(),
                pl.BlockSpec((1, lanes, rows_own), lambda i: (first_pair + i, 0, 0)),
            ] + [hbm] * (len(olds) + len(after)),
            out_specs=(hbm, hbm),
            scratch_shapes=[
                pltpu.VMEM((2 * rows_own, lanes), f32),
                pltpu.VMEM((batch, cap, lanes), f32),
                pltpu.VMEM((devices, per_device, lanes), bf16),
            ] + list_scratch + [pltpu.SemaphoreType.DMA((2,))],
            input_output_aliases={5: 0, 6: 1} if olds else {},
            compiler_params=params(),
            cost_estimate=cost(16 * count),
            name="gather",
        )(me, bounds, rows, samples, paired[0], *olds, *after)

    plane, line = len(ring.stages[1]), len(ring.stages[2])
    each = half // plane

    def core_sums(keep, send, steps, after=(), name="sum_core"):
        return sum_pieces([keep, ring.swap(send, 1)], plane, bf16, steps, after, name)

    def plane_sums(pieces, steps, after=(), name="sum_plane"):
        return sum_pieces(ring.swap_pieces(1, pieces), line, bf16, steps, after, name)

    def line_sum(pieces):
        total = None
        for piece in ring.swap_pieces(2, pieces):
            total = piece.astype(f32) if total is None else total + piece.astype(f32)
        return total

    early = pairs // 2
    rest = pairs - early
    cored_early = core_sums(*gather(0, early, 0, early, (), ()), 2)
    late = gather(early, rest - 1, 0, rest, (), ())
    late = gather(pairs - 1, 1, rest - 1, rest, late, (cored_early[0],))
    planed_early = plane_sums(cored_early, 1)
    cored_late = core_sums(late[0], held_until(late[1], (planed_early[0],)), 2)
    planed_late = plane_sums(cored_late, 1)
    pooled = jnp.concatenate([line_sum(planed_early)[0], line_sum(planed_late)[0]], axis=0)
    inverse = jnp.repeat(1.0 / counts.T.astype(f32), emb_width, axis=1)
    x = (pooled.transpose(1, 0, 2).reshape(per_device, features) * inverse).astype(bf16)

    hidden_shape = jax.ShapeDtypeStruct((experts, n_model, per_device, h_own), bf16)
    weight_spec = pl.BlockSpec((n_data, n_model, 2, 1, f_own, h_own), lambda e: (0, 0, 0, e, 0, 0))
    hidden_spec = pl.BlockSpec((1, n_model, per_device, h_own), lambda e: (e, 0, 0, 0))
    expert_spec = pl.BlockSpec((1, per_device, features), lambda e: (e, 0, 0))
    whole_spec = pl.BlockSpec((per_device, features), lambda e: (0, 0))
    y, act, slope = pl.pallas_call(
        experts_forward,
        grid=(experts,),
        out_shape=(jax.ShapeDtypeStruct((experts, per_device, features), f32), hidden_shape, hidden_shape),
        in_specs=[whole_spec, weight_spec],
        out_specs=(expert_spec, hidden_spec, hidden_spec),
        compiler_params=params(),
        cost_estimate=cost(16),
        name="experts_forward",
    )(x, weights)
    tasks, _, tower_width = tower_w.shape
    spare = lanes - tasks * experts
    gate_low = jnp.pad(gate_w.transpose(1, 0, 2).reshape(features, tasks * experts), ((0, 0), (0, spare))).astype(bf16)
    label_rows = lax.dynamic_slice_in_dim(labels, start, per_device, 0)
    mask_rows = lax.dynamic_slice_in_dim(label_mask, start, per_device, 0)
    marks = jnp.concatenate([label_rows, mask_rows], axis=1).astype(f32)
    d_expert, d_expert_t, d_x_gate, d_tower_part, d_gate_part, tiny = pl.pallas_call(
        functools.partial(head_kernel, sample_total),
        out_shape=(
            jax.ShapeDtypeStruct((experts, per_device, features), bf16),
            jax.ShapeDtypeStruct((experts, features, per_device), bf16),
            jax.ShapeDtypeStruct((per_device, features), f32),
            jax.ShapeDtypeStruct(tower_w.shape, bf16),
            jax.ShapeDtypeStruct((features, lanes), bf16),
            jax.ShapeDtypeStruct((32, lanes), bf16),
        ),
        in_specs=[vmem()] * 6,
        out_specs=(vmem(),) * 6,
        scratch_shapes=[
            pltpu.VMEM((per_device, lanes), f32),
            pltpu.VMEM((tasks, per_device, features), bf16),
            pltpu.VMEM((tasks, per_device, features), f32),
            pltpu.VMEM((per_device, lanes), bf16),
            pltpu.VMEM((2, 16 * tasks * experts, lanes), bf16),
        ],
        compiler_params=params(),
        cost_estimate=cost(12),
        name="towers",
    )(x, y, gate_low, tower_w.astype(bf16), tower_v, marks)
    grads_shape = jax.ShapeDtypeStruct((per_device, lanes), bf16)
    d_hidden, *grads = pl.pallas_call(
        functools.partial(experts_back_rows, pairs),
        grid=(experts,),
        out_shape=(hidden_shape,) + (grads_shape,) * pairs,
        in_specs=[expert_spec, weight_spec, hidden_spec, whole_spec, whole_spec],
        out_specs=(hidden_spec,) + (pl.BlockSpec((per_device, lanes), lambda e: (0, 0)),) * pairs,
        scratch_shapes=[pltpu.VMEM((per_device, features), f32)],
        compiler_params=params(),
        cost_estimate=cost(14),
        name="experts_back_rows",
    )(d_expert, weights, slope, d_x_gate, inverse)
    grads = jnp.concatenate([grads[0], tiny] + grads[1:], axis=0)[None]

    lhs_spec = [
        pl.BlockSpec((1, features, per_device), lambda e, single=single: (0 if single else e, 0, 0))
        for single in (False, True)
    ]
    rows_spec = pl.BlockSpec((1, n_model, per_device, h_own), lambda e: (e, 0, 0, 0))
    half_weights = jax.ShapeDtypeStruct((half, experts, f_own, h_own), bf16)
    half_spec = pl.BlockSpec((half, 1, f_own, h_own), lambda e: (0, e, 0, 0))

    paired_shape = jax.ShapeDtypeStruct(paired[0].shape, f32)
    chunks = 8

    def scatter(pair, at, own, other, olds, after):
        in_specs = [smem(), smem(), hbm, vmem()] + [hbm] * (5 + len(olds) + len(after))
        return pl.pallas_call(
            functools.partial(scatter_kernel, ring, pair, at, per_device, cap),
            out_shape=(paired_shape,) * 3,
            in_specs=in_specs,
            out_specs=(hbm, hbm, hbm),
            scratch_shapes=[
                pltpu.VMEM((2 * rows_own, lanes), f32),
                pltpu.VMEM((batch, cap, lanes), f32),
                pltpu.VMEM((devices, per_device, lanes), bf16),
                pltpu.VMEM((lanes, rows_own), f32),
                pltpu.VMEM((lanes, rows_own), f32),
                pltpu.VMEM((lanes, rows_own), f32),
                *list_scratch,
                pltpu.SemaphoreType.DMA((2,)),
                pltpu.SemaphoreType.DMA((3,)),
                pltpu.SemaphoreType.DMA((3 * chunks,)),
            ],
            input_output_aliases={9: 0, 10: 1, 11: 2} if olds else {},
            compiler_params=params(),
            cost_estimate=cost(26),
            name="scatter",
        )(me, bounds, rows, samples, own, other, *paired, *olds, *after)

    small_rows = tasks * features + features
    small = jnp.concatenate([d_tower_part.reshape(-1, lanes), d_gate_part], axis=0).reshape(2, 1, small_rows // 2, lanes)
    side = me[0] & 1
    give = lax.dynamic_index_in_dim(small, 1 - side, 0, keepdims=False)
    take = lax.dynamic_index_in_dim(small, side, 0, keepdims=False)
    dw_out = pl.pallas_call(
        functools.partial(experts_back_weights, n_model),
        grid=(experts,),
        out_shape=jax.ShapeDtypeStruct((devices, experts, f_own, h_own), bf16),
        in_specs=[lhs_spec[0], rows_spec],
        out_specs=pl.BlockSpec((devices, 1, f_own, h_own), lambda e: (0, e, 0, 0)),
        compiler_params=params(),
        cost_estimate=cost(9),
        name="experts_back_out",
    )(d_expert_t, act)
    lined = join(ring.spread(2, grads), (dw_out,))
    small = sum_pieces([take, ring.swap(give, 1)], 1, bf16, 1, (dw_out,), "sum_small")[0]
    d_w_out = lax.psum_scatter(dw_out, both, scatter_dimension=0, tiled=True)[0].astype(f32)
    keep, send = pl.pallas_call(
        functools.partial(experts_back_placed, ring.place_bits(), n_model),
        grid=(experts,),
        out_shape=(half_weights, half_weights),
        in_specs=[smem(), lhs_spec[1], rows_spec, hbm, hbm],
        out_specs=(half_spec, half_spec),
        compiler_params=params(),
        cost_estimate=cost(9),
        name="experts_back_in",
    )(me, x.T[None], d_hidden, lined, small)
    with_tiny = per_device + tiny.shape[0]
    edges = (0, with_tiny, lined.shape[1])
    spread = [ring.spread(1, lined[:, low:high]) for low, high in zip(edges, edges[1:])]
    far = [1 << bit for bit in range(3, bits_of(devices))] + [2, 4]

    def add_small(small, after, count=1):
        for distance in far[:count]:
            small = sum_pieces([small, ring.swap(small, distance)], 1, bf16, 1, after, "sum_small")[0]
        del far[:count]
        return small

    small = add_small(small, (keep,))
    own = join(spread[0], (small,))
    other = ring.swap(own, 1)
    send = held_until(send, (own,))
    sent = ring.swap(send, 1)
    tiny_sum = jnp.sum(jnp.concatenate([own[:, per_device:], other[:, per_device:]]).astype(f32), axis=0)
    table_outs = scatter(0, 0, own, other, (), ())
    small = add_small(small, (table_outs[0],))
    own = join(spread[1], (small,))
    other = ring.swap(own, 1)
    cored = sum_pieces([keep, sent], plane, bf16, 8, (own,), "sum_core_w")
    for pair in range(1, pairs):
        if pair == pairs - 1:
            planed = plane_sums(cored, 4, (table_outs[0],), "sum_plane_w")
            small = add_small(small, (planed[0],), len(far))
            after = (small,)
        elif pair == 1:
            after = (cored[0],)
        else:
            small = add_small(small, (table_outs[0],))
            after = (small,)
        table_outs = scatter(pair, (pair - 1) * per_device, own, other, table_outs, after)
    take = small
    got = ring.swap(take, 1)
    small = jnp.concatenate([jnp.where(side == 0, take, got), jnp.where(side == 0, got, take)]).astype(f32)
    small = small.reshape(small_rows, lanes)
    d_tower_w = small[: tasks * features].reshape(tower_w.shape)
    d_gate_w = small[tasks * features :, : tasks * experts]
    d_gate_w = d_gate_w.reshape(features, tasks, experts).transpose(1, 0, 2)
    d_w_in = line_sum(planed)[0]
    tiny_sum = jnp.sum(tiny_sum.reshape(4, 8, lanes), axis=0)
    d_tower_v, loss_sum = tiny_sum[:tasks], tiny_sum[tasks, 0]
    table_new = tuple(v.reshape(table_count, emb_width, rows_own).transpose(0, 2, 1) for v in table_outs)
    w_in_new = nesterov(w_in, w_in_mom, w_in_avg, d_w_in, rates[1])
    w_out_new = nesterov(w_out_t, w_out_mom_t, w_out_avg_t, d_w_out, rates[2])
    w_out_new = tuple(v.transpose(0, 2, 1) for v in w_out_new)
    gate_new = nesterov(gate_w, gate_mom, gate_avg, d_gate_w, rates[3])
    tower_new = nesterov(tower_w, tower_w_mom, tower_w_avg, d_tower_w, rates[4])
    vector_new = nesterov(tower_v, tower_v_mom, tower_v_avg, d_tower_v, rates[5])
    return (loss_sum,) + table_new + w_in_new + w_out_new + gate_new + tower_new + vector_new


def solution(mesh):
    group_spec = P("dp", None)
    table_spec = P(None, both, None)
    placed = (
        (P("dp", None, None), group_spec, group_spec, group_spec)
        + (table_spec,) * 3
        + (P(None, "dp", "mp"),) * 3
        + (P(None, "mp", "dp"),) * 3
        + (P(),) * 9
    )
    return jax.shard_map(
        body,
        mesh=mesh,
        in_specs=placed,
        out_specs=(P(),)
        + (table_spec,) * 3
        + (P(None, "dp", "mp"),) * 3
        + (P(None, "mp", "dp"),) * 3
        + (P(),) * 9,
        check_vma=False,
    )
```
